512 devices in a mesh: along: 64 (over y_lo, z, core), cross: 8 (over x, y_hi).
Axes of the slice: x: 4, y: 8 (y_hi: 2, y_lo: 4; y = y_hi * 4 + y_lo), z: 8, core: 2. Of those that a mesh axis runs over, the one named last changes fastest.
Arguments:
- surface: float32 [8192, 2048], P('along', 'cross'), may hold values from -6 to 6
- along_speed: float32 [8192, 2048], P('along', 'cross'), may hold values from -3 to 3
- cross_speed: float32 [8192, 2048], P('along', 'cross'), may hold values from -3 to 3
- water_depth: float32 [8192, 2048], P('along', 'cross'), may hold values from 0.5 to 2
- wet_mask: int32 [8192, 2048], P('along', 'cross'), may hold values 0 or 1
- ship_cells: int32 [2, 8], replicated, may hold values from 0 to 16777215
- ship_pressure: float32 [8], replicated, may hold values from 1 to 4
Outputs:
- surface_out: float32 [8192, 2048], P('along', 'cross')
- along_out: float32 [8192, 2048], P('along', 'cross')
- cross_out: float32 [8192, 2048], P('along', 'cross')
- current_along: float32 [8192, 2048], P('along', 'cross')
- current_cross: float32 [8192, 2048], P('along', 'cross')
The draws below stay inside these ranges and needn't reach their ends.
Inputs may be any that keep to these rules, and one draw needn't show every extreme that they name: `ship_cells`: each entry is a cell index row * 2048 + column.
All inputs are finite; a program needn't handle non-finite values. No bound on the sum of `wet_mask` on one device may be relied on, other than what follows from the above.
Results may differ from the reference program's by a relative error of at most 0.0003.
Values sent between devices are 32-bit elements; how exact they have to be, the bound alone decides.
A program may use at most 64 MiB of HBM per device.

```python
import math
import jax
import jax.numpy as jnp
from jax import lax

STEPS = 2
CIRC = 3
SHIPS = 8
NA = 8192
NC = 2048


def with_ends(values, rng, low, top_value):
    place = [jax.random.randint(jax.random.fold_in(rng, axis), (), 0, length) for axis, length in enumerate(values.shape)]
    main_axis = values.shape.index(max(values.shape))
    beside = place[:main_axis] + [(place[main_axis] + 1) % values.shape[main_axis]] + place[main_axis + 1:]
    return values.at[tuple(place)].set(low).at[tuple(beside)].set(top_value)


def block_scale(key, dims, split, smallest, top_value):
    level = 1.0
    for position, shards_of in split:
        steps = jax.random.uniform(jax.random.fold_in(jax.random.fold_in(key, 6), position), (shards_of,), jnp.float32, smallest / len(split), top_value / len(split))
        level = level * jnp.repeat(jnp.exp(steps), dims[position] // shards_of).reshape((-1,) + (1,) * (len(dims) - 1 - position))
    return level


def gaussian(rng, extent, width, most, split=(), held_as=jnp.bfloat16):
    factor_of = block_scale(rng, extent, split, -0.22, 0.18) if split else 1.0
    result = jax.random.normal(rng, extent, jnp.float32) * width * factor_of
    return jnp.minimum(jnp.maximum(result, -most), most).astype(held_as)


def setup_inputs(seed: int = 0) -> dict:
    splits = jax.random.split(jax.random.key(seed), 8)
    surface = gaussian(splits[0], (NA, NC), 1.0, 6.0, ((0, 64), (1, 8)), jnp.float32)
    along_speed = gaussian(splits[1], (NA, NC), 0.5, 3.0, ((0, 64), (1, 8)), jnp.float32)
    cross_speed = gaussian(splits[2], (NA, NC), 0.5, 3.0, ((0, 64), (1, 8)), jnp.float32)
    water_depth = jnp.clip(jnp.exp(math.log(2.0) - 1.3862944 * jax.random.uniform(splits[3], (NA, NC), jnp.float32) ** block_scale(splits[3], (NA, NC), ((0, 64), (1, 8)), -0.2, 0.2)), 0.5, 2.0)
    wet_mask = with_ends((jax.random.randint(splits[4], (NA, NC), 0, 10) < 9).astype(jnp.int32), jax.random.fold_in(splits[4], 1), 0, 1)
    ship_cells = with_ends(jax.random.randint(splits[5], (STEPS, SHIPS), 0, NA * NC), jax.random.fold_in(splits[5], 1), 0, (NA * NC) - 1).astype(jnp.int32)
    ship_pressure = jnp.clip(jnp.exp(jax.random.uniform(splits[6], (SHIPS,), jnp.float32, math.log(1.0), math.log(4.0))), 1.0, 4.0)
    return dict(surface=surface, along_speed=along_speed, cross_speed=cross_speed, water_depth=water_depth, wet_mask=wet_mask, ship_cells=ship_cells, ship_pressure=ship_pressure)


CONTINUITY = 0.25
MOMENTUM = 0.3
POTENTIAL = 0.5
CIRC_LEVEL = 0.2
CIRC_FORCE = 0.3
FRICTION = 0.1
VISCOSITY = 0.1


def diff_rows(values):
    return 0.5 * (values[..., 2:, 1:-1] - values[..., :-2, 1:-1])


def diff_cols(values):
    return 0.5 * (values[..., 1:-1, 2:] - values[..., 1:-1, :-2])


def laplace(values):
    return (values[..., 2:, 1:-1] + values[..., :-2, 1:-1] + values[..., 1:-1, 2:]
            + values[..., 1:-1, :-2] - 4.0 * values[..., 1:-1, 1:-1])


def interior(values, layers):
    return values[..., layers:values.shape[-2] - layers, layers:values.shape[-1] - layers]


def advance_waves(surface, along_speed, cross_speed, water_depth, wet_share, forcing):
    mass_flux = diff_rows(water_depth * along_speed) + diff_cols(water_depth * cross_speed)
    raised = interior(wet_share, 1) * (interior(surface, 1) - CONTINUITY * mass_flux + interior(forcing, 1))
    curvature = laplace(raised)
    depth_inner = interior(water_depth, 3)
    dispersion = depth_inner * depth_inner / 3.0
    push_along = interior(diff_rows(raised), 1) + dispersion * diff_rows(curvature)
    push_cross = interior(diff_cols(raised), 1) + dispersion * diff_cols(curvature)
    wet_inner = interior(wet_share, 3)
    return (interior(raised, 2),
            wet_inner * (interior(along_speed, 3) - MOMENTUM * push_along),
            wet_inner * (interior(cross_speed, 3) - MOMENTUM * push_cross))


def radiation(water_depth, surface, along_speed, cross_speed):
    potential_part = POTENTIAL * surface * surface
    return jnp.stack([water_depth * along_speed * along_speed + potential_part,
                      water_depth * along_speed * cross_speed,
                      water_depth * cross_speed * cross_speed + potential_part])


def restrict(values):
    leading = values.shape[:-2]
    fine_rows = values.shape[-2]
    fine_cols = values.shape[-1]
    blocks = values.reshape(leading + (fine_rows // 4, 4, fine_cols // 4, 4))
    return jnp.mean(blocks, axis=(-3, -1))


def circulate(coarse, rim):
    depth_coarse = coarse[3]
    wet_coarse = coarse[4]
    stress_wide = rim(coarse[0:3])
    force_along = -(diff_rows(stress_wide[0]) + diff_cols(stress_wide[1])) / depth_coarse
    force_cross = -(diff_rows(stress_wide[1]) + diff_cols(stress_wide[2])) / depth_coarse
    elevation = jnp.zeros_like(depth_coarse)
    flow_along = jnp.zeros_like(depth_coarse)
    flow_cross = jnp.zeros_like(depth_coarse)
    for circ_sweep in range(CIRC):
        moving = rim(jnp.stack([depth_coarse * flow_along, depth_coarse * flow_cross, flow_along, flow_cross]))
        elevation = elevation - CIRC_LEVEL * (diff_rows(moving[0]) + diff_cols(moving[1]))
        surface_slope = rim(elevation[None])[0]
        new_along = wet_coarse * (flow_along + CIRC_FORCE * (force_along - diff_rows(surface_slope))
                                  - FRICTION * flow_along / depth_coarse + VISCOSITY * laplace(moving[2]))
        new_cross = wet_coarse * (flow_cross + CIRC_FORCE * (force_cross - diff_cols(surface_slope))
                                  - FRICTION * flow_cross / depth_coarse + VISCOSITY * laplace(moving[3]))
        flow_along = new_along
        flow_cross = new_cross
    return jnp.stack([flow_along, flow_cross])


def refine_dim(values, along_dim):
    coarse_count = values.shape[along_dim] - 2
    center = lax.slice_in_dim(values, 1, coarse_count + 1, axis=along_dim)
    previous = lax.slice_in_dim(values, 0, coarse_count, axis=along_dim)
    following = lax.slice_in_dim(values, 2, coarse_count + 2, axis=along_dim)
    pieces = jnp.stack([0.625 * center + 0.375 * previous, 0.875 * center + 0.125 * previous,
                        0.875 * center + 0.125 * following, 0.625 * center + 0.375 * following],
                       axis=along_dim + 1)
    new_shape = list(center.shape)
    new_shape[along_dim] = 4 * coarse_count
    return pieces.reshape(tuple(new_shape))


def refine(values):
    return refine_dim(refine_dim(values, 1), 2)


def zero_rim(values):
    return jnp.pad(values, ((0, 0), (1, 1), (1, 1)))


def reference(surface, along_speed, cross_speed, water_depth, wet_mask, ship_cells, ship_pressure):
    wet_share = wet_mask.astype(jnp.float32)
    total_cols = surface.shape[1]
    stress = jnp.zeros((3,) + surface.shape, jnp.float32)
    for wave_section in range(STEPS):
        rows_hit = (ship_cells[wave_section] // total_cols).astype(jnp.int32)
        cols_hit = (ship_cells[wave_section] % total_cols).astype(jnp.int32)
        forcing = jnp.zeros(surface.shape, jnp.float32).at[rows_hit, cols_hit].add(ship_pressure)
        surface, along_speed, cross_speed = advance_waves(
            jnp.pad(surface, 3), jnp.pad(along_speed, 3), jnp.pad(cross_speed, 3),
            jnp.pad(water_depth, 3), jnp.pad(wet_share, 3), jnp.pad(forcing, 3))
        stress = stress + radiation(water_depth, surface, along_speed, cross_speed)
    stress = stress / STEPS
    coarse = restrict(jnp.concatenate([stress, jnp.stack([water_depth, wet_share])], axis=0))
    coarse_flows = circulate(coarse, zero_rim)
    fine_currents = refine(zero_rim(coarse_flows))
    return (surface, along_speed, cross_speed,
            fine_currents[0] * wet_share, fine_currents[1] * wet_share)
```

```python
import functools

import jax
import jax.numpy as jnp
from jax import lax
from jax.experimental import pallas as pl
from jax.experimental.pallas import tpu as pltpu
from jax.sharding import PartitionSpec as P

STEPS = 2
CIRC = 3
CONTINUITY = 0.25
MOMENTUM = 0.3
POTENTIAL = 0.5
CIRC_LEVEL = 0.2
CIRC_FORCE = 0.3
FRICTION = 0.1
VISCOSITY = 0.1

MESH = pl.DeviceIdType.MESH
F32 = jnp.float32
BF16 = jnp.bfloat16

TR = 128
TC = 256
TOP = 16
ER = TR + 2 * TOP
EC = TC + 128
CR = TR // 4
CC = TC // 4
WR = CR + 16
CHUNK = 32
OWN = [(r, CHUNK) for r in range(TOP, TOP + TR, CHUNK)]
ALL = [(TOP - 8, 8)] + OWN + [(TOP + TR, 8)]
DIRS = [(0, -1), (0, 1), (-1, -1), (-1, 1), (1, -1), (1, 1), (-1, 0), (1, 0)]


def iota(shape, dim):
    return lax.broadcasted_iota(jnp.int32, shape, dim)


def halves(x):
    high = x.astype(BF16)
    return high, (x - high.astype(F32)).astype(BF16)


def dot(x, y):
    return jnp.dot(x, y, preferred_element_type=F32)


def dot_nt(x, y):
    return lax.dot_general(x, y, (((1,), (1,)), ((), ())), preferred_element_type=F32)


def row_next(x, keep):
    return pltpu.roll(x, x.shape[0] - 1, 0)[keep]


def row_prev(x, keep):
    return pltpu.roll(x, 1, 0)[keep]


def col_next(x):
    return pltpu.roll(x, x.shape[1] - 1, 1)


def col_prev(x):
    return pltpu.roll(x, 1, 1)


def spread(fine, coarse, fine_dim, shape, first, wrap):
    f = iota(shape, fine_dim)
    c = iota(shape, 1 - fine_dim)
    base = lax.shift_right_logical(f, 2) + first
    k = f & 3
    weight = jnp.where((k == 0) | (k == 3), 0.375, 0.125)
    other = base + jnp.where(k < 2, -1, 1)
    if wrap:
        other = other & (coarse - 1)
    zero = jnp.zeros(shape, F32)
    return (jnp.where(c == base, 1.0 - weight, zero) + jnp.where(c == other, weight, zero)).astype(BF16)


def kernel(
    mesh_rows, mesh_cols,
    s_in, u_in, v_in, d_in, w_in, cells_ref, press_ref,
    s_out, u_out, v_out, ca_out, cc_out,
    ext, speed, wraw, forc, r1, r2, curv, planes, pack, packt, got, corner,
    ts_w, ts_s, side_w, side_s, cw, cs, cur,
    load_sem, store_sem, f_send, f_recv, w_send, w_recv, c_send, c_recv,
):
    a = lax.axis_index("along")
    c = lax.axis_index("cross")
    total_cols = TC * mesh_cols

    def there(da, dc):
        ok = None
        for cond in ([a > 0] if da < 0 else [a < mesh_rows - 1] if da > 0 else []) + (
            [c > 0] if dc < 0 else [c < mesh_cols - 1] if dc > 0 else []
        ):
            ok = cond if ok is None else ok & cond
        return ok

    def device(da, dc):
        return (a + da, c + dc)

    loads = []
    for k, src in enumerate((s_in, u_in, v_in, d_in)):
        loads.append(pltpu.make_async_copy(src, ext.at[k, TOP:TOP + TR, 0:TC], load_sem.at[k]))
    loads.append(pltpu.make_async_copy(w_in, wraw, load_sem.at[4]))
    for cp in loads:
        cp.start()

    for f in range(5):
        ext[f, 0:TOP, :] = jnp.zeros((TOP, EC), F32)
        ext[f, TOP + TR:ER, :] = jnp.zeros((TOP, EC), F32)
    for ref in (r1, r2, curv, speed.at[0], speed.at[1]):
        ref[0:8, :] = jnp.zeros((8, EC), F32)
        ref[ER - 8:ER, :] = jnp.zeros((8, EC), F32)
    got[...] = jnp.zeros_like(got)
    corner[...] = jnp.zeros_like(corner)
    side_w[...] = jnp.zeros_like(side_w)
    side_s[...] = jnp.zeros_like(side_s)
    for ref, nf in ((cw, 2), (cs, 3)):
        for f in range(nf):
            ref[f, 0:8, :] = jnp.zeros((8, 128), F32)
            ref[f, WR - 8:WR, :] = jnp.zeros((8, 128), F32)

    barrier = pltpu.get_barrier_semaphore()
    for da, dc in DIRS:
        @pl.when(there(da, dc))
        def _(da=da, dc=dc):
            pl.semaphore_signal(barrier, inc=1, device_id=device(da, dc), device_id_type=MESH)
    rows_near = 1 + jnp.where(a > 0, 1, 0) + jnp.where(a < mesh_rows - 1, 1, 0)
    cols_near = 1 + jnp.where(c > 0, 1, 0) + jnp.where(c < mesh_cols - 1, 1, 0)
    pl.semaphore_wait(barrier, rows_near * cols_near - 1)

    for cp in loads:
        cp.wait()
    ext[4, TOP:TOP + TR, 0:TC] = wraw[...].astype(F32)

    lane = iota((TR, 128), 1)
    packed = jnp.zeros((TR, 128), F32)
    for f in range(5):
        left = ext[f, TOP:TOP + TR, 0:128]
        right = ext[f, TOP:TOP + TR, TC - 128:TC]
        edge = pltpu.roll(jnp.where(lane >= 120, right, left), 16 * f + 8, 1)
        packed = jnp.where(lax.shift_right_logical(lane, 4) == f, edge, packed)
    pack[...] = packed
    packt[...] = packed.T.reshape(8, 2, 8, 128)

    def fine_copy(n):
        da, dc = DIRS[n]
        if da == 0:
            which = 0 if dc > 0 else 1
            src, dst = packt.at[0:5, which], got.at[0:5, which]
        elif dc == 0:
            src = ext.at[:, TOP:TOP + 8, 0:TC] if da < 0 else ext.at[:, TOP + TR - 8:TOP + TR, 0:TC]
            dst = ext.at[:, TOP + TR:TOP + TR + 8, 0:TC] if da < 0 else ext.at[:, TOP - 8:TOP, 0:TC]
        else:
            src = pack.at[0:8] if da < 0 else pack.at[TR - 8:TR]
            dst = corner.at[1 if da < 0 else 0, 0 if dc > 0 else 1]
        return pltpu.make_async_remote_copy(
            src_ref=src, dst_ref=dst, send_sem=f_send.at[n], recv_sem=f_recv.at[n],
            device_id=device(da, dc), device_id_type=MESH)

    def coarse_copy(ts, side, field, send, recv):
        def make(n):
            da, dc = DIRS[n]
            if dc == 0:
                src = field.at[:, 8:16] if da < 0 else field.at[:, CR:CR + 8]
                dst = field.at[:, CR + 8:CR + 16] if da < 0 else field.at[:, 0:8]
            else:
                src = ts.at[0 if dc < 0 else 1]
                at = CC if dc < 0 else 120
                dst = side.at[{-1: 2, 0: 1, 1: 0}[da], at:at + 8]
            return pltpu.make_async_remote_copy(
                src_ref=src, dst_ref=dst, send_sem=send.at[n], recv_sem=recv.at[n],
                device_id=device(da, dc), device_id_type=MESH)
        return make

    def start_all(make):
        for n, (da, dc) in enumerate(DIRS):
            @pl.when(there(da, dc))
            def _(n=n):
                make(n).start()

    def wait_recv_all(make):
        for n, (da, dc) in enumerate(DIRS):
            @pl.when(there(-da, -dc))
            def _(n=n):
                make(n).wait_recv()

    def wait_send_all(make):
        for n, (da, dc) in enumerate(DIRS):
            @pl.when(there(da, dc))
            def _(n=n):
                make(n).wait_send()

    copy_w = coarse_copy(ts_w, side_w, cw, w_send, w_recv)
    copy_s = coarse_copy(ts_s, side_s, cs, c_send, c_recv)
    start_all(fine_copy)

    pool = (lax.shift_right_logical(iota((TC, 128), 0), 2) == iota((TC, 128), 1)).astype(F32).astype(BF16)
    edge_row = iota((16, TC), 0)
    edge_row = jnp.where(edge_row < 8, edge_row, edge_row + (CC - 16))
    pool_edge = (lax.shift_right_logical(iota((16, TC), 1), 2) == edge_row).astype(F32).astype(BF16)

    def restrict(first, nf, scale, ts, field):
        tall = []
        for f in range(nf):
            wide = []
            for h in range(2):
                n = 2 * (first + f) + h
                total = planes[n, pl.ds(0, CR, stride=4), :]
                for k in range(1, 4):
                    total = total + planes[n, pl.ds(k, CR, stride=4), :]
                wide.append(total * scale)
            tall.append(jnp.concatenate(wide, axis=1))
        tall.append(jnp.zeros((TR - nf * CR, TC), F32))
        high, low = halves(jnp.concatenate(tall, axis=0))
        edges = dot_nt(pool_edge, high) + dot_nt(pool_edge, low)
        ts[0] = edges[0:8]
        ts[1] = edges[8:16]
        coarse = dot(high, pool) + dot(low, pool)
        for f in range(nf):
            field[f, 8:8 + CR] = coarse[f * CR:(f + 1) * CR]

    def widen(field, side, nf):
        up, mid, down = (side[k].T for k in range(3))
        out = []
        for f in range(nf):
            r = f * CR
            out.append(jnp.concatenate([
                field[f, 0:8] + up[r + CR - 8:r + CR],
                field[f, 8:8 + CR] + mid[r:r + CR],
                field[f, CR + 8:WR] + down[r:r + 8],
            ], axis=0))
        return out

    for h in range(2):
        planes[6 + h] = ext[3, TOP:TOP + TR, 128 * h:128 * h + 128]
        planes[8 + h] = ext[4, TOP:TOP + TR, 128 * h:128 * h + 128]
    restrict(3, 2, 1.0 / 16.0, ts_w, cw)
    start_all(copy_w)

    ext_row = a * TR - TOP + iota((ER, 8), 0)
    ext_col = iota((EC, 8), 0)
    ext_col = c * TC + jnp.where(ext_col < TC + 64, ext_col, ext_col - EC)
    for step in range(STEPS):
        cells = cells_ref[step:step + 1, :]
        row_hit = jnp.where(ext_row == lax.div(cells, total_cols), press_ref[...], 0.0)
        col_hit = jnp.where(ext_col == lax.rem(cells, total_cols), 1.0, 0.0)
        forc[step] = lax.dot_general(
            row_hit, col_hit, (((1,), (1,)), ((), ())),
            precision=lax.Precision.HIGHEST, preferred_element_type=F32)

    wait_recv_all(fine_copy)
    is_right = (lane & 15) >= 8
    mid = got[...].reshape(TR, 128).T
    top = jnp.where(is_right[0:8], corner[0, 1], corner[0, 0])
    bottom = jnp.where(is_right[0:8], corner[1, 1], corner[1, 0])
    halo = jnp.concatenate([top, mid, bottom], axis=0)
    halo_lane = iota((TR + 16, 128), 1)
    for f in range(5):
        moved = pltpu.roll(halo, 120 - 16 * f, 1)
        ext[f, TOP - 8:TOP + TR + 8, TC:EC] = jnp.where((halo_lane < 8) | (halo_lane >= 120), moved, 0.0)

    surface, along, cross = ext.at[0], ext.at[1], ext.at[2]
    for step in range(STEPS):
        raised = r1 if step == 0 else r2
        for r, n in ALL:
            keep = slice(8, 8 + n)
            wide = slice(r - 8, r + n + 8)
            here = slice(r, r + n)
            depth = ext[3, wide, :]
            du = depth * along[wide, :]
            dv = depth[keep] * cross[here, :]
            flux = (row_next(du, keep) - row_prev(du, keep)) + (col_next(dv) - col_prev(dv))
            raised[here, :] = ext[4, here, :] * (
                surface[here, :] - (0.5 * CONTINUITY) * flux + forc[step, here, :])
        if step == STEPS - 1:
            surface_store = pltpu.make_async_copy(
                raised.at[TOP:TOP + TR, 0:TC], s_out, store_sem.at[0])
            surface_store.start()
        for r, n in ALL:
            keep = slice(8, 8 + n)
            x = raised[r - 8:r + n + 8, :]
            mid = x[keep]
            curv[r:r + n, :] = (
                row_next(x, keep) + row_prev(x, keep) + col_next(mid) + col_prev(mid) - 4.0 * mid)
        for r, n in (ALL if step < STEPS - 1 else OWN):
            keep = slice(8, 8 + n)
            here = slice(r, r + n)
            x = raised[r - 8:r + n + 8, :]
            k = curv[r - 8:r + n + 8, :]
            depth = ext[3, here, :]
            wet = ext[4, here, :]
            disp = depth * depth * (1.0 / 3.0)
            push_a = (row_next(x, keep) - row_prev(x, keep)) + disp * (row_next(k, keep) - row_prev(k, keep))
            x = x[keep]
            k = k[keep]
            push_c = (col_next(x) - col_prev(x)) + disp * (col_next(k) - col_prev(k))
            u = wet * (along[here, :] - (0.5 * MOMENTUM) * push_a)
            v = wet * (cross[here, :] - (0.5 * MOMENTUM) * push_c)
            speed[0, here, :] = u
            speed[1, here, :] = v
            if (r, n) in OWN:
                pot = POTENTIAL * x * x
                stress = (depth * u * u + pot, depth * u * v, depth * v * v + pot)
                at = slice(r - TOP, r - TOP + n)
                for f in range(3):
                    for h in range(2):
                        part = stress[f][:, 128 * h:128 * h + 128]
                        if step > 0:
                            part = part + planes[2 * f + h, at]
                        planes[2 * f + h, at] = part
        surface, along, cross = raised, speed.at[0], speed.at[1]

    restrict(0, 3, 1.0 / (16.0 * STEPS), ts_s, cs)
    start_all(copy_s)
    speed_stores = [
        pltpu.make_async_copy(speed.at[0, TOP:TOP + TR, 0:TC], u_out, store_sem.at[1]),
        pltpu.make_async_copy(speed.at[1, TOP:TOP + TR, 0:TC], v_out, store_sem.at[2]),
    ]
    for cp in speed_stores:
        cp.start()

    cols_out = spread(TC, 128, 1, (128, TC), 0, True)
    cols_out = jnp.concatenate([cols_out, cols_out], axis=0)
    rows_out = spread(TR, WR, 0, (TR, WR), 8, False)
    rows_out = jnp.concatenate([rows_out, rows_out], axis=1)
    wait_recv_all(copy_w)
    depth, wet = widen(cw, side_w, 2)
    inside = depth > 0.25
    inv_depth = 1.0 / jnp.maximum(depth, 0.25)

    wait_recv_all(copy_s)
    s0, s1, s2 = widen(cs, side_s, 3)

    def dr(x):
        return 0.5 * (pltpu.roll(x, WR - 1, 0) - pltpu.roll(x, 1, 0))

    def dc(x):
        return 0.5 * (col_next(x) - col_prev(x))

    def laplace(x):
        return pltpu.roll(x, WR - 1, 0) + pltpu.roll(x, 1, 0) + col_next(x) + col_prev(x) - 4.0 * x

    force_a = -(dr(s0) + dc(s1)) * inv_depth
    force_c = -(dr(s1) + dc(s2)) * inv_depth
    flow_a = wet * (CIRC_FORCE * force_a)
    flow_c = wet * (CIRC_FORCE * force_c)
    elevation = jnp.zeros_like(depth)
    for _ in range(CIRC - 1):
        level = elevation - CIRC_LEVEL * (dr(depth * flow_a) + dc(depth * flow_c))
        elevation = jnp.where(inside, level, 0.0)
        flow_a, flow_c = (
            wet * (flow_a + CIRC_FORCE * (force_a - dr(elevation))
                   - FRICTION * flow_a * inv_depth + VISCOSITY * laplace(flow_a)),
            wet * (flow_c + CIRC_FORCE * (force_c - dc(elevation))
                   - FRICTION * flow_c * inv_depth + VISCOSITY * laplace(flow_c)),
        )

    high, low = halves(jnp.concatenate([flow_a, flow_c], axis=0))
    wide = dot(jnp.concatenate([high, low], axis=1), cols_out)
    high, low = halves(jnp.concatenate([wide[0:WR], wide[WR:2 * WR]], axis=1))
    fine = dot(rows_out, jnp.concatenate([high, low], axis=0))
    mask = ext[4, TOP:TOP + TR, 0:TC]
    cur[0] = fine[:, 0:TC] * mask
    cur[1] = fine[:, TC:2 * TC] * mask
    last = [
        pltpu.make_async_copy(cur.at[0], ca_out, store_sem.at[3]),
        pltpu.make_async_copy(cur.at[1], cc_out, store_sem.at[4]),
    ]
    for cp in last:
        cp.start()
    surface_store.wait()
    for cp in speed_stores:
        cp.wait()
    wait_send_all(fine_copy)
    wait_send_all(copy_w)
    wait_send_all(copy_s)
    for cp in last:
        cp.wait()


def solution(mesh):
    mesh_rows, mesh_cols = mesh.shape["along"], mesh.shape["cross"]
    hbm = pl.BlockSpec(memory_space=pl.ANY)
    vmem = pl.BlockSpec(memory_space=pltpu.VMEM)

    def per_device(surface, along_speed, cross_speed, water_depth, wet_mask, ship_cells, ship_pressure):
        tile = jax.ShapeDtypeStruct((TR, TC), F32)
        sems = [pltpu.SemaphoreType.DMA((8,))] * 6
        return pl.pallas_call(
            functools.partial(kernel, mesh_rows, mesh_cols),
            out_shape=[tile] * 5,
            in_specs=[hbm] * 5 + [vmem] * 2,
            out_specs=[hbm] * 5,
            scratch_shapes=[
                pltpu.VMEM((5, ER, EC), F32),
                pltpu.VMEM((2, ER, EC), F32),
                pltpu.VMEM((TR, TC), jnp.int32),
                pltpu.VMEM((STEPS, ER, EC), F32),
                pltpu.VMEM((ER, EC), F32),
                pltpu.VMEM((ER, EC), F32),
                pltpu.VMEM((ER, EC), F32),
                pltpu.VMEM((10, TR, 128), F32),
                pltpu.VMEM((TR, 128), F32),
                pltpu.VMEM((8, 2, 8, 128), F32),
                pltpu.VMEM((8, 2, 8, 128), F32),
                pltpu.VMEM((2, 2, 8, 128), F32),
                pltpu.VMEM((2, 8, 128), F32),
                pltpu.VMEM((2, 8, 128), F32),
                pltpu.VMEM((3, 128, 128), F32),
                pltpu.VMEM((3, 128, 128), F32),
                pltpu.VMEM((2, WR, 128), F32),
                pltpu.VMEM((3, WR, 128), F32),
                pltpu.VMEM((2, TR, TC), F32),
                pltpu.SemaphoreType.DMA((5,)),
                pltpu.SemaphoreType.DMA((5,)),
            ] + sems,
            compiler_params=pltpu.CompilerParams(
                collective_id=0, has_side_effects=True, vmem_limit_bytes=32 * 1024 * 1024),
        )(surface, along_speed, cross_speed, water_depth, wet_mask, ship_cells,
          ship_pressure.reshape(1, ship_pressure.shape[0]))

    tiled = P("along", "cross")
    return jax.shard_map(
        per_device,
        mesh=mesh,
        in_specs=(tiled,) * 5 + (P(), P()),
        out_specs=(tiled,) * 5,
        check_vma=False,
    )
```

```python
import functools

import jax
import jax.numpy as jnp
from jax import lax
from jax.experimental import pallas as pl
from jax.experimental.pallas import tpu as pltpu
from jax.sharding import PartitionSpec as P

STEPS = 2
CIRC = 3
CONTINUITY = 0.25
MOMENTUM = 0.3
POTENTIAL = 0.5
CIRC_LEVEL = 0.2
CIRC_FORCE = 0.3
FRICTION = 0.1
VISCOSITY = 0.1

MESH = pl.DeviceIdType.MESH
F32 = jnp.float32
BF16 = jnp.bfloat16

TR = 128
TC = 256
TOP = 16
ER = TR + 2 * TOP
EC = TC + 128
CR = TR // 4
CC = TC // 4
WR = CR + 16
CHUNK = 32
OWN = [(r, CHUNK) for r in range(TOP, TOP + TR, CHUNK)]
ALL = [(TOP - 8, 8)] + OWN + [(TOP + TR, 8)]
DIRS = [(0, -1), (0, 1), (-1, -1), (-1, 1), (1, -1), (1, 1), (-1, 0), (1, 0)]


def iota(shape, dim):
    return lax.broadcasted_iota(jnp.int32, shape, dim)


def halves(x):
    high = x.astype(BF16)
    return high, (x - high.astype(F32)).astype(BF16)


def dot(x, y):
    return jnp.dot(x, y, preferred_element_type=F32)


def dot_nt(x, y):
    return lax.dot_general(x, y, (((1,), (1,)), ((), ())), preferred_element_type=F32)


def row_next(x, keep):
    return pltpu.roll(x, x.shape[0] - 1, 0)[keep]


def row_prev(x, keep):
    return pltpu.roll(x, 1, 0)[keep]


def col_next(x):
    return pltpu.roll(x, x.shape[1] - 1, 1)


def col_prev(x):
    return pltpu.roll(x, 1, 1)


def spread(fine, coarse, fine_dim, shape, first, wrap):
    f = iota(shape, fine_dim)
    c = iota(shape, 1 - fine_dim)
    base = lax.shift_right_logical(f, 2) + first
    k = f & 3
    weight = jnp.where((k == 0) | (k == 3), 0.375, 0.125)
    other = base + jnp.where(k < 2, -1, 1)
    if wrap:
        other = other & (coarse - 1)
    zero = jnp.zeros(shape, F32)
    return (jnp.where(c == base, 1.0 - weight, zero) + jnp.where(c == other, weight, zero)).astype(BF16)


def kernel(
    mesh_rows, mesh_cols,
    s_in, u_in, v_in, d_in, w_in, cells_in, press_in,
    r2, u_out, v_out, flow_out, mask_out,
    ext, wraw, cells_ref, press_ref, forc, r1, curv, planes, pack, packt, got, corner,
    ts_w, ts_s, side_w, side_s, cw, cs,
    load_sem, f_send, f_recv, w_send, w_recv, c_send, c_recv,
):
    a = lax.axis_index("along")
    c = lax.axis_index("cross")
    total_cols = TC * mesh_cols
    outs = (r2, u_out, v_out)

    def there(da, dc):
        ok = None
        for cond in ([a > 0] if da < 0 else [a < mesh_rows - 1] if da > 0 else []) + (
            [c > 0] if dc < 0 else [c < mesh_cols - 1] if dc > 0 else []
        ):
            ok = cond if ok is None else ok & cond
        return ok

    def device(da, dc):
        return (a + da, c + dc)

    barrier = pltpu.get_barrier_semaphore()
    for da, dc in DIRS:
        @pl.when(there(da, dc))
        def _(da=da, dc=dc):
            pl.semaphore_signal(barrier, inc=1, device_id=device(da, dc), device_id_type=MESH)

    loads = []
    for k, src in enumerate((s_in, u_in, v_in, d_in)):
        loads.append(pltpu.make_async_copy(src, ext.at[k, TOP:TOP + TR, 0:TC], load_sem.at[k]))
    loads.append(pltpu.make_async_copy(w_in, wraw, load_sem.at[4]))
    loads.append(pltpu.make_async_copy(cells_in, cells_ref, load_sem.at[5]))
    loads.append(pltpu.make_async_copy(press_in, press_ref, load_sem.at[6]))
    for cp in loads:
        cp.start()

    for f in range(5):
        ext[f, 0:8, :] = jnp.zeros((8, EC), F32)
        ext[f, ER - 8:ER, :] = jnp.zeros((8, EC), F32)
    for ref in (r1, curv, *outs):
        ref[0:8, :] = jnp.zeros((8, EC), F32)
        ref[ER - 8:ER, :] = jnp.zeros((8, EC), F32)
    for side in (side_w, side_s):
        for k in range(3):
            side[k, 0:CC] = jnp.zeros((CC, 128), F32)
            side[k, CC + 8:120] = jnp.zeros((112 - CC, 128), F32)
    for da, dc in DIRS:
        @pl.when(jnp.logical_not(there(da, dc)))
        def _(da=da, dc=dc):
            if dc == 0:
                at = TOP - 8 if da < 0 else TOP + TR
                for f in range(5):
                    ext[f, at:at + 8, 0:TC] = jnp.zeros((8, TC), F32)
                at = 0 if da < 0 else WR - 8
                for ref, nf in ((cw, 2), (cs, 3)):
                    for f in range(nf):
                        ref[f, at:at + 8] = jnp.zeros((8, 128), F32)
                return
            right = 1 if dc > 0 else 0
            if da == 0:
                for f in range(5):
                    got[f, right] = jnp.zeros((8, 128), F32)
            else:
                corner[0 if da < 0 else 1, right] = jnp.zeros((8, 128), F32)
            at = CC if right else 120
            for side in (side_w, side_s):
                side[da + 1, at:at + 8] = jnp.zeros((8, 128), F32)

    rows_near = 1 + jnp.where(a > 0, 1, 0) + jnp.where(a < mesh_rows - 1, 1, 0)
    cols_near = 1 + jnp.where(c > 0, 1, 0) + jnp.where(c < mesh_cols - 1, 1, 0)
    for cp in loads:
        cp.wait()
    own_wet = wraw[...].astype(F32)
    ext[4, TOP:TOP + TR, 0:TC] = own_wet
    mask_out[...] = own_wet

    lane = iota((TR, 128), 1)
    packed = jnp.zeros((TR, 128), F32)
    for f in range(5):
        left = ext[f, TOP:TOP + TR, 0:128]
        right = ext[f, TOP:TOP + TR, TC - 128:TC]
        edge = pltpu.roll(jnp.where(lane >= 120, right, left), 16 * f + 8, 1)
        packed = jnp.where(lax.shift_right_logical(lane, 4) == f, edge, packed)
    pack[...] = packed
    packt[...] = packed.T.reshape(8, 2, 8, 128)

    def fine_copy(n):
        da, dc = DIRS[n]
        if da == 0:
            which = 0 if dc > 0 else 1
            src, dst = packt.at[0:5, which], got.at[0:5, which]
        elif dc == 0:
            src = ext.at[:, TOP:TOP + 8, 0:TC] if da < 0 else ext.at[:, TOP + TR - 8:TOP + TR, 0:TC]
            dst = ext.at[:, TOP + TR:TOP + TR + 8, 0:TC] if da < 0 else ext.at[:, TOP - 8:TOP, 0:TC]
        else:
            src = pack.at[0:8] if da < 0 else pack.at[TR - 8:TR]
            dst = corner.at[1 if da < 0 else 0, 0 if dc > 0 else 1]
        return pltpu.make_async_remote_copy(
            src_ref=src, dst_ref=dst, send_sem=f_send.at[n], recv_sem=f_recv.at[n],
            device_id=device(da, dc), device_id_type=MESH)

    def coarse_copy(ts, side, field, send, recv):
        def make(n):
            da, dc = DIRS[n]
            if dc == 0:
                src = field.at[:, 8:16] if da < 0 else field.at[:, CR:CR + 8]
                dst = field.at[:, CR + 8:CR + 16] if da < 0 else field.at[:, 0:8]
            else:
                src = ts.at[0 if dc < 0 else 1]
                at = CC if dc < 0 else 120
                dst = side.at[{-1: 2, 0: 1, 1: 0}[da], at:at + 8]
            return pltpu.make_async_remote_copy(
                src_ref=src, dst_ref=dst, send_sem=send.at[n], recv_sem=recv.at[n],
                device_id=device(da, dc), device_id_type=MESH)
        return make

    def start_all(make):
        for n, (da, dc) in enumerate(DIRS):
            @pl.when(there(da, dc))
            def _(n=n):
                make(n).start()

    def wait_recv_all(make):
        for n, (da, dc) in enumerate(DIRS):
            @pl.when(there(-da, -dc))
            def _(n=n):
                make(n).wait_recv()

    def wait_send_all(make):
        for n, (da, dc) in enumerate(DIRS):
            @pl.when(there(da, dc))
            def _(n=n):
                make(n).wait_send()

    pl.semaphore_wait(barrier, rows_near * cols_near - 1)
    copy_w = coarse_copy(ts_w, side_w, cw, w_send, w_recv)
    copy_s = coarse_copy(ts_s, side_s, cs, c_send, c_recv)
    start_all(fine_copy)

    pool = (lax.shift_right_logical(iota((TC, 128), 0), 2) == iota((TC, 128), 1)).astype(F32).astype(BF16)
    edge_row = iota((16, TC), 0)
    edge_row = jnp.where(edge_row < 8, edge_row, edge_row + (CC - 16))
    pool_edge = (lax.shift_right_logical(iota((16, TC), 1), 2) == edge_row).astype(F32).astype(BF16)

    def restrict(first, nf, scale, ts, field):
        tall = []
        for f in range(nf):
            wide = []
            for h in range(2):
                n = 2 * (first + f) + h
                total = planes[n, pl.ds(0, CR, stride=4), :]
                for k in range(1, 4):
                    total = total + planes[n, pl.ds(k, CR, stride=4), :]
                wide.append(total * scale)
            tall.append(jnp.concatenate(wide, axis=1))
        tall.append(jnp.zeros((TR - nf * CR, TC), F32))
        high, low = halves(jnp.concatenate(tall, axis=0))
        edges = dot_nt(pool_edge, high) + dot_nt(pool_edge, low)
        ts[0] = edges[0:8]
        ts[1] = edges[8:16]
        coarse = dot(high, pool) + dot(low, pool)
        for f in range(nf):
            field[f, 8:8 + CR] = coarse[f * CR:(f + 1) * CR]

    def widen(field, side, nf):
        up, mid, down = (side[k].T for k in range(3))
        out = []
        for f in range(nf):
            r = f * CR
            out.append(jnp.concatenate([
                field[f, 0:8] + up[r + CR - 8:r + CR],
                field[f, 8:8 + CR] + mid[r:r + CR],
                field[f, CR + 8:WR] + down[r:r + 8],
            ], axis=0))
        return out

    for h in range(2):
        planes[6 + h] = ext[3, TOP:TOP + TR, 128 * h:128 * h + 128]
        planes[8 + h] = ext[4, TOP:TOP + TR, 128 * h:128 * h + 128]
    restrict(3, 2, 1.0 / 16.0, ts_w, cw)
    start_all(copy_w)

    ext_row = a * TR - TOP + iota((ER, 8), 0)
    ext_col = iota((EC, 8), 0)
    ext_col = c * TC + jnp.where(ext_col < TC + 64, ext_col, ext_col - EC)
    for step in range(STEPS):
        cells = cells_ref[step:step + 1, :]
        row_hit = jnp.where(ext_row == lax.div(cells, total_cols), press_ref[...], 0.0)
        col_hit = jnp.where(ext_col == lax.rem(cells, total_cols), 1.0, 0.0)
        forc[step] = lax.dot_general(
            row_hit, col_hit, (((1,), (1,)), ((), ())),
            precision=lax.Precision.HIGHEST, preferred_element_type=F32)

    wait_recv_all(fine_copy)
    is_right = (lane & 15) >= 8
    mid = got[...].reshape(TR, 128).T
    top = jnp.where(is_right[0:8], corner[0, 1], corner[0, 0])
    bottom = jnp.where(is_right[0:8], corner[1, 1], corner[1, 0])
    halo = jnp.concatenate([top, mid, bottom], axis=0)
    halo_lane = iota((TR + 16, 128), 1)
    for f in range(5):
        moved = pltpu.roll(halo, 120 - 16 * f, 1)
        ext[f, TOP - 8:TOP + TR + 8, TC:EC] = jnp.where((halo_lane < 8) | (halo_lane >= 120), moved, 0.0)

    surface, along, cross = ext.at[0], ext.at[1], ext.at[2]
    for step in range(STEPS):
        raised = r1 if step == 0 else r2
        for r, n in ALL:
            keep = slice(8, 8 + n)
            wide = slice(r - 8, r + n + 8)
            here = slice(r, r + n)
            depth = ext[3, wide, :]
            du = depth * along[wide, :]
            dv = depth[keep] * cross[here, :]
            flux = (row_next(du, keep) - row_prev(du, keep)) + (col_next(dv) - col_prev(dv))
            raised[here, :] = ext[4, here, :] * (
                surface[here, :] - (0.5 * CONTINUITY) * flux + forc[step, here, :])
        for r, n in ALL:
            keep = slice(8, 8 + n)
            x = raised[r - 8:r + n + 8, :]
            mid = x[keep]
            curv[r:r + n, :] = (
                row_next(x, keep) + row_prev(x, keep) + col_next(mid) + col_prev(mid) - 4.0 * mid)
        for r, n in (ALL if step < STEPS - 1 else OWN):
            keep = slice(8, 8 + n)
            here = slice(r, r + n)
            x = raised[r - 8:r + n + 8, :]
            k = curv[r - 8:r + n + 8, :]
            depth = ext[3, here, :]
            wet = ext[4, here, :]
            disp = depth * depth * (1.0 / 3.0)
            push_a = (row_next(x, keep) - row_prev(x, keep)) + disp * (row_next(k, keep) - row_prev(k, keep))
            x = x[keep]
            k = k[keep]
            push_c = (col_next(x) - col_prev(x)) + disp * (col_next(k) - col_prev(k))
            u = wet * (along[here, :] - (0.5 * MOMENTUM) * push_a)
            v = wet * (cross[here, :] - (0.5 * MOMENTUM) * push_c)
            u_out[here, :] = u
            v_out[here, :] = v
            if (r, n) in OWN:
                pot = POTENTIAL * x * x
                stress = (depth * u * u + pot, depth * u * v, depth * v * v + pot)
                at = slice(r - TOP, r - TOP + n)
                for f in range(3):
                    for h in range(2):
                        part = stress[f][:, 128 * h:128 * h + 128]
                        if step > 0:
                            part = part + planes[2 * f + h, at]
                        planes[2 * f + h, at] = part
        surface, along, cross = raised, u_out, v_out

    restrict(0, 3, 1.0 / (16.0 * STEPS), ts_s, cs)
    start_all(copy_s)
    wait_recv_all(copy_w)
    depth, wet = widen(cw, side_w, 2)
    inside = depth > 0.25
    inv_depth = 1.0 / jnp.maximum(depth, 0.25)

    wait_recv_all(copy_s)
    s0, s1, s2 = widen(cs, side_s, 3)

    def dr(x):
        return 0.5 * (pltpu.roll(x, WR - 1, 0) - pltpu.roll(x, 1, 0))

    def dc(x):
        return 0.5 * (col_next(x) - col_prev(x))

    def laplace(x):
        return pltpu.roll(x, WR - 1, 0) + pltpu.roll(x, 1, 0) + col_next(x) + col_prev(x) - 4.0 * x

    force_a = -(dr(s0) + dc(s1)) * inv_depth
    force_c = -(dr(s1) + dc(s2)) * inv_depth
    flow_a = wet * (CIRC_FORCE * force_a)
    flow_c = wet * (CIRC_FORCE * force_c)
    elevation = jnp.zeros_like(depth)
    for _ in range(CIRC - 1):
        level = elevation - CIRC_LEVEL * (dr(depth * flow_a) + dc(depth * flow_c))
        elevation = jnp.where(inside, level, 0.0)
        flow_a, flow_c = (
            wet * (flow_a + CIRC_FORCE * (force_a - dr(elevation))
                   - FRICTION * flow_a * inv_depth + VISCOSITY * laplace(flow_a)),
            wet * (flow_c + CIRC_FORCE * (force_c - dc(elevation))
                   - FRICTION * flow_c * inv_depth + VISCOSITY * laplace(flow_c)),
        )

    flow_out[0] = flow_a
    flow_out[1] = flow_c
    wait_send_all(fine_copy)
    wait_send_all(copy_w)
    wait_send_all(copy_s)


def finish(s_ref, u_ref, v_ref, flow_ref, mask_ref, s_out, u_out, v_out, ca_out, cc_out, cur, store_sem):
    stores = [
        pltpu.make_async_copy(ref.at[TOP:TOP + TR, 0:TC], out, store_sem.at[k])
        for k, (ref, out) in enumerate(((s_ref, s_out), (u_ref, u_out), (v_ref, v_out)))
    ]
    for cp in stores:
        cp.start()
    cols_out = spread(TC, 128, 1, (128, TC), 0, True)
    cols_out = jnp.concatenate([cols_out, cols_out], axis=0)
    rows_out = spread(TR, WR, 0, (TR, WR), 8, False)
    rows_out = jnp.concatenate([rows_out, rows_out], axis=1)
    high, low = halves(flow_ref[...].reshape(2 * WR, 128))
    wide = dot(jnp.concatenate([high, low], axis=1), cols_out)
    high, low = halves(jnp.concatenate([wide[0:WR], wide[WR:2 * WR]], axis=1))
    fine = dot(rows_out, jnp.concatenate([high, low], axis=0))
    mask = mask_ref[...]
    cur[0] = fine[:, 0:TC] * mask
    cur[1] = fine[:, TC:2 * TC] * mask
    last = [
        pltpu.make_async_copy(cur.at[0], ca_out, store_sem.at[3]),
        pltpu.make_async_copy(cur.at[1], cc_out, store_sem.at[4]),
    ]
    for cp in last:
        cp.start()
    for cp in stores + last:
        cp.wait()


def solution(mesh):
    mesh_rows, mesh_cols = mesh.shape["along"], mesh.shape["cross"]
    hbm = pl.BlockSpec(memory_space=pltpu.HBM)
    vmem = pl.BlockSpec(memory_space=pltpu.VMEM)

    def shape(*dims):
        return jax.ShapeDtypeStruct(dims, F32)

    def per_device(surface, along_speed, cross_speed, water_depth, wet_mask, ship_cells, ship_pressure):
        ships = ship_pressure.shape[0]
        state = pl.pallas_call(
            functools.partial(kernel, mesh_rows, mesh_cols),
            out_shape=[shape(ER, EC)] * 3 + [shape(2, WR, 128), shape(TR, TC)],
            in_specs=[hbm] * 7,
            out_specs=[vmem] * 5,
            scratch_shapes=[
                pltpu.VMEM((5, ER, EC), F32),
                pltpu.VMEM((TR, TC), jnp.int32),
                pltpu.VMEM((STEPS, ships), jnp.int32),
                pltpu.VMEM((1, ships), F32),
                pltpu.VMEM((STEPS, ER, EC), F32),
                pltpu.VMEM((ER, EC), F32),
                pltpu.VMEM((ER, EC), F32),
                pltpu.VMEM((10, TR, 128), F32),
                pltpu.VMEM((TR, 128), F32),
                pltpu.VMEM((8, 2, 8, 128), F32),
                pltpu.VMEM((8, 2, 8, 128), F32),
                pltpu.VMEM((2, 2, 8, 128), F32),
                pltpu.VMEM((2, 8, 128), F32),
                pltpu.VMEM((2, 8, 128), F32),
                pltpu.VMEM((3, 128, 128), F32),
                pltpu.VMEM((3, 128, 128), F32),
                pltpu.VMEM((2, WR, 128), F32),
                pltpu.VMEM((3, WR, 128), F32),
                pltpu.SemaphoreType.DMA((7,)),
            ] + [pltpu.SemaphoreType.DMA((8,))] * 6,
            compiler_params=pltpu.CompilerParams(
                collective_id=0, has_side_effects=True, vmem_limit_bytes=32 * 1024 * 1024),
        )(*(pltpu.with_memory_space_constraint(x, pltpu.HBM) for x in (
            surface, along_speed, cross_speed, water_depth, wet_mask, ship_cells,
            ship_pressure.reshape(1, ships))))
        return pl.pallas_call(
            finish,
            out_shape=[shape(TR, TC)] * 5,
            in_specs=[vmem] * 5,
            out_specs=[hbm] * 5,
            scratch_shapes=[pltpu.VMEM((2, TR, TC), F32), pltpu.SemaphoreType.DMA((5,))],
            compiler_params=pltpu.CompilerParams(vmem_limit_bytes=16 * 1024 * 1024),
        )(*state)

    tiled = P("along", "cross")
    return jax.shard_map(
        per_device,
        mesh=mesh,
        in_specs=(tiled,) * 5 + (P(), P()),
        out_specs=(tiled,) * 5,
        check_vma=False,
    )
```

```python
import functools

import jax
import jax.numpy as jnp
from jax import lax
from jax.experimental import pallas as pl
from jax.experimental.pallas import tpu as pltpu
from jax.sharding import PartitionSpec as P

STEPS = 2
CIRC = 3
CONTINUITY = 0.25
MOMENTUM = 0.3
POTENTIAL = 0.5
CIRC_LEVEL = 0.2
CIRC_FORCE = 0.3
FRICTION = 0.1
VISCOSITY = 0.1

MESH = pl.DeviceIdType.MESH
F32 = jnp.float32
BF16 = jnp.bfloat16

TR = 128
TC = 256
TOP = 16
ER = TR + 2 * TOP
EC = 128
SIDE = 58
CR = TR // 4
CC = TC // 4
WR = CR + 16
CHUNK = 32
OWN = [(r, CHUNK) for r in range(TOP, TOP + TR, CHUNK)]
ALL = [(TOP - 8, 8)] + OWN + [(TOP + TR, 8)]
CROSS = [(0, -1), (0, 1)]
ALONG = [(-1, 0), (1, 0)]
DIRS = CROSS + [(-1, -1), (-1, 1), (1, -1), (1, 1)] + ALONG
HALO = 6


def iota(shape, dim):
    return lax.broadcasted_iota(jnp.int32, shape, dim)


def halves(x):
    high = x.astype(BF16)
    return high, (x - high.astype(F32)).astype(BF16)


def dot(x, y):
    return jnp.dot(x, y, preferred_element_type=F32)


def dot_nt(x, y):
    return lax.dot_general(x, y, (((1,), (1,)), ((), ())), preferred_element_type=F32)


def row_next(x, keep):
    return pltpu.roll(x, x.shape[0] - 1, 0)[keep]


def row_prev(x, keep):
    return pltpu.roll(x, 1, 0)[keep]


def col_next(x):
    return pltpu.roll(x, x.shape[1] - 1, 1)


def col_prev(x):
    return pltpu.roll(x, 1, 1)


def slant(x, step):
    row = iota(x.shape, 0)
    for bit in (1, 2, 4):
        if step * bit % 128:
            x = jnp.where((row & bit) != 0, pltpu.roll(x, step * bit % 128, 1), x)
    return x


def spread(fine, coarse, fine_dim, shape, first, wrap):
    f = iota(shape, fine_dim)
    c = iota(shape, 1 - fine_dim)
    base = lax.shift_right_logical(f, 2) + first
    k = f & 3
    weight = jnp.where((k == 0) | (k == 3), 0.375, 0.125)
    other = base + jnp.where(k < 2, -1, 1)
    if wrap:
        other = other & (coarse - 1)
    zero = jnp.zeros(shape, F32)
    return (jnp.where(c == base, 1.0 - weight, zero) + jnp.where(c == other, weight, zero)).astype(BF16)


def kernel(
    mesh_rows, mesh_cols,
    s_in, u_in, v_in, d_in, w_in, cells_in, press_in,
    s_out, u_out, v_out, flow_out, mask_out,
    ext, wraw, cells_ref, press_ref, forc, r1, curv, planes,
    e_ext, e_forc, e_r1, e_s, e_u, e_v, e_curv, e_planes,
    packt, got, corner_send, corner, corner_s_send, corner_s,
    ts_w, ts_s, side_w, side_s, cw, cs,
    load_sem, f_send, f_recv, w_send, w_recv, c_send, c_recv,
):
    a = lax.axis_index("along")
    c = lax.axis_index("cross")
    total_cols = TC * mesh_cols

    def there(da, dc):
        ok = None
        for cond in ([a > 0] if da < 0 else [a < mesh_rows - 1] if da > 0 else []) + (
            [c > 0] if dc < 0 else [c < mesh_cols - 1] if dc > 0 else []
        ):
            ok = cond if ok is None else ok & cond
        return ok

    def device(da, dc):
        return (a + da, c + dc)

    barrier = pltpu.get_barrier_semaphore()
    for da, dc in DIRS:
        @pl.when(there(da, dc))
        def _(da=da, dc=dc):
            pl.semaphore_signal(barrier, inc=1, device_id=device(da, dc), device_id_type=MESH)

    loads = []
    for k, src in enumerate((s_in, u_in, v_in, d_in)):
        loads.append(pltpu.make_async_copy(src, ext.at[k, TOP:TOP + TR, 0:TC], load_sem.at[k]))
    loads.append(pltpu.make_async_copy(w_in, wraw, load_sem.at[4]))
    loads.append(pltpu.make_async_copy(cells_in, cells_ref, load_sem.at[5]))
    loads.append(pltpu.make_async_copy(press_in, press_ref, load_sem.at[6]))
    for cp in loads:
        cp.start()

    for ref in (ext, e_ext):
        for f in range(5):
            ref[f, 0:8, :] = jnp.zeros((8, ref.shape[2]), F32)
            ref[f, ER - 8:ER, :] = jnp.zeros((8, ref.shape[2]), F32)
    for ref in (r1, s_out, u_out, v_out, curv, e_r1, e_s, e_u, e_v, e_curv):
        ref[0:8, :] = jnp.zeros((8, ref.shape[1]), F32)
        ref[ER - 8:ER, :] = jnp.zeros((8, ref.shape[1]), F32)
    for side in (side_w, side_s):
        side[0:CC] = jnp.zeros((CC, 128), F32)
        side[CC + 8:120] = jnp.zeros((112 - CC, 128), F32)
    for da, dc in DIRS:
        @pl.when(jnp.logical_not(there(da, dc)))
        def _(da=da, dc=dc):
            if dc == 0:
                at = TOP - 8 if da < 0 else TOP + TR
                for f in range(5):
                    ext[f, at:at + 8, 0:TC] = jnp.zeros((8, TC), F32)
                at = 0 if da < 0 else WR - 8
                for ref, nf in ((cw, 2), (cs, 3)):
                    for f in range(nf):
                        ref[f, at:at + 8] = jnp.zeros((8, 128), F32)
                return
            right = 1 if dc > 0 else 0
            if da == 0:
                got[32 * right:32 * right + 32] = jnp.zeros((32, 128), F32)
                at = CC if right else 120
                side_w[at:at + 8] = jnp.zeros((8, 128), F32)
                side_s[at:at + 8] = jnp.zeros((8, 128), F32)
            else:
                corner[0 if da < 0 else 1, right] = jnp.zeros((2, 128), F32)
                corner_s[0 if da < 0 else 1, right] = jnp.zeros((2, 128), F32)

    rows_near = 1 + jnp.where(a > 0, 1, 0) + jnp.where(a < mesh_rows - 1, 1, 0)
    cols_near = 1 + jnp.where(c > 0, 1, 0) + jnp.where(c < mesh_cols - 1, 1, 0)
    for cp in loads:
        cp.wait()
    own_wet = wraw[...].astype(F32)
    ext[4, TOP:TOP + TR, 0:TC] = own_wet
    mask_out[...] = own_wet

    lane = iota((TR, 128), 1)
    packed = jnp.zeros((TR, 128), F32)
    for f in range(5):
        for part, start, move in ((1, HALO * f, HALO * f + HALO), (0, 32 + HALO * f, 32 + HALO * f)):
            edge = pltpu.roll(ext[f, TOP:TOP + TR, 128 * part:128 * part + 128], move, 1)
            packed = jnp.where((lane >= start) & (lane < start + HALO), edge, packed)
    packt[...] = packed.T
    for t in range(2):
        rows = packed[0:8] if t == 0 else packed[TR - 8:TR]
        for side in range(2):
            block = rows if side == 0 else pltpu.roll(rows, 96, 1)
            block = jnp.where(lane[0:8] < 32, block, 0.0)
            block = slant(block, 32)
            corner_send[t, side, 0:1] = jnp.sum(block[0:4], axis=0, keepdims=True)
            corner_send[t, side, 1:2] = jnp.sum(block[4:8], axis=0, keepdims=True)

    def fine_copy(n):
        da, dc = DIRS[n]
        if da == 0:
            at = 0 if dc > 0 else 32
            src, dst = packt.at[at:at + 32], got.at[at:at + 32]
        elif dc == 0:
            src = ext.at[:, TOP:TOP + 8, 0:TC] if da < 0 else ext.at[:, TOP + TR - 8:TOP + TR, 0:TC]
            dst = ext.at[:, TOP + TR:TOP + TR + 8, 0:TC] if da < 0 else ext.at[:, TOP - 8:TOP, 0:TC]
        else:
            side = 0 if dc > 0 else 1
            src = corner_send.at[0 if da < 0 else 1, side]
            dst = corner.at[1 if da < 0 else 0, side]
        return pltpu.make_async_remote_copy(
            src_ref=src, dst_ref=dst, send_sem=f_send.at[n], recv_sem=f_recv.at[n],
            device_id=device(da, dc), device_id_type=MESH)

    def coarse_copy(ts, side, field, send, recv):
        def make(n):
            da, dc = DIRS[n]
            if dc == 0:
                src = field.at[:, 8:16] if da < 0 else field.at[:, CR:CR + 8]
                dst = field.at[:, CR + 8:CR + 16] if da < 0 else field.at[:, 0:8]
            elif da == 0:
                at = CC if dc < 0 else 120
                src = ts.at[0 if dc < 0 else 1]
                dst = side.at[at:at + 8]
            else:
                src = corner_s_send.at[0 if da < 0 else 1, 0 if dc > 0 else 1]
                dst = corner_s.at[1 if da < 0 else 0, 0 if dc > 0 else 1]
            return pltpu.make_async_remote_copy(
                src_ref=src, dst_ref=dst, send_sem=send.at[n], recv_sem=recv.at[n],
                device_id=device(da, dc), device_id_type=MESH)
        return make

    def start_all(make, chosen=DIRS):
        for da, dc in chosen:
            n = DIRS.index((da, dc))
            @pl.when(there(da, dc))
            def _(n=n):
                make(n).start()

    def wait_recv_all(make, chosen=DIRS):
        for da, dc in chosen:
            n = DIRS.index((da, dc))
            @pl.when(there(-da, -dc))
            def _(n=n):
                make(n).wait_recv()

    def wait_send_all(make, chosen=DIRS):
        for da, dc in chosen:
            n = DIRS.index((da, dc))
            @pl.when(there(da, dc))
            def _(n=n):
                make(n).wait_send()

    pl.semaphore_wait(barrier, rows_near * cols_near - 1)
    copy_w = coarse_copy(ts_w, side_w, cw, w_send, w_recv)
    copy_s = coarse_copy(ts_s, side_s, cs, c_send, c_recv)
    start_all(fine_copy)

    def pool_matrix(width, wanted, shift, split):
        col = iota((width, 128), 0)
        col = jnp.where(col < split, col - shift[0], col - shift[1])
        to = iota((width, 128), 1)
        hit = (lax.shift_right_arithmetic(col, 2) == to) & wanted(to) & (to < CC)
        one = jnp.where(hit, 1.0, 0.0).astype(BF16)
        return jnp.concatenate([one, one], axis=0)

    def edge_matrix(width, shift, split):
        to = iota((16, width), 0)
        to = jnp.where(to < 8, to, to + (CC - 16))
        col = iota((16, width), 1)
        col = jnp.where(col < split, col - shift[0], col - shift[1])
        one = jnp.where(lax.shift_right_arithmetic(col, 2) == to, 1.0, 0.0).astype(BF16)
        return jnp.concatenate([one, one], axis=1)

    def row_means(ref, first, nf, nh, scale):
        tall = []
        for f in range(nf):
            wide = []
            for h in range(nh):
                n = nh * (first + f) + h
                total = ref[n, pl.ds(0, CR, stride=4), :]
                for k in range(1, 4):
                    total = total + ref[n, pl.ds(k, CR, stride=4), :]
                wide.append(total * scale)
            tall.append(jnp.concatenate(wide, axis=1) if nh > 1 else wide[0])
        tall.append(jnp.zeros((TR - nf * CR, 128 * nh), F32))
        return jnp.concatenate(halves(jnp.concatenate(tall, axis=0)), axis=1)

    own = (0, 0)
    sides = (HALO, 128 - HALO - TC)
    pool_all = pool_matrix(TC, lambda j: j >= 0, own, TC)
    pool_mid = pool_matrix(TC, lambda j: (j >= 8) & (j < CC - 8), own, TC)
    pool_side = pool_matrix(EC, lambda j: (j < 8) | (j >= CC - 8), sides, EC // 2)
    edge_all = edge_matrix(TC, own, TC)
    edge_side = edge_matrix(EC, sides, EC // 2)

    for h in range(2):
        planes[6 + h] = ext[3, TOP:TOP + TR, 128 * h:128 * h + 128]
        planes[8 + h] = ext[4, TOP:TOP + TR, 128 * h:128 * h + 128]
    means = row_means(planes, 3, 2, 2, 1.0 / 16.0)
    edges = dot_nt(edge_all, means)
    ts_w[0] = edges[0:8]
    ts_w[1] = edges[8:16]
    coarse = dot(means, pool_all)
    for f in range(2):
        cw[f, 8:8 + CR] = coarse[f * CR:(f + 1) * CR]
    start_all(copy_w, CROSS)

    ext_row = a * TR - TOP + iota((ER, 8), 0)
    own_col = c * TC + iota((TC, 8), 0)
    side_col = iota((EC, 8), 0)
    side_col = c * TC + jnp.where(side_col < EC // 2, side_col - sides[0], side_col - sides[1])
    for step in range(STEPS):
        cells = cells_ref[step:step + 1, :]
        row_hit = jnp.where(ext_row == lax.div(cells, total_cols), press_ref[...], 0.0)
        for ref, col in ((forc, own_col), (e_forc, side_col)):
            col_hit = jnp.where(col == lax.rem(cells, total_cols), 1.0, 0.0)
            ref[step] = lax.dot_general(
                row_hit, col_hit, (((1,), (1,)), ((), ())),
                precision=lax.Precision.HIGHEST, preferred_element_type=F32)

    def waves(base, force, first, last, bend, u_ref, v_ref, stress_ref, nh):
        surface, along, cross = base.at[0], base.at[1], base.at[2]
        for step in range(STEPS):
            raised = first if step == 0 else last
            for r, n in ALL:
                keep = slice(8, 8 + n)
                wide = slice(r - 8, r + n + 8)
                here = slice(r, r + n)
                depth = base[3, wide, :]
                du = depth * along[wide, :]
                dv = depth[keep] * cross[here, :]
                flux = (row_next(du, keep) - row_prev(du, keep)) + (col_next(dv) - col_prev(dv))
                raised[here, :] = base[4, here, :] * (
                    surface[here, :] - (0.5 * CONTINUITY) * flux + force[step, here, :])
            for r, n in ALL:
                keep = slice(8, 8 + n)
                x = raised[r - 8:r + n + 8, :]
                mid = x[keep]
                bend[r:r + n, :] = (
                    row_next(x, keep) + row_prev(x, keep) + col_next(mid) + col_prev(mid) - 4.0 * mid)
            for r, n in (ALL if step < STEPS - 1 else OWN):
                keep = slice(8, 8 + n)
                here = slice(r, r + n)
                x = raised[r - 8:r + n + 8, :]
                k = bend[r - 8:r + n + 8, :]
                depth = base[3, here, :]
                wet = base[4, here, :]
                disp = depth * depth * (1.0 / 3.0)
                push_a = (row_next(x, keep) - row_prev(x, keep)) + disp * (row_next(k, keep) - row_prev(k, keep))
                x = x[keep]
                k = k[keep]
                push_c = (col_next(x) - col_prev(x)) + disp * (col_next(k) - col_prev(k))
                u = wet * (along[here, :] - (0.5 * MOMENTUM) * push_a)
                v = wet * (cross[here, :] - (0.5 * MOMENTUM) * push_c)
                u_ref[here, :] = u
                v_ref[here, :] = v
                if (r, n) in OWN:
                    pot = POTENTIAL * x * x
                    stress = (depth * u * u + pot, depth * u * v, depth * v * v + pot)
                    at = slice(r - TOP, r - TOP + n)
                    for f in range(3):
                        for h in range(nh):
                            part = stress[f][:, 128 * h:128 * h + 128]
                            if step > 0:
                                part = part + stress_ref[nh * f + h, at]
                            stress_ref[nh * f + h, at] = part
            surface, along, cross = raised, u_ref, v_ref

    wait_recv_all(fine_copy, ALONG)
    waves(ext, forc, r1, s_out, curv, u_out, v_out, planes, 2)
    coarse_mid = dot(row_means(planes, 0, 3, 2, 1.0 / (16.0 * STEPS)), pool_mid)

    rows = slice(TOP - 8, TOP + TR + 8)
    halo_lane = iota((TR + 16, 128), 1)
    for f in range(5):
        left = pltpu.roll(ext[f, rows, 0:128], HALO, 1)
        right = pltpu.roll(ext[f, rows, 128:256], 128 - HALO, 1)
        e_ext[f, rows, :] = jnp.where(halo_lane < EC // 2, left, right)

    wait_recv_all(fine_copy, DIRS[:6])

    def open_corner(t):
        rows = jnp.zeros((8, 128), F32)
        for side in range(2):
            block = jnp.concatenate([
                jnp.broadcast_to(corner[t, side, 0:1], (4, 128)),
                jnp.broadcast_to(corner[t, side, 1:2], (4, 128))], axis=0)
            block = slant(pltpu.roll(block, 32, 1) if side else block, 96)
            rows = jnp.where(lax.shift_right_logical(lane[0:8], 5) == side, block, rows)
        return rows

    halo = jnp.concatenate([open_corner(0), got[...].T, open_corner(1)], axis=0)
    for f in range(5):
        left = pltpu.roll(halo, (128 - HALO * f) % 128, 1)
        right = pltpu.roll(halo, 128 - HALO - 32 - HALO * f, 1)
        e_ext[f, rows, :] = jnp.where(
            halo_lane < HALO, left, jnp.where(halo_lane >= 128 - HALO, right, e_ext[f, rows, :]))
    waves(e_ext, e_forc, e_r1, e_s, e_curv, e_u, e_v, e_planes, 1)

    means = row_means(e_planes, 0, 3, 1, 1.0 / (16.0 * STEPS))
    edges = dot_nt(edge_side, means)
    ts_s[0] = edges[0:8]
    ts_s[1] = edges[8:16]
    start_all(copy_s, CROSS)
    coarse = dot(means, pool_side)
    small = iota((8, 128), 1)
    for t in range(2):
        for side in range(2):
            at = 0 if side else CC - 8
            packed = [jnp.zeros((8, 128), F32)] * 2
            for f in range(3):
                r = f * CR + (0 if t == 0 else CR - 8)
                block = jnp.where((small >= at) & (small < at + 8), coarse[r:r + 8], 0.0)
                block = pltpu.roll(block, (128 - at + 64 * (f % 2)) % 128, 1, stride=8, stride_axis=0)
                packed[f // 2] = packed[f // 2] + block
            for k in range(2):
                corner_s_send[t, side, k:k + 1] = jnp.sum(packed[k], axis=0, keepdims=True)
    start_all(copy_s, DIRS[2:6])
    coarse = coarse + coarse_mid
    for f in range(3):
        cs[f, 8:8 + CR] = coarse[f * CR:(f + 1) * CR]
    start_all(copy_s, ALONG)

    rows = slice(TOP, TOP + TR)
    for ref, edge in ((s_out, e_s), (u_out, e_u), (v_out, e_v)):
        ref[rows, 0:128] = jnp.where(lane < 16, pltpu.roll(edge[rows], 128 - HALO, 1), ref[rows, 0:128])
        ref[rows, 128:256] = jnp.where(lane >= 112, pltpu.roll(edge[rows], HALO, 1), ref[rows, 128:256])

    wait_recv_all(copy_w, CROSS)
    mid = side_w[...].T
    for f in range(2):
        cw[f, 8:8 + CR] = cw[f, 8:8 + CR] + mid[f * CR:(f + 1) * CR]
    start_all(copy_w, ALONG)
    wait_recv_all(copy_w, ALONG)
    depth, wet = cw[0], cw[1]
    inside = depth > 0.25
    inv_depth = 1.0 / jnp.maximum(depth, 0.25)

    wait_recv_all(copy_s)
    mid = side_s[...].T
    wide = []
    for f in range(3):
        ends = []
        for t in range(2):
            rows = cs[f, 0:8] if t == 0 else cs[f, WR - 8:WR]
            for side in range(2):
                at = CC if side else 120
                block = jnp.broadcast_to(corner_s[t, side, f // 2:f // 2 + 1], (8, 128))
                block = slant(pltpu.roll(block, (at - 64 * (f % 2)) % 128, 1), 120)
                rows = rows + jnp.where((small >= at) & (small < at + 8), block, 0.0)
            ends.append(rows)
        wide.append(jnp.concatenate(
            [ends[0], cs[f, 8:8 + CR] + mid[f * CR:(f + 1) * CR], ends[1]], axis=0))
    s0, s1, s2 = wide

    def dr(x):
        return 0.5 * (pltpu.roll(x, WR - 1, 0) - pltpu.roll(x, 1, 0))

    def dc(x):
        return 0.5 * (col_next(x) - col_prev(x))

    def laplace(x):
        return pltpu.roll(x, WR - 1, 0) + pltpu.roll(x, 1, 0) + col_next(x) + col_prev(x) - 4.0 * x

    force_a = -(dr(s0) + dc(s1)) * inv_depth
    force_c = -(dr(s1) + dc(s2)) * inv_depth
    flow_a = wet * (CIRC_FORCE * force_a)
    flow_c = wet * (CIRC_FORCE * force_c)
    elevation = jnp.zeros_like(depth)
    for _ in range(CIRC - 1):
        level = elevation - CIRC_LEVEL * (dr(depth * flow_a) + dc(depth * flow_c))
        elevation = jnp.where(inside, level, 0.0)
        flow_a, flow_c = (
            wet * (flow_a + CIRC_FORCE * (force_a - dr(elevation))
                   - FRICTION * flow_a * inv_depth + VISCOSITY * laplace(flow_a)),
            wet * (flow_c + CIRC_FORCE * (force_c - dc(elevation))
                   - FRICTION * flow_c * inv_depth + VISCOSITY * laplace(flow_c)),
        )

    flow_out[0] = flow_a
    flow_out[1] = flow_c
    wait_send_all(fine_copy)
    wait_send_all(copy_w, CROSS + ALONG)
    wait_send_all(copy_s)


def finish(s_ref, u_ref, v_ref, flow_ref, mask_ref, s_out, u_out, v_out, ca_out, cc_out, cur, store_sem):
    stores = [
        pltpu.make_async_copy(ref.at[TOP:TOP + TR, 0:TC], out, store_sem.at[k])
        for k, (ref, out) in enumerate(((s_ref, s_out), (u_ref, u_out), (v_ref, v_out)))
    ]
    for cp in stores:
        cp.start()
    cols_out = spread(TC, 128, 1, (128, TC), 0, True)
    cols_out = jnp.concatenate([cols_out, cols_out], axis=0)
    rows_out = spread(TR, WR, 0, (TR, WR), 8, False)
    rows_out = jnp.concatenate([rows_out, rows_out], axis=1)
    high, low = halves(flow_ref[...].reshape(2 * WR, 128))
    wide = dot(jnp.concatenate([high, low], axis=1), cols_out)
    high, low = halves(jnp.concatenate([wide[0:WR], wide[WR:2 * WR]], axis=1))
    fine = dot(rows_out, jnp.concatenate([high, low], axis=0))
    mask = mask_ref[...]
    cur[0] = fine[:, 0:TC] * mask
    cur[1] = fine[:, TC:2 * TC] * mask
    last = [
        pltpu.make_async_copy(cur.at[0], ca_out, store_sem.at[3]),
        pltpu.make_async_copy(cur.at[1], cc_out, store_sem.at[4]),
    ]
    for cp in last:
        cp.start()
    for cp in stores + last:
        cp.wait()


def solution(mesh):
    mesh_rows, mesh_cols = mesh.shape["along"], mesh.shape["cross"]
    hbm = pl.BlockSpec(memory_space=pltpu.HBM)
    vmem = pl.BlockSpec(memory_space=pltpu.VMEM)

    def shape(*dims):
        return jax.ShapeDtypeStruct(dims, F32)

    def per_device(surface, along_speed, cross_speed, water_depth, wet_mask, ship_cells, ship_pressure):
        ships = ship_pressure.shape[0]
        state = pl.pallas_call(
            functools.partial(kernel, mesh_rows, mesh_cols),
            out_shape=[shape(ER, TC)] * 3 + [shape(2, WR, 128), shape(TR, TC)],
            in_specs=[hbm] * 7,
            out_specs=[vmem] * 5,
            scratch_shapes=[
                pltpu.VMEM((5, ER, TC), F32),
                pltpu.VMEM((TR, TC), jnp.int32),
                pltpu.VMEM((STEPS, ships), jnp.int32),
                pltpu.VMEM((1, ships), F32),
                pltpu.VMEM((STEPS, ER, TC), F32),
                pltpu.VMEM((ER, TC), F32),
                pltpu.VMEM((ER, TC), F32),
                pltpu.VMEM((10, TR, 128), F32),
                pltpu.VMEM((5, ER, EC), F32),
                pltpu.VMEM((STEPS, ER, EC), F32),
            ] + [pltpu.VMEM((ER, EC), F32)] * 5 + [
                pltpu.VMEM((3, TR, 128), F32),
                pltpu.VMEM((128, 128), F32),
                pltpu.VMEM((128, 128), F32),
            ] + [pltpu.VMEM((2, 2, 2, 128), F32)] * 4 + [
                pltpu.VMEM((2, 8, 128), F32),
                pltpu.VMEM((2, 8, 128), F32),
                pltpu.VMEM((128, 128), F32),
                pltpu.VMEM((128, 128), F32),
                pltpu.VMEM((2, WR, 128), F32),
                pltpu.VMEM((3, WR, 128), F32),
                pltpu.SemaphoreType.DMA((7,)),
            ] + [pltpu.SemaphoreType.DMA((8,))] * 6,
            compiler_params=pltpu.CompilerParams(
                collective_id=0, has_side_effects=True, vmem_limit_bytes=32 * 1024 * 1024),
        )(*(pltpu.with_memory_space_constraint(x, pltpu.HBM) for x in (
            surface, along_speed, cross_speed, water_depth, wet_mask, ship_cells,
            ship_pressure.reshape(1, ships))))
        return pl.pallas_call(
            finish,
            out_shape=[shape(TR, TC)] * 5,
            in_specs=[vmem] * 5,
            out_specs=[hbm] * 5,
            scratch_shapes=[pltpu.VMEM((2, TR, TC), F32), pltpu.SemaphoreType.DMA((5,))],
            compiler_params=pltpu.CompilerParams(vmem_limit_bytes=16 * 1024 * 1024),
        )(*state)

    tiled = P("along", "cross")
    return jax.shard_map(
        per_device,
        mesh=mesh,
        in_specs=(tiled,) * 5 + (P(), P()),
        out_specs=(tiled,) * 5,
        check_vma=False,
    )
```

```python
import functools

import jax
import jax.numpy as jnp
from jax import lax
from jax.experimental import pallas as pl
from jax.experimental.pallas import tpu as pltpu
from jax.sharding import PartitionSpec as P

STEPS = 2
CIRC = 3
CONTINUITY = 0.25
MOMENTUM = 0.3
POTENTIAL = 0.5
CIRC_LEVEL = 0.2
CIRC_FORCE = 0.3
FRICTION = 0.1
VISCOSITY = 0.1

MESH = pl.DeviceIdType.MESH
F32 = jnp.float32
BF16 = jnp.bfloat16

TR = 128
TC = 256
TOP = 16
ER = TR + 2 * TOP
EC = 128
SIDE = 58
CR = TR // 4
CC = TC // 4
WR = CR + 16
CHUNK = 32
OWN = [(r, CHUNK) for r in range(TOP, TOP + TR, CHUNK)]
ALL = [(TOP - 8, 8)] + OWN + [(TOP + TR, 8)]
CROSS = [(0, -1), (0, 1)]
ALONG = [(-1, 0), (1, 0)]
DIRS = CROSS + [(-1, -1), (-1, 1), (1, -1), (1, 1)] + ALONG
HALO = 6
E_BOTH = [(TOP - 8, TR // 2 + 8), (TOP + TR // 2, TR // 2 + 8)]
E_OWN = [(TOP, TR // 2), (TOP + TR // 2, TR // 2)]
E_ALL = [(TOP - 8, 8)] + E_OWN + [(TOP + TR, 8)]


def iota(shape, dim):
    return lax.broadcasted_iota(jnp.int32, shape, dim)


def halves(x):
    high = x.astype(BF16)
    return high, (x - high.astype(F32)).astype(BF16)


def dot(x, y):
    return jnp.dot(x, y, preferred_element_type=F32)


def dot_nt(x, y):
    return lax.dot_general(x, y, (((1,), (1,)), ((), ())), preferred_element_type=F32)


def row_next(x, keep):
    return pltpu.roll(x, x.shape[0] - 1, 0)[keep]


def row_prev(x, keep):
    return pltpu.roll(x, 1, 0)[keep]


def col_next(x):
    return pltpu.roll(x, x.shape[1] - 1, 1)


def col_prev(x):
    return pltpu.roll(x, 1, 1)


def slant(x, step):
    row = iota(x.shape, 0)
    for bit in (1, 2, 4):
        if step * bit % 128:
            x = jnp.where((row & bit) != 0, pltpu.roll(x, step * bit % 128, 1), x)
    return x


def spread(fine, coarse, fine_dim, shape, first, wrap):
    f = iota(shape, fine_dim)
    c = iota(shape, 1 - fine_dim)
    base = lax.shift_right_logical(f, 2) + first
    k = f & 3
    weight = jnp.where((k == 0) | (k == 3), 0.375, 0.125)
    other = base + jnp.where(k < 2, -1, 1)
    if wrap:
        other = other & (coarse - 1)
    zero = jnp.zeros(shape, F32)
    return (jnp.where(c == base, 1.0 - weight, zero) + jnp.where(c == other, weight, zero)).astype(BF16)


def kernel(
    mesh_rows, mesh_cols,
    s_in, u_in, v_in, d_in, w_in, cells_in, press_in,
    s_out, u_out, v_out, flow_out, mask_out, cols_out, rows_out,
    ext, wraw, cells_ref, press_ref, forc, r1, curv, slope, planes,
    e_ext, e_forc, e_r1, e_s, e_u, e_v, e_curv, e_du, e_slope, e_planes,
    packt, got, corner_send, corner, corner_s_send, corner_s,
    ts_w, ts_s, side_w, side_s, cw, cs,
    load_sem, f_send, f_recv, w_send, w_recv, c_send, c_recv,
):
    a = lax.axis_index("along")
    c = lax.axis_index("cross")
    total_cols = TC * mesh_cols

    def there(da, dc):
        ok = None
        for cond in ([a > 0] if da < 0 else [a < mesh_rows - 1] if da > 0 else []) + (
            [c > 0] if dc < 0 else [c < mesh_cols - 1] if dc > 0 else []
        ):
            ok = cond if ok is None else ok & cond
        return ok

    def device(da, dc):
        return (a + da, c + dc)

    barrier = pltpu.get_barrier_semaphore()
    for da, dc in DIRS:
        @pl.when(there(da, dc))
        def _(da=da, dc=dc):
            pl.semaphore_signal(barrier, inc=1, device_id=device(da, dc), device_id_type=MESH)

    loads = []
    for k, src in enumerate((s_in, u_in, v_in, d_in)):
        loads.append(pltpu.make_async_copy(src, ext.at[k, TOP:TOP + TR, 0:TC], load_sem.at[k]))
    loads.append(pltpu.make_async_copy(w_in, wraw, load_sem.at[4]))
    loads.append(pltpu.make_async_copy(cells_in, cells_ref, load_sem.at[5]))
    loads.append(pltpu.make_async_copy(press_in, press_ref, load_sem.at[6]))
    for cp in loads:
        cp.start()

    for ref in (ext, e_ext):
        for f in range(5):
            ref[f, 0:8, :] = jnp.zeros((8, ref.shape[2]), F32)
            ref[f, ER - 8:ER, :] = jnp.zeros((8, ref.shape[2]), F32)
    for ref in (r1, s_out, u_out, v_out, curv, e_r1, e_s, e_u, e_v, e_curv):
        ref[0:8, :] = jnp.zeros((8, ref.shape[1]), F32)
        ref[ER - 8:ER, :] = jnp.zeros((8, ref.shape[1]), F32)
    for side in (side_w, side_s):
        side[0:CC] = jnp.zeros((CC, 128), F32)
        side[CC + 8:120] = jnp.zeros((112 - CC, 128), F32)
    for da, dc in DIRS:
        @pl.when(jnp.logical_not(there(da, dc)))
        def _(da=da, dc=dc):
            if dc == 0:
                at = TOP - 8 if da < 0 else TOP + TR
                for f in range(5):
                    ext[f, at:at + 8, 0:TC] = jnp.zeros((8, TC), F32)
                at = 0 if da < 0 else WR - 8
                for ref, nf in ((cw, 2), (cs, 3)):
                    for f in range(nf):
                        ref[f, at:at + 8] = jnp.zeros((8, 128), F32)
                return
            right = 1 if dc > 0 else 0
            if da == 0:
                got[32 * right:32 * right + 32] = jnp.zeros((32, 128), F32)
                at = CC if right else 120
                side_w[at:at + 8] = jnp.zeros((8, 128), F32)
                side_s[at:at + 8] = jnp.zeros((8, 128), F32)
            else:
                corner[0 if da < 0 else 1, right] = jnp.zeros((2, 128), F32)
                corner_s[0 if da < 0 else 1, right] = jnp.zeros((2, 128), F32)

    rows_near = 1 + jnp.where(a > 0, 1, 0) + jnp.where(a < mesh_rows - 1, 1, 0)
    cols_near = 1 + jnp.where(c > 0, 1, 0) + jnp.where(c < mesh_cols - 1, 1, 0)
    for cp in loads:
        cp.wait()
    own_wet = wraw[...].astype(F32)
    ext[4, TOP:TOP + TR, 0:TC] = own_wet
    mask_out[...] = own_wet

    lane = iota((TR, 128), 1)
    packed = jnp.zeros((TR, 128), F32)
    for f in range(5):
        for part, start, move in ((1, HALO * f, HALO * f + HALO), (0, 32 + HALO * f, 32 + HALO * f)):
            edge = pltpu.roll(ext[f, TOP:TOP + TR, 128 * part:128 * part + 128], move, 1)
            packed = jnp.where((lane >= start) & (lane < start + HALO), edge, packed)
    packt[...] = packed.T
    for t in range(2):
        rows = packed[0:8] if t == 0 else packed[TR - 8:TR]
        for side in range(2):
            block = jnp.where(lax.shift_right_logical(lane[0:8], 5) == side, rows, 0.0)
            block = slant(block, 32)
            corner_send[t, side, 0:1] = jnp.sum(block[0:4], axis=0, keepdims=True)
            corner_send[t, side, 1:2] = jnp.sum(block[4:8], axis=0, keepdims=True)

    def fine_copy(n):
        da, dc = DIRS[n]
        if da == 0:
            at = 0 if dc > 0 else 32
            src, dst = packt.at[at:at + 32], got.at[at:at + 32]
        elif dc == 0:
            src = ext.at[:, TOP:TOP + 8, 0:TC] if da < 0 else ext.at[:, TOP + TR - 8:TOP + TR, 0:TC]
            dst = ext.at[:, TOP + TR:TOP + TR + 8, 0:TC] if da < 0 else ext.at[:, TOP - 8:TOP, 0:TC]
        else:
            side = 0 if dc > 0 else 1
            src = corner_send.at[0 if da < 0 else 1, side]
            dst = corner.at[1 if da < 0 else 0, side]
        return pltpu.make_async_remote_copy(
            src_ref=src, dst_ref=dst, send_sem=f_send.at[n], recv_sem=f_recv.at[n],
            device_id=device(da, dc), device_id_type=MESH)

    def coarse_copy(ts, side, field, send, recv):
        def make(n):
            da, dc = DIRS[n]
            if dc == 0:
                src = field.at[:, 8:16] if da < 0 else field.at[:, CR:CR + 8]
                dst = field.at[:, CR + 8:CR + 16] if da < 0 else field.at[:, 0:8]
            elif da == 0:
                at = CC if dc < 0 else 120
                src = ts.at[0 if dc < 0 else 1]
                dst = side.at[at:at + 8]
            else:
                src = corner_s_send.at[0 if da < 0 else 1, 0 if dc > 0 else 1]
                dst = corner_s.at[1 if da < 0 else 0, 0 if dc > 0 else 1]
            return pltpu.make_async_remote_copy(
                src_ref=src, dst_ref=dst, send_sem=send.at[n], recv_sem=recv.at[n],
                device_id=device(da, dc), device_id_type=MESH)
        return make

    def start_all(make, chosen=DIRS):
        for da, dc in chosen:
            n = DIRS.index((da, dc))
            @pl.when(there(da, dc))
            def _(n=n):
                make(n).start()

    def wait_recv_all(make, chosen=DIRS):
        for da, dc in chosen:
            n = DIRS.index((da, dc))
            @pl.when(there(-da, -dc))
            def _(n=n):
                make(n).wait_recv()

    def wait_send_all(make, chosen=DIRS):
        for da, dc in chosen:
            n = DIRS.index((da, dc))
            @pl.when(there(da, dc))
            def _(n=n):
                make(n).wait_send()

    pl.semaphore_wait(barrier, rows_near * cols_near - 1)
    copy_w = coarse_copy(ts_w, side_w, cw, w_send, w_recv)
    copy_s = coarse_copy(ts_s, side_s, cs, c_send, c_recv)
    start_all(fine_copy, DIRS[2:6] + CROSS + ALONG)

    def pool_matrix(width, wanted, shift, split):
        col = iota((width, 128), 0)
        col = jnp.where(col < split, col - shift[0], col - shift[1])
        to = iota((width, 128), 1)
        hit = (lax.shift_right_arithmetic(col, 2) == to) & wanted(to) & (to < CC)
        one = jnp.where(hit, 1.0, 0.0).astype(BF16)
        return jnp.concatenate([one, one], axis=0)

    def edge_matrix(width, shift, split):
        to = iota((16, width), 0)
        to = jnp.where(to < 8, to, to + (CC - 16))
        col = iota((16, width), 1)
        col = jnp.where(col < split, col - shift[0], col - shift[1])
        one = jnp.where(lax.shift_right_arithmetic(col, 2) == to, 1.0, 0.0).astype(BF16)
        return jnp.concatenate([one, one], axis=1)

    def row_means(ref, first, nf, nh, scale):
        tall = []
        for f in range(nf):
            wide = []
            for h in range(nh):
                n = nh * (first + f) + h
                total = ref[n, pl.ds(0, CR, stride=4), :]
                for k in range(1, 4):
                    total = total + ref[n, pl.ds(k, CR, stride=4), :]
                wide.append(total * scale)
            tall.append(jnp.concatenate(wide, axis=1) if nh > 1 else wide[0])
        tall.append(jnp.zeros((TR - nf * CR, 128 * nh), F32))
        return jnp.concatenate(halves(jnp.concatenate(tall, axis=0)), axis=1)

    own = (0, 0)
    sides = (HALO, 128 - HALO - TC)
    pool_all = pool_matrix(TC, lambda j: j >= 0, own, TC)
    pool_mid = pool_matrix(TC, lambda j: (j >= 8) & (j < CC - 8), own, TC)
    pool_side = pool_matrix(EC, lambda j: (j < 8) | (j >= CC - 8), sides, EC // 2)
    edge_all = edge_matrix(TC, own, TC)
    edge_side = edge_matrix(EC, sides, EC // 2)

    for h in range(2):
        planes[6 + h] = ext[3, TOP:TOP + TR, 128 * h:128 * h + 128]
        planes[8 + h] = ext[4, TOP:TOP + TR, 128 * h:128 * h + 128]
    means = row_means(planes, 3, 2, 2, 1.0 / 16.0)
    edges = dot_nt(edge_all, means)
    ts_w[0] = edges[0:8]
    ts_w[1] = edges[8:16]
    coarse = dot(means, pool_all)
    for f in range(2):
        cw[f, 8:8 + CR] = coarse[f * CR:(f + 1) * CR]
    start_all(copy_w, CROSS)

    ext_row = a * TR - TOP + iota((ER, 8), 0)
    own_col = c * TC + iota((TC, 8), 0)
    side_col = iota((EC, 8), 0)
    side_col = c * TC + jnp.where(side_col < EC // 2, side_col - sides[0], side_col - sides[1])
    for step in range(STEPS):
        cells = cells_ref[step:step + 1, :]
        row_hit = jnp.where(ext_row == lax.div(cells, total_cols), press_ref[...], 0.0)
        for ref, col in ((forc, own_col), (e_forc, side_col)):
            col_hit = jnp.where(col == lax.rem(cells, total_cols), 1.0, 0.0)
            ref[step] = lax.dot_general(
                row_hit, col_hit, (((1,), (1,)), ((), ())),
                precision=lax.Precision.HIGHEST, preferred_element_type=F32)

    def own_waves():
        base, force, first, last, bend = ext, forc, r1, s_out, curv
        u_ref, v_ref, stress_ref, nh = u_out, v_out, planes, 2
        surface, along, cross = base.at[0], base.at[1], base.at[2]
        for step in range(STEPS):
            raised = first if step == 0 else last
            for r, n in ALL:
                keep = slice(8, 8 + n)
                wide = slice(r - 8, r + n + 8)
                here = slice(r, r + n)
                depth = base[3, wide, :]
                du = depth * along[wide, :]
                dv = depth[keep] * cross[here, :]
                flux = (row_next(du, keep) - row_prev(du, keep)) + (col_next(dv) - col_prev(dv))
                raised[here, :] = base[4, here, :] * (
                    surface[here, :] - (0.5 * CONTINUITY) * flux + force[step, here, :])
            for r, n in ALL:
                keep = slice(8, 8 + n)
                x = raised[r - 8:r + n + 8, :]
                mid = x[keep]
                down, up, right, left = row_next(x, keep), row_prev(x, keep), col_next(mid), col_prev(mid)
                slope[0, r:r + n, :] = down - up
                slope[1, r:r + n, :] = right - left
                bend[r:r + n, :] = down + up + right + left - 4.0 * mid
            for r, n in (ALL if step < STEPS - 1 else OWN):
                keep = slice(8, 8 + n)
                here = slice(r, r + n)
                x = raised[here, :]
                k = bend[r - 8:r + n + 8, :]
                depth = base[3, here, :]
                wet = base[4, here, :]
                disp = depth * depth * (1.0 / 3.0)
                push_a = slope[0, here, :] + disp * (row_next(k, keep) - row_prev(k, keep))
                k = k[keep]
                push_c = slope[1, here, :] + disp * (col_next(k) - col_prev(k))
                u = wet * (along[here, :] - (0.5 * MOMENTUM) * push_a)
                v = wet * (cross[here, :] - (0.5 * MOMENTUM) * push_c)
                u_ref[here, :] = u
                v_ref[here, :] = v
                if (r, n) in OWN:
                    pot = POTENTIAL * x * x
                    stress = (depth * u * u + pot, depth * u * v, depth * v * v + pot)
                    at = slice(r - TOP, r - TOP + n)
                    for f in range(3):
                        for h in range(nh):
                            part = stress[f][:, 128 * h:128 * h + 128]
                            if step > 0:
                                part = part + stress_ref[nh * f + h, at]
                            stress_ref[nh * f + h, at] = part
            surface, along, cross = raised, u_ref, v_ref

    def edge_waves():
        surface, along, cross = e_ext.at[0], e_ext.at[1], e_ext.at[2]
        for step in range(STEPS):
            raised = e_r1 if step == 0 else e_s
            e_du[...] = e_ext[3] * along[...]
            for r, n in E_BOTH:
                here, down, up = slice(r, r + n), slice(r + 1, r + n + 1), slice(r - 1, r + n - 1)
                dv = e_ext[3, here, :] * cross[here, :]
                flux = (e_du[down, :] - e_du[up, :]) + (col_next(dv) - col_prev(dv))
                raised[here, :] = e_ext[4, here, :] * (
                    surface[here, :] - (0.5 * CONTINUITY) * flux + e_forc[step, here, :])
            for r, n in E_BOTH:
                here, down, up = slice(r, r + n), slice(r + 1, r + n + 1), slice(r - 1, r + n - 1)
                mid = raised[here, :]
                right, left = col_next(mid), col_prev(mid)
                e_slope[here, :] = right - left
                e_curv[here, :] = raised[down, :] + raised[up, :] + right + left - 4.0 * mid
            for r, n in (E_ALL if step < STEPS - 1 else E_OWN):
                here, down, up = slice(r, r + n), slice(r + 1, r + n + 1), slice(r - 1, r + n - 1)
                depth = e_ext[3, here, :]
                wet = e_ext[4, here, :]
                disp = depth * depth * (1.0 / 3.0)
                k = e_curv[here, :]
                push_a = (raised[down, :] - raised[up, :]) + disp * (e_curv[down, :] - e_curv[up, :])
                push_c = e_slope[here, :] + disp * (col_next(k) - col_prev(k))
                u = wet * (along[here, :] - (0.5 * MOMENTUM) * push_a)
                v = wet * (cross[here, :] - (0.5 * MOMENTUM) * push_c)
                e_u[here, :] = u
                e_v[here, :] = v
                if (r, n) in E_OWN:
                    x = raised[here, :]
                    pot = POTENTIAL * x * x
                    at = slice(r - TOP, r - TOP + n)
                    for f, part in enumerate((depth * u * u + pot, depth * u * v, depth * v * v + pot)):
                        e_planes[f, at] = part + e_planes[f, at] if step > 0 else part
            surface, along, cross = raised, e_u, e_v

    def corner_matrix(side):
        lane_of = iota((EC, 128), 0)
        to = (iota((EC, 128), 1) & 7) * 4 + (HALO if side else 128 - HALO - 32)
        one = jnp.where((lane_of >= to) & (lane_of < to + 4), 1.0, 0.0).astype(BF16)
        return jnp.concatenate([one, one], axis=0)

    pool_corner = jnp.concatenate([corner_matrix(0), corner_matrix(1)], axis=1)

    def open_matrix(at):
        lane_of = iota((128, 128), 0)
        to = iota((128, 128), 1)
        one = jnp.where((to >= at) & (to < at + 8) & ((lane_of & 7) == to - at), 1.0, 0.0).astype(BF16)
        return jnp.concatenate([one, one], axis=0)

    open_corners = jnp.concatenate([open_matrix(120), open_matrix(CC)], axis=0)

    def fill_edge(r, n):
        at = iota((n, 128), 1)
        for f in range(5):
            left = pltpu.roll(ext[f, r:r + n, 0:128], HALO, 1)
            right = pltpu.roll(ext[f, r:r + n, 128:256], 128 - HALO, 1)
            both = jnp.where(at < EC // 2, left, right)
            e_ext[f, r:r + n, :] = jnp.where((at >= HALO) & (at < 128 - HALO), both, 0.0)

    fill_edge(TOP, TR)

    n_lane = iota((192, 5 * 128), 0)
    to = iota((192, 5 * 128), 1)
    to_field, to_lane = lax.shift_right_logical(to, 7), to & 127
    from_lane = HALO * to_field + jnp.where(to_lane < HALO, to_lane, to_lane - (128 - HALO) + 32)
    hit = ((n_lane & 63) == from_lane) & ((to_lane < HALO) | (to_lane >= 128 - HALO))
    place = jnp.where(hit, 1.0, 0.0).astype(BF16)

    wait_recv_all(fine_copy, ALONG)
    own_waves()
    coarse_mid = dot(row_means(planes, 0, 3, 2, 1.0 / (16.0 * STEPS)), pool_mid)

    fill_edge(TOP - 8, 8)
    fill_edge(TOP + TR, 8)
    def open_corner(t):
        rows = jnp.zeros((8, 128), F32)
        for side in range(2):
            block = jnp.concatenate([
                jnp.broadcast_to(corner[t, side, 0:1], (4, 128)),
                jnp.broadcast_to(corner[t, side, 1:2], (4, 128))], axis=0)
            block = slant(block, 96)
            rows = jnp.where(lax.shift_right_logical(lane[0:8], 5) == side, block, rows)
        return rows

    wait_recv_all(fine_copy, CROSS)
    arrived = got[0:64]
    high = arrived.astype(BF16)
    rest = arrived - high.astype(F32)
    middle = rest.astype(BF16)
    low = (rest - middle.astype(F32)).astype(BF16)
    moved = lax.dot_general(
        jnp.concatenate([high, middle, low], axis=0), place,
        (((0,), (0,)), ((), ())), preferred_element_type=F32)
    rows = slice(TOP, TOP + TR)
    for f in range(5):
        e_ext[f, rows, :] = e_ext[f, rows, :] + moved[:, 128 * f:128 * f + 128]
    wait_recv_all(fine_copy, DIRS[2:6])
    few = iota((8, 128), 1)
    for t in range(2):
        halo = open_corner(t)
        at = TOP - 8 if t == 0 else TOP + TR
        for f in range(5):
            left = pltpu.roll(halo, (128 - HALO * f) % 128, 1)
            right = pltpu.roll(halo, 128 - HALO - 32 - HALO * f, 1)
            e_ext[f, at:at + 8, :] = jnp.where(
                few < HALO, left, jnp.where(few >= 128 - HALO, right, e_ext[f, at:at + 8, :]))
    edge_waves()

    means = row_means(e_planes, 0, 3, 1, 1.0 / (16.0 * STEPS))
    edges = dot_nt(edge_side, means)
    ts_s[0] = edges[0:8]
    ts_s[1] = edges[8:16]
    start_all(copy_s, CROSS)
    coarse = dot(means, pool_corner)
    small = iota((8, 128), 1)
    group = lax.shift_right_logical(small, 3)
    row = iota((8, 128), 0)
    for t in range(2):
        for side in range(2):
            packed = [jnp.zeros((8, 128), F32)] * 2
            for f in range(3):
                r = f * CR + (0 if t == 0 else CR - 8)
                block = coarse[r:r + 8, 128 * side:128 * side + 128]
                packed[f // 2] = packed[f // 2] + jnp.where(group == row + 8 * (f % 2), block, 0.0)
            for k in range(2):
                corner_s_send[t, side, k:k + 1] = jnp.sum(packed[k], axis=0, keepdims=True)
    start_all(copy_s, DIRS[2:6])
    coarse = dot(means, pool_side) + coarse_mid
    for f in range(3):
        cs[f, 8:8 + CR] = coarse[f * CR:(f + 1) * CR]
    start_all(copy_s, ALONG)

    rows = slice(TOP, TOP + TR)
    for ref, edge in ((s_out, e_s), (u_out, e_u), (v_out, e_v)):
        ref[rows, 0:128] = jnp.where(lane < 16, pltpu.roll(edge[rows], 128 - HALO, 1), ref[rows, 0:128])
        ref[rows, 128:256] = jnp.where(lane >= 112, pltpu.roll(edge[rows], HALO, 1), ref[rows, 128:256])

    weights = spread(TC, 128, 1, (128, TC), 0, True)
    cols_out[...] = jnp.concatenate([weights, weights], axis=0)
    weights = spread(TR, WR, 0, (TR, WR), 8, False)
    rows_out[...] = jnp.concatenate([weights, weights], axis=1)

    wait_recv_all(copy_w, CROSS)
    mid = side_w[...].T
    for f in range(2):
        cw[f, 8:8 + CR] = cw[f, 8:8 + CR] + mid[f * CR:(f + 1) * CR]
    start_all(copy_w, ALONG)
    wait_recv_all(copy_w, ALONG)
    depth, wet = cw[0], cw[1]
    inside = depth > 0.25
    inv_depth = 1.0 / jnp.maximum(depth, 0.25)

    wait_send_all(fine_copy)
    wait_send_all(copy_w, CROSS)

    wait_recv_all(copy_s, CROSS + ALONG)
    mid = side_s[...].T
    wait_recv_all(copy_s, DIRS[2:6])
    blocks = []
    for t in range(2):
        for f in range(3):
            parts = []
            for side in range(2):
                block = jnp.broadcast_to(corner_s[t, side, f // 2:f // 2 + 1], (8, 128))
                parts += list(halves(jnp.where(group == row + 8 * (f % 2), block, 0.0)))
            blocks.append(jnp.concatenate([x.astype(F32) for x in parts], axis=1))
    ends = dot(jnp.concatenate(blocks, axis=0).astype(BF16), open_corners)
    wide = []
    for f in range(3):
        wide.append(jnp.concatenate([
            cs[f, 0:8] + ends[8 * f:8 * f + 8],
            cs[f, 8:8 + CR] + mid[f * CR:(f + 1) * CR],
            cs[f, WR - 8:WR] + ends[24 + 8 * f:32 + 8 * f]], axis=0))
    s0, s1, s2 = wide

    def dr(x):
        return 0.5 * (pltpu.roll(x, WR - 1, 0) - pltpu.roll(x, 1, 0))

    def dc(x):
        return 0.5 * (col_next(x) - col_prev(x))

    def laplace(x):
        return pltpu.roll(x, WR - 1, 0) + pltpu.roll(x, 1, 0) + col_next(x) + col_prev(x) - 4.0 * x

    force_a = -(dr(s0) + dc(s1)) * inv_depth
    force_c = -(dr(s1) + dc(s2)) * inv_depth
    flow_a = wet * (CIRC_FORCE * force_a)
    flow_c = wet * (CIRC_FORCE * force_c)
    elevation = jnp.zeros_like(depth)
    for _ in range(CIRC - 1):
        level = elevation - CIRC_LEVEL * (dr(depth * flow_a) + dc(depth * flow_c))
        elevation = jnp.where(inside, level, 0.0)
        flow_a, flow_c = (
            wet * (flow_a + CIRC_FORCE * (force_a - dr(elevation))
                   - FRICTION * flow_a * inv_depth + VISCOSITY * laplace(flow_a)),
            wet * (flow_c + CIRC_FORCE * (force_c - dc(elevation))
                   - FRICTION * flow_c * inv_depth + VISCOSITY * laplace(flow_c)),
        )

    flow_out[0] = flow_a
    flow_out[1] = flow_c
    wait_send_all(copy_w, ALONG)
    wait_send_all(copy_s)


def finish(s_ref, u_ref, v_ref, flow_ref, mask_ref, cols_ref, rows_ref, s_out, u_out, v_out, ca_out, cc_out, cur, store_sem):
    stores = [
        pltpu.make_async_copy(ref.at[TOP:TOP + TR, 0:TC], out, store_sem.at[k])
        for k, (ref, out) in enumerate(((s_ref, s_out), (u_ref, u_out), (v_ref, v_out)))
    ]
    for cp in stores:
        cp.start()
    high, low = halves(flow_ref[...].reshape(2 * WR, 128))
    wide = dot(jnp.concatenate([high, low], axis=1), cols_ref[...])
    high, low = halves(jnp.concatenate([wide[0:WR], wide[WR:2 * WR]], axis=1))
    fine = dot(rows_ref[...], jnp.concatenate([high, low], axis=0))
    mask = mask_ref[...]
    for k, out in enumerate((ca_out, cc_out)):
        cur[k] = fine[:, k * TC:k * TC + TC] * mask
        stores.append(pltpu.make_async_copy(cur.at[k], out, store_sem.at[3 + k]))
        stores[-1].start()
    for cp in stores:
        cp.wait()


def solution(mesh):
    mesh_rows, mesh_cols = mesh.shape["along"], mesh.shape["cross"]
    hbm = pl.BlockSpec(memory_space=pltpu.HBM)
    vmem = pl.BlockSpec(memory_space=pltpu.VMEM)

    def shape(*dims):
        return jax.ShapeDtypeStruct(dims, F32)

    def per_device(surface, along_speed, cross_speed, water_depth, wet_mask, ship_cells, ship_pressure):
        ships = ship_pressure.shape[0]
        state = pl.pallas_call(
            functools.partial(kernel, mesh_rows, mesh_cols),
            out_shape=[shape(ER, TC)] * 3 + [shape(2, WR, 128), shape(TR, TC)] + [
                jax.ShapeDtypeStruct((256, TC), BF16), jax.ShapeDtypeStruct((TR, 2 * WR), BF16)],
            in_specs=[hbm] * 7,
            out_specs=[vmem] * 7,
            scratch_shapes=[
                pltpu.VMEM((5, ER, TC), F32),
                pltpu.VMEM((TR, TC), jnp.int32),
                pltpu.VMEM((STEPS, ships), jnp.int32),
                pltpu.VMEM((1, ships), F32),
                pltpu.VMEM((STEPS, ER, TC), F32),
                pltpu.VMEM((ER, TC), F32),
                pltpu.VMEM((ER, TC), F32),
                pltpu.VMEM((2, ER, TC), F32),
                pltpu.VMEM((10, TR, 128), F32),
                pltpu.VMEM((5, ER, EC), F32),
                pltpu.VMEM((STEPS, ER, EC), F32),
            ] + [pltpu.VMEM((ER, EC), F32)] * 7 + [
                pltpu.VMEM((3, TR, 128), F32),
                pltpu.VMEM((128, 128), F32),
                pltpu.VMEM((128, 128), F32),
            ] + [pltpu.VMEM((2, 2, 2, 128), F32)] * 4 + [
                pltpu.VMEM((2, 8, 128), F32),
                pltpu.VMEM((2, 8, 128), F32),
                pltpu.VMEM((128, 128), F32),
                pltpu.VMEM((128, 128), F32),
                pltpu.VMEM((2, WR, 128), F32),
                pltpu.VMEM((3, WR, 128), F32),
                pltpu.SemaphoreType.DMA((7,)),
            ] + [pltpu.SemaphoreType.DMA((8,))] * 6,
            compiler_params=pltpu.CompilerParams(
                collective_id=0, has_side_effects=True, vmem_limit_bytes=32 * 1024 * 1024),
        )(*(pltpu.with_memory_space_constraint(x, pltpu.HBM) for x in (
            surface, along_speed, cross_speed, water_depth, wet_mask, ship_cells,
            ship_pressure.reshape(1, ships))))
        return pl.pallas_call(
            finish,
            out_shape=[shape(TR, TC)] * 5,
            in_specs=[vmem] * 7,
            out_specs=[hbm] * 5,
            scratch_shapes=[pltpu.VMEM((2, TR, TC), F32), pltpu.SemaphoreType.DMA((5,))],
            compiler_params=pltpu.CompilerParams(vmem_limit_bytes=16 * 1024 * 1024),
        )(*state)

    tiled = P("along", "cross")
    return jax.shard_map(
        per_device,
        mesh=mesh,
        in_specs=(tiled,) * 5 + (P(), P()),
        out_specs=(tiled,) * 5,
        check_vma=False,
    )
```

```python
import functools

import jax
import jax.numpy as jnp
from jax import lax
from jax.experimental import pallas as pl
from jax.experimental.pallas import tpu as pltpu
from jax.sharding import PartitionSpec as P

STEPS = 2
CIRC = 3
CONTINUITY = 0.25
MOMENTUM = 0.3
POTENTIAL = 0.5
CIRC_LEVEL = 0.2
CIRC_FORCE = 0.3
FRICTION = 0.1
VISCOSITY = 0.1

MESH = pl.DeviceIdType.MESH
F32 = jnp.float32
BF16 = jnp.bfloat16

TR = 128
TC = 256
TOP = 16
ER = TR + 2 * TOP
EC = 128
SIDE = 58
CR = TR // 4
CC = TC // 4
WR = CR + 16
CHUNK = 32
OWN = [(r, CHUNK) for r in range(TOP, TOP + TR, CHUNK)]
ALL = [(TOP - 8, 8)] + OWN + [(TOP + TR, 8)]
CROSS = [(0, -1), (0, 1)]
ALONG = [(-1, 0), (1, 0)]
DIRS = CROSS + [(-1, -1), (-1, 1), (1, -1), (1, 1)] + ALONG
HALO = 6
SENT = (5, 5, 5, 3, 5)
FIRST = (0, 5, 10, 20, 15)
E_BOTH = [(TOP - 8, TR // 2 + 8), (TOP + TR // 2, TR // 2 + 8)]
E_OWN = [(TOP, TR // 2), (TOP + TR // 2, TR // 2)]
E_ALL = [(TOP - 8, 8)] + E_OWN + [(TOP + TR, 8)]


def iota(shape, dim):
    return lax.broadcasted_iota(jnp.int32, shape, dim)


def halves(x):
    high = x.astype(BF16)
    return high, (x - high.astype(F32)).astype(BF16)


def dot(x, y):
    return jnp.dot(x, y, preferred_element_type=F32)


def dot_nt(x, y):
    return lax.dot_general(x, y, (((1,), (1,)), ((), ())), preferred_element_type=F32)


def row_next(x, keep):
    return pltpu.roll(x, x.shape[0] - 1, 0)[keep]


def row_prev(x, keep):
    return pltpu.roll(x, 1, 0)[keep]


def col_next(x):
    return pltpu.roll(x, x.shape[1] - 1, 1)


def col_prev(x):
    return pltpu.roll(x, 1, 1)


def slant(x, step):
    row = iota(x.shape, 0)
    for bit in (1, 2, 4):
        if step * bit % 128:
            x = jnp.where((row & bit) != 0, pltpu.roll(x, step * bit % 128, 1), x)
    return x


def spread(fine, coarse, fine_dim, shape, first, wrap):
    f = iota(shape, fine_dim)
    c = iota(shape, 1 - fine_dim)
    base = lax.shift_right_logical(f, 2) + first
    k = f & 3
    weight = jnp.where((k == 0) | (k == 3), 0.375, 0.125)
    other = base + jnp.where(k < 2, -1, 1)
    if wrap:
        other = other & (coarse - 1)
    zero = jnp.zeros(shape, F32)
    return (jnp.where(c == base, 1.0 - weight, zero) + jnp.where(c == other, weight, zero)).astype(BF16)


def kernel(
    mesh_rows, mesh_cols,
    s_in, u_in, v_in, d_in, w_in, cells_in, press_in,
    s_out, u_out, v_out, flow_out, mask_out, cols_out, rows_out,
    ext, wraw, cells_ref, press_ref, forc, r1, curv, slope, planes,
    e_ext, e_forc, e_r1, e_s, e_u, e_v, e_curv, e_du, e_slope, e_planes,
    packt, got, corner_send, corner, corner_s_send, corner_s,
    ts_w, ts_s, side_w, side_s, cw, cs,
    load_sem, f_send, f_recv, w_send, w_recv, c_send, c_recv,
):
    a = lax.axis_index("along")
    c = lax.axis_index("cross")
    total_cols = TC * mesh_cols

    def there(da, dc):
        ok = None
        for cond in ([a > 0] if da < 0 else [a < mesh_rows - 1] if da > 0 else []) + (
            [c > 0] if dc < 0 else [c < mesh_cols - 1] if dc > 0 else []
        ):
            ok = cond if ok is None else ok & cond
        return ok

    def device(da, dc):
        return (a + da, c + dc)

    barrier = pltpu.get_barrier_semaphore()
    for da, dc in DIRS[2:6] + CROSS + ALONG:
        @pl.when(there(da, dc))
        def _(da=da, dc=dc):
            pl.semaphore_signal(barrier, inc=1, device_id=device(da, dc), device_id_type=MESH)

    loads = []
    for k, src in enumerate((s_in, u_in, v_in, d_in)):
        loads.append(pltpu.make_async_copy(src, ext.at[k, TOP:TOP + TR, 0:TC], load_sem.at[k]))
    loads.append(pltpu.make_async_copy(w_in, wraw, load_sem.at[4]))
    loads.append(pltpu.make_async_copy(cells_in, cells_ref, load_sem.at[5]))
    loads.append(pltpu.make_async_copy(press_in, press_ref, load_sem.at[6]))
    for cp in loads:
        cp.start()

    for ref in (ext, e_ext):
        for f in range(5):
            ref[f, 0:8, :] = jnp.zeros((8, ref.shape[2]), F32)
            ref[f, ER - 8:ER, :] = jnp.zeros((8, ref.shape[2]), F32)
    for ref in (r1, s_out, u_out, v_out, curv, e_r1, e_s, e_u, e_v, e_curv):
        ref[0:8, :] = jnp.zeros((8, ref.shape[1]), F32)
        ref[ER - 8:ER, :] = jnp.zeros((8, ref.shape[1]), F32)
    for k in range(2):
        got[32 * k + 24:32 * k + 32] = jnp.zeros((8, 128), F32)
    for side in (side_w, side_s):
        side[0:CC] = jnp.zeros((CC, 128), F32)
        side[CC + 8:120] = jnp.zeros((112 - CC, 128), F32)
    for da, dc in DIRS:
        @pl.when(jnp.logical_not(there(da, dc)))
        def _(da=da, dc=dc):
            if dc == 0:
                at = TOP - 8 if da < 0 else TOP + TR
                for f in range(5):
                    ext[f, at:at + 8, 0:TC] = jnp.zeros((8, TC), F32)
                at = 0 if da < 0 else WR - 8
                for ref, nf in ((cw, 2), (cs, 3)):
                    for f in range(nf):
                        ref[f, at:at + 8] = jnp.zeros((8, 128), F32)
                return
            right = 1 if dc > 0 else 0
            if da == 0:
                got[32 * right:32 * right + 24] = jnp.zeros((24, 128), F32)
                at = CC if right else 120
                side_w[at:at + 8] = jnp.zeros((8, 128), F32)
                side_s[at:at + 8] = jnp.zeros((8, 128), F32)
            else:
                corner[0 if da < 0 else 1, right] = jnp.zeros((2, 128), F32)
                corner_s[0 if da < 0 else 1, right] = jnp.zeros((2, 128), F32)

    rows_near = 1 + jnp.where(a > 0, 1, 0) + jnp.where(a < mesh_rows - 1, 1, 0)
    cols_near = 1 + jnp.where(c > 0, 1, 0) + jnp.where(c < mesh_cols - 1, 1, 0)
    for cp in loads:
        cp.wait()
    own_wet = wraw[...].astype(F32)
    ext[4, TOP:TOP + TR, 0:TC] = own_wet
    mask_out[...] = own_wet

    lane = iota((TR, 128), 1)
    packed = jnp.zeros((TR, 128), F32)
    for part in range(2):
        surface, along, cross, depth, wet = (
            ext[f, TOP:TOP + TR, 128 * part:128 * part + 128] for f in range(5))
        far = 128 - lane if part else lane + 1
        product = (far == 4) | (far == 5)
        flow = depth * cross
        beyond = -col_prev(flow) if part else col_next(flow)
        edges = (
            jnp.where(far == 5, surface - (0.5 * CONTINUITY) * beyond, surface),
            jnp.where(product, depth * along, along),
            jnp.where(product, flow, cross),
            depth, wet)
        for f in range(5):
            start = FIRST[f] + (0 if part else 32)
            move = start + (SENT[f] if part else 0)
            packed = jnp.where(
                (lane >= start) & (lane < start + SENT[f]), pltpu.roll(edges[f], move, 1), packed)
    packt[...] = packed.T
    for t in range(2):
        rows = packed[0:8] if t == 0 else packed[TR - 8:TR]
        for side in range(2):
            block = jnp.where(lax.shift_right_logical(lane[0:8], 5) == side, rows, 0.0)
            block = slant(block, 32)
            corner_send[t, side, 0:1] = jnp.sum(block[0:4], axis=0, keepdims=True)
            corner_send[t, side, 1:2] = jnp.sum(block[4:8], axis=0, keepdims=True)

    def fine_copy(n):
        da, dc = DIRS[n]
        if da == 0:
            at = 0 if dc > 0 else 32
            src, dst = packt.at[at:at + 24], got.at[at:at + 24]
        elif dc == 0:
            src = ext.at[:, TOP:TOP + 8, 0:TC] if da < 0 else ext.at[:, TOP + TR - 8:TOP + TR, 0:TC]
            dst = ext.at[:, TOP + TR:TOP + TR + 8, 0:TC] if da < 0 else ext.at[:, TOP - 8:TOP, 0:TC]
        else:
            side = 0 if dc > 0 else 1
            src = corner_send.at[0 if da < 0 else 1, side]
            dst = corner.at[1 if da < 0 else 0, side]
        return pltpu.make_async_remote_copy(
            src_ref=src, dst_ref=dst, send_sem=f_send.at[n], recv_sem=f_recv.at[n],
            device_id=device(da, dc), device_id_type=MESH)

    def coarse_copy(ts, side, field, send, recv):
        def make(n):
            da, dc = DIRS[n]
            if dc == 0:
                src = field.at[:, 8:16] if da < 0 else field.at[:, CR:CR + 8]
                dst = field.at[:, CR + 8:CR + 16] if da < 0 else field.at[:, 0:8]
            elif da == 0:
                at = CC if dc < 0 else 120
                src = ts.at[0 if dc < 0 else 1]
                dst = side.at[at:at + 8]
            else:
                src = corner_s_send.at[0 if da < 0 else 1, 0 if dc > 0 else 1]
                dst = corner_s.at[1 if da < 0 else 0, 0 if dc > 0 else 1]
            return pltpu.make_async_remote_copy(
                src_ref=src, dst_ref=dst, send_sem=send.at[n], recv_sem=recv.at[n],
                device_id=device(da, dc), device_id_type=MESH)
        return make

    def start_all(make, chosen=DIRS):
        for da, dc in chosen:
            n = DIRS.index((da, dc))
            @pl.when(there(da, dc))
            def _(n=n):
                make(n).start()

    def wait_recv_all(make, chosen=DIRS):
        for da, dc in chosen:
            n = DIRS.index((da, dc))
            @pl.when(there(-da, -dc))
            def _(n=n):
                make(n).wait_recv()

    def wait_send_all(make, chosen=DIRS):
        for da, dc in chosen:
            n = DIRS.index((da, dc))
            @pl.when(there(da, dc))
            def _(n=n):
                make(n).wait_send()

    pl.semaphore_wait(barrier, rows_near * cols_near - 1)
    copy_w = coarse_copy(ts_w, side_w, cw, w_send, w_recv)
    copy_s = coarse_copy(ts_s, side_s, cs, c_send, c_recv)
    start_all(fine_copy, DIRS[2:6] + CROSS + ALONG)

    def pool_matrix(width, wanted, shift, split):
        col = iota((width, 128), 0)
        col = jnp.where(col < split, col - shift[0], col - shift[1])
        to = iota((width, 128), 1)
        hit = (lax.shift_right_arithmetic(col, 2) == to) & wanted(to) & (to < CC)
        one = jnp.where(hit, 1.0, 0.0).astype(BF16)
        return jnp.concatenate([one, one], axis=0)

    def edge_matrix(width, shift, split):
        to = iota((16, width), 0)
        to = jnp.where(to < 8, to, to + (CC - 16))
        col = iota((16, width), 1)
        col = jnp.where(col < split, col - shift[0], col - shift[1])
        one = jnp.where(lax.shift_right_arithmetic(col, 2) == to, 1.0, 0.0).astype(BF16)
        return jnp.concatenate([one, one], axis=1)

    def row_means(ref, first, nf, nh, scale):
        tall = []
        for f in range(nf):
            wide = []
            for h in range(nh):
                n = nh * (first + f) + h
                total = ref[n, pl.ds(0, CR, stride=4), :]
                for k in range(1, 4):
                    total = total + ref[n, pl.ds(k, CR, stride=4), :]
                wide.append(total * scale)
            tall.append(jnp.concatenate(wide, axis=1) if nh > 1 else wide[0])
        tall.append(jnp.zeros((TR - nf * CR, 128 * nh), F32))
        return jnp.concatenate(halves(jnp.concatenate(tall, axis=0)), axis=1)

    own = (0, 0)
    sides = (HALO, 128 - HALO - TC)
    pool_all = pool_matrix(TC, lambda j: j >= 0, own, TC)
    pool_mid = pool_matrix(TC, lambda j: (j >= 8) & (j < CC - 8), own, TC)
    pool_side = pool_matrix(EC, lambda j: (j < 8) | (j >= CC - 8), sides, EC // 2)
    edge_all = edge_matrix(TC, own, TC)
    edge_side = edge_matrix(EC, sides, EC // 2)

    for h in range(2):
        planes[6 + h] = ext[3, TOP:TOP + TR, 128 * h:128 * h + 128]
        planes[8 + h] = ext[4, TOP:TOP + TR, 128 * h:128 * h + 128]
    means = row_means(planes, 3, 2, 2, 1.0 / 16.0)
    edges = dot_nt(edge_all, means)
    ts_w[0] = edges[0:8]
    ts_w[1] = edges[8:16]
    coarse = dot(means, pool_all)
    for f in range(2):
        cw[f, 8:8 + CR] = coarse[f * CR:(f + 1) * CR]
    start_all(copy_w, CROSS)

    ext_row = a * TR - TOP + iota((ER, 8), 0)
    own_col = c * TC + iota((TC, 8), 0)
    side_col = iota((EC, 8), 0)
    side_col = c * TC + jnp.where(side_col < EC // 2, side_col - sides[0], side_col - sides[1])
    for step in range(STEPS):
        cells = cells_ref[step:step + 1, :]
        row_hit = jnp.where(ext_row == lax.div(cells, total_cols), press_ref[...], 0.0)
        for ref, col in ((forc, own_col), (e_forc, side_col)):
            col_hit = jnp.where(col == lax.rem(cells, total_cols), 1.0, 0.0)
            ref[step] = lax.dot_general(
                row_hit, col_hit, (((1,), (1,)), ((), ())),
                precision=lax.Precision.HIGHEST, preferred_element_type=F32)

    def own_waves():
        base, force, first, last, bend = ext, forc, r1, s_out, curv
        u_ref, v_ref, stress_ref, nh = u_out, v_out, planes, 2
        surface, along, cross = base.at[0], base.at[1], base.at[2]
        for step in range(STEPS):
            raised = first if step == 0 else last
            for r, n in ALL:
                keep = slice(8, 8 + n)
                wide = slice(r - 8, r + n + 8)
                here = slice(r, r + n)
                depth = base[3, wide, :]
                du = depth * along[wide, :]
                dv = depth[keep] * cross[here, :]
                flux = (row_next(du, keep) - row_prev(du, keep)) + (col_next(dv) - col_prev(dv))
                raised[here, :] = base[4, here, :] * (
                    surface[here, :] - (0.5 * CONTINUITY) * flux + force[step, here, :])
            for r, n in ALL:
                keep = slice(8, 8 + n)
                x = raised[r - 8:r + n + 8, :]
                mid = x[keep]
                down, up, right, left = row_next(x, keep), row_prev(x, keep), col_next(mid), col_prev(mid)
                slope[0, r:r + n, :] = down - up
                slope[1, r:r + n, :] = right - left
                bend[r:r + n, :] = down + up + right + left - 4.0 * mid
            for r, n in (ALL if step < STEPS - 1 else OWN):
                keep = slice(8, 8 + n)
                here = slice(r, r + n)
                x = raised[here, :]
                k = bend[r - 8:r + n + 8, :]
                depth = base[3, here, :]
                wet = base[4, here, :]
                disp = depth * depth * (1.0 / 3.0)
                push_a = slope[0, here, :] + disp * (row_next(k, keep) - row_prev(k, keep))
                k = k[keep]
                push_c = slope[1, here, :] + disp * (col_next(k) - col_prev(k))
                u = wet * (along[here, :] - (0.5 * MOMENTUM) * push_a)
                v = wet * (cross[here, :] - (0.5 * MOMENTUM) * push_c)
                u_ref[here, :] = u
                v_ref[here, :] = v
                if (r, n) in OWN:
                    pot = POTENTIAL * x * x
                    stress = (depth * u * u + pot, depth * u * v, depth * v * v + pot)
                    at = slice(r - TOP, r - TOP + n)
                    for f in range(3):
                        for h in range(nh):
                            part = stress[f][:, 128 * h:128 * h + 128]
                            if step > 0:
                                part = part + stress_ref[nh * f + h, at]
                            stress_ref[nh * f + h, at] = part
            surface, along, cross = raised, u_ref, v_ref

    def edge_waves():
        surface, along, cross = e_ext.at[0], e_ext.at[1], e_ext.at[2]
        for step in range(STEPS):
            raised = e_r1 if step == 0 else e_s
            e_du[...] = e_ext[3] * along[...]
            for r, n in E_BOTH:
                here, down, up = slice(r, r + n), slice(r + 1, r + n + 1), slice(r - 1, r + n - 1)
                dv = e_ext[3, here, :] * cross[here, :]
                flux = (e_du[down, :] - e_du[up, :]) + (col_next(dv) - col_prev(dv))
                raised[here, :] = e_ext[4, here, :] * (
                    surface[here, :] - (0.5 * CONTINUITY) * flux + e_forc[step, here, :])
            for r, n in E_BOTH:
                here, down, up = slice(r, r + n), slice(r + 1, r + n + 1), slice(r - 1, r + n - 1)
                mid = raised[here, :]
                right, left = col_next(mid), col_prev(mid)
                e_slope[here, :] = right - left
                e_curv[here, :] = raised[down, :] + raised[up, :] + right + left - 4.0 * mid
            for r, n in (E_ALL if step < STEPS - 1 else E_OWN):
                here, down, up = slice(r, r + n), slice(r + 1, r + n + 1), slice(r - 1, r + n - 1)
                depth = e_ext[3, here, :]
                wet = e_ext[4, here, :]
                disp = depth * depth * (1.0 / 3.0)
                k = e_curv[here, :]
                push_a = (raised[down, :] - raised[up, :]) + disp * (e_curv[down, :] - e_curv[up, :])
                push_c = e_slope[here, :] + disp * (col_next(k) - col_prev(k))
                u = wet * (along[here, :] - (0.5 * MOMENTUM) * push_a)
                v = wet * (cross[here, :] - (0.5 * MOMENTUM) * push_c)
                e_u[here, :] = u
                e_v[here, :] = v
                if (r, n) in E_OWN:
                    x = raised[here, :]
                    pot = POTENTIAL * x * x
                    at = slice(r - TOP, r - TOP + n)
                    for f, part in enumerate((depth * u * u + pot, depth * u * v, depth * v * v + pot)):
                        e_planes[f, at] = part + e_planes[f, at] if step > 0 else part
            surface, along, cross = raised, e_u, e_v

    def corner_matrix(side):
        lane_of = iota((EC, 128), 0)
        to = (iota((EC, 128), 1) & 7) * 4 + (HALO if side else 128 - HALO - 32)
        one = jnp.where((lane_of >= to) & (lane_of < to + 4), 1.0, 0.0).astype(BF16)
        return jnp.concatenate([one, one], axis=0)

    pool_corner = jnp.concatenate([corner_matrix(0), corner_matrix(1)], axis=1)

    def open_matrix(at):
        lane_of = iota((128, 128), 0)
        to = iota((128, 128), 1)
        one = jnp.where((to >= at) & (to < at + 8) & ((lane_of & 7) == to - at), 1.0, 0.0).astype(BF16)
        return jnp.concatenate([one, one], axis=0)

    open_corners = jnp.concatenate([open_matrix(120), open_matrix(CC)], axis=0)

    def fill_edge(r, n):
        at = iota((n, 128), 1)
        for f in range(5):
            left = pltpu.roll(ext[f, r:r + n, 0:128], HALO, 1)
            right = pltpu.roll(ext[f, r:r + n, 128:256], 128 - HALO, 1)
            both = jnp.where(at < EC // 2, left, right)
            rest = 0.0
            if f == 3:
                rest = jnp.where((at < HALO - SENT[f]) | (at >= 128 - HALO + SENT[f]), 1.0, 0.0)
            e_ext[f, r:r + n, :] = jnp.where((at >= HALO) & (at < 128 - HALO), both, rest)

    fill_edge(TOP, TR)

    n_lane = iota((192, 5 * 128), 0)
    to = iota((192, 5 * 128), 1)
    to_field, to_lane = lax.shift_right_logical(to, 7), to & 127
    hit = jnp.zeros((192, 5 * 128), jnp.bool_)
    for f in range(5):
        left = (to_lane >= HALO - SENT[f]) & (to_lane < HALO) & ((n_lane & 63) == to_lane - (HALO - SENT[f]) + FIRST[f])
        right = (to_lane >= 128 - HALO) & (to_lane < 128 - HALO + SENT[f]) & (
            (n_lane & 63) == to_lane - (128 - HALO) + 32 + FIRST[f])
        hit = hit | ((to_field == f) & (left | right))
    place = jnp.where(hit, 1.0, 0.0).astype(BF16)

    wait_recv_all(fine_copy, ALONG)
    own_waves()
    coarse_mid = dot(row_means(planes, 0, 3, 2, 1.0 / (16.0 * STEPS)), pool_mid)

    fill_edge(TOP - 8, 8)
    fill_edge(TOP + TR, 8)
    def open_corner(t):
        rows = jnp.zeros((8, 128), F32)
        for side in range(2):
            block = jnp.concatenate([
                jnp.broadcast_to(corner[t, side, 0:1], (4, 128)),
                jnp.broadcast_to(corner[t, side, 1:2], (4, 128))], axis=0)
            block = slant(block, 96)
            rows = jnp.where(lax.shift_right_logical(lane[0:8], 5) == side, block, rows)
        return rows

    wait_recv_all(fine_copy, CROSS)
    arrived = got[0:64]
    high = arrived.astype(BF16)
    rest = arrived - high.astype(F32)
    middle = rest.astype(BF16)
    low = (rest - middle.astype(F32)).astype(BF16)
    moved = lax.dot_general(
        jnp.concatenate([high, middle, low], axis=0), place,
        (((0,), (0,)), ((), ())), preferred_element_type=F32)
    rows = slice(TOP, TOP + TR)
    for f in range(5):
        e_ext[f, rows, :] = e_ext[f, rows, :] + moved[:, 128 * f:128 * f + 128]
    wait_recv_all(fine_copy, DIRS[2:6])
    few = iota((8, 128), 1)
    for t in range(2):
        halo = open_corner(t)
        at = TOP - 8 if t == 0 else TOP + TR
        for f in range(5):
            left = pltpu.roll(halo, (HALO - SENT[f] - FIRST[f]) % 128, 1)
            right = pltpu.roll(halo, 128 - HALO - 32 - FIRST[f], 1)
            e_ext[f, at:at + 8, :] = jnp.where(
                (few >= HALO - SENT[f]) & (few < HALO), left,
                jnp.where((few >= 128 - HALO) & (few < 128 - HALO + SENT[f]), right, e_ext[f, at:at + 8, :]))
    edge_waves()

    means = row_means(e_planes, 0, 3, 1, 1.0 / (16.0 * STEPS))
    edges = dot_nt(edge_side, means)
    ts_s[0] = edges[0:8]
    ts_s[1] = edges[8:16]
    start_all(copy_s, CROSS)
    coarse = dot(means, pool_corner)
    small = iota((8, 128), 1)
    group = lax.shift_right_logical(small, 3)
    row = iota((8, 128), 0)
    for t in range(2):
        for side in range(2):
            packed = [jnp.zeros((8, 128), F32)] * 2
            for f in range(3):
                r = f * CR + (0 if t == 0 else CR - 8)
                block = coarse[r:r + 8, 128 * side:128 * side + 128]
                packed[f // 2] = packed[f // 2] + jnp.where(group == row + 8 * (f % 2), block, 0.0)
            for k in range(2):
                corner_s_send[t, side, k:k + 1] = jnp.sum(packed[k], axis=0, keepdims=True)
    start_all(copy_s, DIRS[2:6])
    coarse = dot(means, pool_side) + coarse_mid
    for f in range(3):
        cs[f, 8:8 + CR] = coarse[f * CR:(f + 1) * CR]
    start_all(copy_s, ALONG)

    rows = slice(TOP, TOP + TR)
    for ref, edge in ((s_out, e_s), (u_out, e_u), (v_out, e_v)):
        ref[rows, 0:128] = jnp.where(lane < 16, pltpu.roll(edge[rows], 128 - HALO, 1), ref[rows, 0:128])
        ref[rows, 128:256] = jnp.where(lane >= 112, pltpu.roll(edge[rows], HALO, 1), ref[rows, 128:256])

    weights = spread(TC, 128, 1, (128, TC), 0, True)
    cols_out[...] = jnp.concatenate([weights, weights], axis=0)
    weights = spread(TR, WR, 0, (TR, WR), 8, False)
    rows_out[...] = jnp.concatenate([weights, weights], axis=1)

    wait_recv_all(copy_w, CROSS)
    mid = side_w[...].T
    for f in range(2):
        cw[f, 8:8 + CR] = cw[f, 8:8 + CR] + mid[f * CR:(f + 1) * CR]
    start_all(copy_w, ALONG)
    wait_recv_all(copy_w, ALONG)
    depth, wet = cw[0], cw[1]
    inside = depth > 0.25
    inv_depth = 1.0 / jnp.maximum(depth, 0.25)

    wait_send_all(fine_copy)
    wait_send_all(copy_w, CROSS)

    wait_recv_all(copy_s, CROSS + ALONG)
    mid = side_s[...].T
    wait_recv_all(copy_s, DIRS[2:6])
    blocks = []
    for t in range(2):
        for f in range(3):
            parts = []
            for side in range(2):
                block = jnp.broadcast_to(corner_s[t, side, f // 2:f // 2 + 1], (8, 128))
                parts += list(halves(jnp.where(group == row + 8 * (f % 2), block, 0.0)))
            blocks.append(jnp.concatenate([x.astype(F32) for x in parts], axis=1))
    ends = dot(jnp.concatenate(blocks, axis=0).astype(BF16), open_corners)
    wide = []
    for f in range(3):
        wide.append(jnp.concatenate([
            cs[f, 0:8] + ends[8 * f:8 * f + 8],
            cs[f, 8:8 + CR] + mid[f * CR:(f + 1) * CR],
            cs[f, WR - 8:WR] + ends[24 + 8 * f:32 + 8 * f]], axis=0))
    s0, s1, s2 = wide

    def dr(x):
        return 0.5 * (pltpu.roll(x, WR - 1, 0) - pltpu.roll(x, 1, 0))

    def dc(x):
        return 0.5 * (col_next(x) - col_prev(x))

    def laplace(x):
        return pltpu.roll(x, WR - 1, 0) + pltpu.roll(x, 1, 0) + col_next(x) + col_prev(x) - 4.0 * x

    force_a = -(dr(s0) + dc(s1)) * inv_depth
    force_c = -(dr(s1) + dc(s2)) * inv_depth
    flow_a = wet * (CIRC_FORCE * force_a)
    flow_c = wet * (CIRC_FORCE * force_c)
    elevation = jnp.zeros_like(depth)
    for _ in range(CIRC - 1):
        level = elevation - CIRC_LEVEL * (dr(depth * flow_a) + dc(depth * flow_c))
        elevation = jnp.where(inside, level, 0.0)
        flow_a, flow_c = (
            wet * (flow_a + CIRC_FORCE * (force_a - dr(elevation))
                   - FRICTION * flow_a * inv_depth + VISCOSITY * laplace(flow_a)),
            wet * (flow_c + CIRC_FORCE * (force_c - dc(elevation))
                   - FRICTION * flow_c * inv_depth + VISCOSITY * laplace(flow_c)),
        )

    flow_out[0] = flow_a
    flow_out[1] = flow_c
    wait_send_all(copy_w, ALONG)
    wait_send_all(copy_s)


def finish(s_ref, u_ref, v_ref, flow_ref, mask_ref, cols_ref, rows_ref, s_out, u_out, v_out, ca_out, cc_out, cur, store_sem):
    stores = [
        pltpu.make_async_copy(ref.at[TOP:TOP + TR, 0:TC], out, store_sem.at[k])
        for k, (ref, out) in enumerate(((s_ref, s_out), (u_ref, u_out), (v_ref, v_out)))
    ]
    for cp in stores:
        cp.start()
    high, low = halves(flow_ref[...].reshape(2 * WR, 128))
    wide = dot(jnp.concatenate([high, low], axis=1), cols_ref[...])
    high, low = halves(jnp.concatenate([wide[0:WR], wide[WR:2 * WR]], axis=1))
    fine = dot(rows_ref[...], jnp.concatenate([high, low], axis=0))
    mask = mask_ref[...]
    for k, out in enumerate((ca_out, cc_out)):
        cur[k] = fine[:, k * TC:k * TC + TC] * mask
        stores.append(pltpu.make_async_copy(cur.at[k], out, store_sem.at[3 + k]))
        stores[-1].start()
    for cp in stores:
        cp.wait()


def solution(mesh):
    mesh_rows, mesh_cols = mesh.shape["along"], mesh.shape["cross"]
    hbm = pl.BlockSpec(memory_space=pltpu.HBM)
    vmem = pl.BlockSpec(memory_space=pltpu.VMEM)

    def shape(*dims):
        return jax.ShapeDtypeStruct(dims, F32)

    def per_device(surface, along_speed, cross_speed, water_depth, wet_mask, ship_cells, ship_pressure):
        ships = ship_pressure.shape[0]
        state = pl.pallas_call(
            functools.partial(kernel, mesh_rows, mesh_cols),
            out_shape=[shape(ER, TC)] * 3 + [shape(2, WR, 128), shape(TR, TC)] + [
                jax.ShapeDtypeStruct((256, TC), BF16), jax.ShapeDtypeStruct((TR, 2 * WR), BF16)],
            in_specs=[hbm] * 7,
            out_specs=[vmem] * 7,
            scratch_shapes=[
                pltpu.VMEM((5, ER, TC), F32),
                pltpu.VMEM((TR, TC), jnp.int32),
                pltpu.VMEM((STEPS, ships), jnp.int32),
                pltpu.VMEM((1, ships), F32),
                pltpu.VMEM((STEPS, ER, TC), F32),
                pltpu.VMEM((ER, TC), F32),
                pltpu.VMEM((ER, TC), F32),
                pltpu.VMEM((2, ER, TC), F32),
                pltpu.VMEM((10, TR, 128), F32),
                pltpu.VMEM((5, ER, EC), F32),
                pltpu.VMEM((STEPS, ER, EC), F32),
            ] + [pltpu.VMEM((ER, EC), F32)] * 7 + [
                pltpu.VMEM((3, TR, 128), F32),
                pltpu.VMEM((128, 128), F32),
                pltpu.VMEM((128, 128), F32),
            ] + [pltpu.VMEM((2, 2, 2, 128), F32)] * 4 + [
                pltpu.VMEM((2, 8, 128), F32),
                pltpu.VMEM((2, 8, 128), F32),
                pltpu.VMEM((128, 128), F32),
                pltpu.VMEM((128, 128), F32),
                pltpu.VMEM((2, WR, 128), F32),
                pltpu.VMEM((3, WR, 128), F32),
                pltpu.SemaphoreType.DMA((7,)),
            ] + [pltpu.SemaphoreType.DMA((8,))] * 6,
            compiler_params=pltpu.CompilerParams(
                collective_id=0, has_side_effects=True, vmem_limit_bytes=32 * 1024 * 1024),
        )(*(pltpu.with_memory_space_constraint(x, pltpu.HBM) for x in (
            surface, along_speed, cross_speed, water_depth, wet_mask, ship_cells,
            ship_pressure.reshape(1, ships))))
        return pl.pallas_call(
            finish,
            out_shape=[shape(TR, TC)] * 5,
            in_specs=[vmem] * 7,
            out_specs=[hbm] * 5,
            scratch_shapes=[pltpu.VMEM((2, TR, TC), F32), pltpu.SemaphoreType.DMA((5,))],
            compiler_params=pltpu.CompilerParams(vmem_limit_bytes=16 * 1024 * 1024),
        )(*state)

    tiled = P("along", "cross")
    return jax.shard_map(
        per_device,
        mesh=mesh,
        in_specs=(tiled,) * 5 + (P(), P()),
        out_specs=(tiled,) * 5,
        check_vma=False,
    )
```

```python
import functools

import jax
import jax.numpy as jnp
from jax import lax
from jax.experimental import pallas as pl
from jax.experimental.pallas import tpu as pltpu
from jax.sharding import PartitionSpec as P

STEPS = 2
CIRC = 3
CONTINUITY = 0.25
MOMENTUM = 0.3
POTENTIAL = 0.5
CIRC_LEVEL = 0.2
CIRC_FORCE = 0.3
FRICTION = 0.1
VISCOSITY = 0.1

MESH = pl.DeviceIdType.MESH
F32 = jnp.float32
BF16 = jnp.bfloat16

TR = 128
TC = 256
TOP = 16
ER = TR + 2 * TOP
EC = 128
SIDE = 58
CR = TR // 4
CC = TC // 4
WR = CR + 16
CHUNK = 32
OWN = [(r, CHUNK) for r in range(TOP, TOP + TR, CHUNK)]
ALL = [(TOP - 8, 8)] + OWN + [(TOP + TR, 8)]
CROSS = [(0, -1), (0, 1)]
ALONG = [(-1, 0), (1, 0)]
DIRS = CROSS + [(-1, -1), (-1, 1), (1, -1), (1, 1)] + ALONG
HALO = 6
SENT = (5, 5, 5, 3, 5)
FIRST = (0, 5, 10, 20, 15)
E_BOTH = [(TOP - 8, TR // 2 + 8), (TOP + TR // 2, TR // 2 + 8)]
E_OWN = [(TOP, TR // 2), (TOP + TR // 2, TR // 2)]
E_ALL = [(TOP - 8, 8)] + E_OWN + [(TOP + TR, 8)]


def iota(shape, dim):
    return lax.broadcasted_iota(jnp.int32, shape, dim)


def halves(x):
    high = x.astype(BF16)
    return high, (x - high.astype(F32)).astype(BF16)


def dot(x, y):
    return jnp.dot(x, y, preferred_element_type=F32)


def dot_nt(x, y):
    return lax.dot_general(x, y, (((1,), (1,)), ((), ())), preferred_element_type=F32)


def row_next(x, keep):
    return pltpu.roll(x, x.shape[0] - 1, 0)[keep]


def row_prev(x, keep):
    return pltpu.roll(x, 1, 0)[keep]


def col_next(x):
    return pltpu.roll(x, x.shape[1] - 1, 1)


def col_prev(x):
    return pltpu.roll(x, 1, 1)


def spread(fine, coarse, fine_dim, shape, first, wrap):
    f = iota(shape, fine_dim)
    c = iota(shape, 1 - fine_dim)
    base = lax.shift_right_logical(f, 2) + first
    k = f & 3
    weight = jnp.where((k == 0) | (k == 3), 0.375, 0.125)
    other = base + jnp.where(k < 2, -1, 1)
    if wrap:
        other = other & (coarse - 1)
    zero = jnp.zeros(shape, F32)
    return (jnp.where(c == base, 1.0 - weight, zero) + jnp.where(c == other, weight, zero)).astype(BF16)


def kernel(
    mesh_rows, mesh_cols,
    s_in, u_in, v_in, d_in, w_in, cells_in, press_in,
    s_out, u_out, v_out, flow_out, mask_out, cols_out, rows_out,
    ext, wraw, cells_ref, press_ref, forc, r1, curv, slope, planes,
    e_ext, e_forc, e_r1, e_s, e_u, e_v, e_curv, e_du, e_slope, e_planes,
    packt, got, corner_send, corner, corner_s_send, corner_s,
    ts_w, ts_s, side_w, side_s, cw, cs,
    load_sem, f_send, f_recv, w_send, w_recv, c_send, c_recv,
):
    a = lax.axis_index("along")
    c = lax.axis_index("cross")
    total_cols = TC * mesh_cols

    def there(da, dc):
        ok = None
        for cond in ([a > 0] if da < 0 else [a < mesh_rows - 1] if da > 0 else []) + (
            [c > 0] if dc < 0 else [c < mesh_cols - 1] if dc > 0 else []
        ):
            ok = cond if ok is None else ok & cond
        return ok

    def device(da, dc):
        return (a + da, c + dc)

    barrier = pltpu.get_barrier_semaphore()
    for da, dc in DIRS[2:6] + CROSS + ALONG:
        @pl.when(there(da, dc))
        def _(da=da, dc=dc):
            pl.semaphore_signal(barrier, inc=1, device_id=device(da, dc), device_id_type=MESH)

    loads = []
    for k, src in enumerate((s_in, u_in, v_in, d_in)):
        loads.append(pltpu.make_async_copy(src, ext.at[k, TOP:TOP + TR, 0:TC], load_sem.at[k]))
    loads.append(pltpu.make_async_copy(w_in, wraw, load_sem.at[4]))
    loads.append(pltpu.make_async_copy(cells_in, cells_ref, load_sem.at[5]))
    loads.append(pltpu.make_async_copy(press_in, press_ref, load_sem.at[6]))
    for cp in loads:
        cp.start()

    for ref in (ext, e_ext):
        for f in range(5):
            ref[f, 0:8, :] = jnp.zeros((8, ref.shape[2]), F32)
            ref[f, ER - 8:ER, :] = jnp.zeros((8, ref.shape[2]), F32)
    for ref in (r1, s_out, u_out, v_out, curv, e_r1, e_s, e_u, e_v, e_curv):
        ref[0:8, :] = jnp.zeros((8, ref.shape[1]), F32)
        ref[ER - 8:ER, :] = jnp.zeros((8, ref.shape[1]), F32)
    for k in range(2):
        got[32 * k + 24:32 * k + 32] = jnp.zeros((8, 128), F32)
    for side in (side_w, side_s):
        side[0:CC] = jnp.zeros((CC, 128), F32)
        side[CC + 8:120] = jnp.zeros((112 - CC, 128), F32)
    for da, dc in DIRS:
        @pl.when(jnp.logical_not(there(da, dc)))
        def _(da=da, dc=dc):
            if dc == 0:
                at = TOP - 8 if da < 0 else TOP + TR
                for f in range(5):
                    ext[f, at:at + 8, 0:TC] = jnp.zeros((8, TC), F32)
                at = 0 if da < 0 else WR - 8
                for ref, nf in ((cw, 2), (cs, 3)):
                    for f in range(nf):
                        ref[f, at:at + 8] = jnp.zeros((8, 128), F32)
                return
            right = 1 if dc > 0 else 0
            if da == 0:
                got[32 * right:32 * right + 24] = jnp.zeros((24, 128), F32)
                at = CC if right else 120
                side_w[at:at + 8] = jnp.zeros((8, 128), F32)
                side_s[at:at + 8] = jnp.zeros((8, 128), F32)
            else:
                corner[0 if da < 0 else 1, right] = jnp.zeros((8, 128), F32)
                corner_s[0 if da < 0 else 1, right] = jnp.zeros((8, 128), F32)

    rows_near = 1 + jnp.where(a > 0, 1, 0) + jnp.where(a < mesh_rows - 1, 1, 0)
    cols_near = 1 + jnp.where(c > 0, 1, 0) + jnp.where(c < mesh_cols - 1, 1, 0)
    for cp in loads:
        cp.wait()
    own_wet = wraw[...].astype(F32)
    ext[4, TOP:TOP + TR, 0:TC] = own_wet
    mask_out[...] = own_wet

    lane = iota((TR, 128), 1)
    packed = jnp.zeros((TR, 128), F32)
    for part in range(2):
        surface, along, cross, depth, wet = (
            ext[f, TOP:TOP + TR, 128 * part:128 * part + 128] for f in range(5))
        far = 128 - lane if part else lane + 1
        product = (far == 4) | (far == 5)
        flow = depth * cross
        beyond = -col_prev(flow) if part else col_next(flow)
        edges = (
            jnp.where(far == 5, surface - (0.5 * CONTINUITY) * beyond, surface),
            jnp.where(product, depth * along, along),
            jnp.where(product, flow, cross),
            depth, wet)
        for f in range(5):
            start = FIRST[f] + (0 if part else 32)
            move = start + (SENT[f] if part else 0)
            packed = jnp.where(
                (lane >= start) & (lane < start + SENT[f]), pltpu.roll(edges[f], move, 1), packed)
    packt[...] = packed.T
    corner_send[0] = packed[0:8]
    corner_send[1] = packed[TR - 8:TR]

    def fine_copy(n):
        da, dc = DIRS[n]
        if da == 0:
            at = 0 if dc > 0 else 32
            src, dst = packt.at[at:at + 24], got.at[at:at + 24]
        elif dc == 0:
            src = ext.at[:, TOP:TOP + 8, 0:TC] if da < 0 else ext.at[:, TOP + TR - 8:TOP + TR, 0:TC]
            dst = ext.at[:, TOP + TR:TOP + TR + 8, 0:TC] if da < 0 else ext.at[:, TOP - 8:TOP, 0:TC]
        else:
            side = 0 if dc > 0 else 1
            src = corner_send.at[0 if da < 0 else 1]
            dst = corner.at[1 if da < 0 else 0, side]
        return pltpu.make_async_remote_copy(
            src_ref=src, dst_ref=dst, send_sem=f_send.at[n], recv_sem=f_recv.at[n],
            device_id=device(da, dc), device_id_type=MESH)

    def coarse_copy(ts, side, field, send, recv):
        def make(n):
            da, dc = DIRS[n]
            if dc == 0:
                src = field.at[:, 8:16] if da < 0 else field.at[:, CR:CR + 8]
                dst = field.at[:, CR + 8:CR + 16] if da < 0 else field.at[:, 0:8]
            elif da == 0:
                at = CC if dc < 0 else 120
                src = ts.at[0 if dc < 0 else 1]
                dst = side.at[at:at + 8]
            else:
                src = corner_s_send.at[0 if da < 0 else 1, 0 if dc > 0 else 1]
                dst = corner_s.at[1 if da < 0 else 0, 0 if dc > 0 else 1]
            return pltpu.make_async_remote_copy(
                src_ref=src, dst_ref=dst, send_sem=send.at[n], recv_sem=recv.at[n],
                device_id=device(da, dc), device_id_type=MESH)
        return make

    def start_all(make, chosen=DIRS):
        for da, dc in chosen:
            n = DIRS.index((da, dc))
            @pl.when(there(da, dc))
            def _(n=n):
                make(n).start()

    def wait_recv_all(make, chosen=DIRS):
        for da, dc in chosen:
            n = DIRS.index((da, dc))
            @pl.when(there(-da, -dc))
            def _(n=n):
                make(n).wait_recv()

    def wait_send_all(make, chosen=DIRS):
        for da, dc in chosen:
            n = DIRS.index((da, dc))
            @pl.when(there(da, dc))
            def _(n=n):
                make(n).wait_send()

    pl.semaphore_wait(barrier, rows_near * cols_near - 1)
    copy_w = coarse_copy(ts_w, side_w, cw, w_send, w_recv)
    copy_s = coarse_copy(ts_s, side_s, cs, c_send, c_recv)
    start_all(fine_copy, DIRS[2:6] + CROSS + ALONG)

    def pool_matrix(width, wanted, shift, split):
        col = iota((width, 128), 0)
        col = jnp.where(col < split, col - shift[0], col - shift[1])
        to = iota((width, 128), 1)
        hit = (lax.shift_right_arithmetic(col, 2) == to) & wanted(to) & (to < CC)
        one = jnp.where(hit, 1.0, 0.0).astype(BF16)
        return jnp.concatenate([one, one], axis=0)

    def edge_matrix(width, shift, split):
        to = iota((16, width), 0)
        to = jnp.where(to < 8, to, to + (CC - 16))
        col = iota((16, width), 1)
        col = jnp.where(col < split, col - shift[0], col - shift[1])
        one = jnp.where(lax.shift_right_arithmetic(col, 2) == to, 1.0, 0.0).astype(BF16)
        return jnp.concatenate([one, one], axis=1)

    def row_means(ref, first, nf, nh, scale):
        tall = []
        for f in range(nf):
            wide = []
            for h in range(nh):
                n = nh * (first + f) + h
                total = ref[n, pl.ds(0, CR, stride=4), :]
                for k in range(1, 4):
                    total = total + ref[n, pl.ds(k, CR, stride=4), :]
                wide.append(total * scale)
            tall.append(jnp.concatenate(wide, axis=1) if nh > 1 else wide[0])
        tall.append(jnp.zeros((TR - nf * CR, 128 * nh), F32))
        return jnp.concatenate(halves(jnp.concatenate(tall, axis=0)), axis=1)

    own = (0, 0)
    sides = (HALO, 128 - HALO - TC)
    pool_all = pool_matrix(TC, lambda j: j >= 0, own, TC)
    pool_mid = pool_matrix(TC, lambda j: (j >= 8) & (j < CC - 8), own, TC)
    pool_side = pool_matrix(EC, lambda j: (j < 8) | (j >= CC - 8), sides, EC // 2)
    edge_all = edge_matrix(TC, own, TC)
    edge_side = edge_matrix(EC, sides, EC // 2)

    for h in range(2):
        planes[6 + h] = ext[3, TOP:TOP + TR, 128 * h:128 * h + 128]
        planes[8 + h] = ext[4, TOP:TOP + TR, 128 * h:128 * h + 128]
    means = row_means(planes, 3, 2, 2, 1.0 / 16.0)
    edges = dot_nt(edge_all, means)
    ts_w[0] = edges[0:8]
    ts_w[1] = edges[8:16]
    coarse = dot(means, pool_all)
    for f in range(2):
        cw[f, 8:8 + CR] = coarse[f * CR:(f + 1) * CR]
    start_all(copy_w, CROSS)

    ext_row = a * TR - TOP + iota((ER, 8), 0)
    own_col = c * TC + iota((TC, 8), 0)
    side_col = iota((EC, 8), 0)
    side_col = c * TC + jnp.where(side_col < EC // 2, side_col - sides[0], side_col - sides[1])
    for step in range(STEPS):
        cells = cells_ref[step:step + 1, :]
        row_hit = jnp.where(ext_row == lax.div(cells, total_cols), press_ref[...], 0.0)
        for ref, col in ((forc, own_col), (e_forc, side_col)):
            col_hit = jnp.where(col == lax.rem(cells, total_cols), 1.0, 0.0)
            ref[step] = lax.dot_general(
                row_hit, col_hit, (((1,), (1,)), ((), ())),
                precision=lax.Precision.HIGHEST, preferred_element_type=F32)

    def own_waves():
        base, force, first, last, bend = ext, forc, r1, s_out, curv
        u_ref, v_ref, stress_ref, nh = u_out, v_out, planes, 2
        surface, along, cross = base.at[0], base.at[1], base.at[2]
        for step in range(STEPS):
            raised = first if step == 0 else last
            for r, n in ALL:
                keep = slice(8, 8 + n)
                wide = slice(r - 8, r + n + 8)
                here = slice(r, r + n)
                depth = base[3, wide, :]
                du = depth * along[wide, :]
                dv = depth[keep] * cross[here, :]
                flux = (row_next(du, keep) - row_prev(du, keep)) + (col_next(dv) - col_prev(dv))
                raised[here, :] = base[4, here, :] * (
                    surface[here, :] - (0.5 * CONTINUITY) * flux + force[step, here, :])
            for r, n in ALL:
                keep = slice(8, 8 + n)
                x = raised[r - 8:r + n + 8, :]
                mid = x[keep]
                down, up, right, left = row_next(x, keep), row_prev(x, keep), col_next(mid), col_prev(mid)
                slope[0, r:r + n, :] = down - up
                slope[1, r:r + n, :] = right - left
                bend[r:r + n, :] = down + up + right + left - 4.0 * mid
            for r, n in (ALL if step < STEPS - 1 else OWN):
                keep = slice(8, 8 + n)
                here = slice(r, r + n)
                x = raised[here, :]
                k = bend[r - 8:r + n + 8, :]
                depth = base[3, here, :]
                wet = base[4, here, :]
                disp = depth * depth * (1.0 / 3.0)
                push_a = slope[0, here, :] + disp * (row_next(k, keep) - row_prev(k, keep))
                k = k[keep]
                push_c = slope[1, here, :] + disp * (col_next(k) - col_prev(k))
                u = wet * (along[here, :] - (0.5 * MOMENTUM) * push_a)
                v = wet * (cross[here, :] - (0.5 * MOMENTUM) * push_c)
                u_ref[here, :] = u
                v_ref[here, :] = v
                if (r, n) in OWN:
                    pot = POTENTIAL * x * x
                    stress = (depth * u * u + pot, depth * u * v, depth * v * v + pot)
                    at = slice(r - TOP, r - TOP + n)
                    for f in range(3):
                        for h in range(nh):
                            part = stress[f][:, 128 * h:128 * h + 128]
                            if step > 0:
                                part = part + stress_ref[nh * f + h, at]
                            stress_ref[nh * f + h, at] = part
            surface, along, cross = raised, u_ref, v_ref

    def edge_waves():
        surface, along, cross = e_ext.at[0], e_ext.at[1], e_ext.at[2]
        for step in range(STEPS):
            raised = e_r1 if step == 0 else e_s
            e_du[...] = e_ext[3] * along[...]
            for r, n in E_BOTH:
                here, down, up = slice(r, r + n), slice(r + 1, r + n + 1), slice(r - 1, r + n - 1)
                dv = e_ext[3, here, :] * cross[here, :]
                flux = (e_du[down, :] - e_du[up, :]) + (col_next(dv) - col_prev(dv))
                raised[here, :] = e_ext[4, here, :] * (
                    surface[here, :] - (0.5 * CONTINUITY) * flux + e_forc[step, here, :])
            for r, n in E_BOTH:
                here, down, up = slice(r, r + n), slice(r + 1, r + n + 1), slice(r - 1, r + n - 1)
                mid = raised[here, :]
                right, left = col_next(mid), col_prev(mid)
                e_slope[here, :] = right - left
                e_curv[here, :] = raised[down, :] + raised[up, :] + right + left - 4.0 * mid
            for r, n in (E_ALL if step < STEPS - 1 else E_OWN):
                here, down, up = slice(r, r + n), slice(r + 1, r + n + 1), slice(r - 1, r + n - 1)
                depth = e_ext[3, here, :]
                wet = e_ext[4, here, :]
                disp = depth * depth * (1.0 / 3.0)
                k = e_curv[here, :]
                push_a = (raised[down, :] - raised[up, :]) + disp * (e_curv[down, :] - e_curv[up, :])
                push_c = e_slope[here, :] + disp * (col_next(k) - col_prev(k))
                u = wet * (along[here, :] - (0.5 * MOMENTUM) * push_a)
                v = wet * (cross[here, :] - (0.5 * MOMENTUM) * push_c)
                e_u[here, :] = u
                e_v[here, :] = v
                if (r, n) in E_OWN:
                    x = raised[here, :]
                    pot = POTENTIAL * x * x
                    at = slice(r - TOP, r - TOP + n)
                    for f, part in enumerate((depth * u * u + pot, depth * u * v, depth * v * v + pot)):
                        e_planes[f, at] = part + e_planes[f, at] if step > 0 else part
            surface, along, cross = raised, e_u, e_v

    def corner_matrix(side):
        lane_of = iota((EC, 128), 0)
        to = (iota((EC, 128), 1) & 7) * 4 + (HALO if side else 128 - HALO - 32)
        one = jnp.where((lane_of >= to) & (lane_of < to + 4), 1.0, 0.0).astype(BF16)
        return jnp.concatenate([one, one], axis=0)

    pool_corner = jnp.concatenate([corner_matrix(0), corner_matrix(1)], axis=1)

    def fill_edge(r, n):
        at = iota((n, 128), 1)
        for f in range(5):
            left = pltpu.roll(ext[f, r:r + n, 0:128], HALO, 1)
            right = pltpu.roll(ext[f, r:r + n, 128:256], 128 - HALO, 1)
            both = jnp.where(at < EC // 2, left, right)
            rest = 0.0
            if f == 3:
                rest = jnp.where((at < HALO - SENT[f]) | (at >= 128 - HALO + SENT[f]), 1.0, 0.0)
            e_ext[f, r:r + n, :] = jnp.where((at >= HALO) & (at < 128 - HALO), both, rest)

    fill_edge(TOP, TR)

    n_lane = iota((192, 5 * 128), 0)
    to = iota((192, 5 * 128), 1)
    to_field, to_lane = lax.shift_right_logical(to, 7), to & 127
    hit = jnp.zeros((192, 5 * 128), jnp.bool_)
    for f in range(5):
        left = (to_lane >= HALO - SENT[f]) & (to_lane < HALO) & ((n_lane & 63) == to_lane - (HALO - SENT[f]) + FIRST[f])
        right = (to_lane >= 128 - HALO) & (to_lane < 128 - HALO + SENT[f]) & (
            (n_lane & 63) == to_lane - (128 - HALO) + 32 + FIRST[f])
        hit = hit | ((to_field == f) & (left | right))
    place = jnp.where(hit, 1.0, 0.0).astype(BF16)

    wait_recv_all(fine_copy, ALONG)
    own_waves()
    coarse_mid = dot(row_means(planes, 0, 3, 2, 1.0 / (16.0 * STEPS)), pool_mid)

    fill_edge(TOP - 8, 8)
    fill_edge(TOP + TR, 8)
    wait_recv_all(fine_copy, CROSS)
    arrived = got[0:64]
    high = arrived.astype(BF16)
    rest = arrived - high.astype(F32)
    middle = rest.astype(BF16)
    low = (rest - middle.astype(F32)).astype(BF16)
    moved = lax.dot_general(
        jnp.concatenate([high, middle, low], axis=0), place,
        (((0,), (0,)), ((), ())), preferred_element_type=F32)
    rows = slice(TOP, TOP + TR)
    for f in range(5):
        e_ext[f, rows, :] = e_ext[f, rows, :] + moved[:, 128 * f:128 * f + 128]
    wait_recv_all(fine_copy, DIRS[2:6])
    few = iota((8, 128), 1)
    for t in range(2):
        halo = jnp.where(few < 32, corner[t, 0], corner[t, 1])
        at = TOP - 8 if t == 0 else TOP + TR
        for f in range(5):
            left = pltpu.roll(halo, (HALO - SENT[f] - FIRST[f]) % 128, 1)
            right = pltpu.roll(halo, 128 - HALO - 32 - FIRST[f], 1)
            e_ext[f, at:at + 8, :] = jnp.where(
                (few >= HALO - SENT[f]) & (few < HALO), left,
                jnp.where((few >= 128 - HALO) & (few < 128 - HALO + SENT[f]), right, e_ext[f, at:at + 8, :]))
    edge_waves()

    means = row_means(e_planes, 0, 3, 1, 1.0 / (16.0 * STEPS))
    edges = dot_nt(edge_side, means)
    ts_s[0] = edges[0:8]
    ts_s[1] = edges[8:16]
    start_all(copy_s, CROSS)
    coarse = dot(means, pool_corner)
    small = iota((8, 128), 1)
    group = lax.shift_right_logical(small, 3)
    for t in range(2):
        for side in range(2):
            tile = jnp.zeros((8, 128), F32)
            for f in range(3):
                r = f * CR + (0 if t == 0 else CR - 8)
                tile = jnp.where(group == f, coarse[r:r + 8, 128 * side:128 * side + 128], tile)
            corner_s_send[t, side] = tile
    start_all(copy_s, DIRS[2:6])
    coarse = dot(means, pool_side) + coarse_mid
    for f in range(3):
        cs[f, 8:8 + CR] = coarse[f * CR:(f + 1) * CR]
    start_all(copy_s, ALONG)

    rows = slice(TOP, TOP + TR)
    for ref, edge in ((s_out, e_s), (u_out, e_u), (v_out, e_v)):
        ref[rows, 0:128] = jnp.where(lane < 16, pltpu.roll(edge[rows], 128 - HALO, 1), ref[rows, 0:128])
        ref[rows, 128:256] = jnp.where(lane >= 112, pltpu.roll(edge[rows], HALO, 1), ref[rows, 128:256])

    weights = spread(TC, 128, 1, (128, TC), 0, True)
    cols_out[...] = jnp.concatenate([weights, weights], axis=0)
    weights = spread(TR, WR, 0, (TR, WR), 8, False)
    rows_out[...] = jnp.concatenate([weights, weights], axis=1)

    wait_recv_all(copy_w, CROSS)
    mid = side_w[...].T
    for f in range(2):
        cw[f, 8:8 + CR] = cw[f, 8:8 + CR] + mid[f * CR:(f + 1) * CR]
    start_all(copy_w, ALONG)
    wait_recv_all(copy_w, ALONG)
    depth, wet = cw[0], cw[1]
    inside = depth > 0.25
    inv_depth = 1.0 / jnp.maximum(depth, 0.25)

    wait_send_all(fine_copy)
    wait_send_all(copy_w, CROSS)

    wait_recv_all(copy_s, CROSS + ALONG)
    mid = side_s[...].T
    wait_recv_all(copy_s, DIRS[2:6])
    ends = []
    for t in range(2):
        for f in range(3):
            block = jnp.zeros((8, 128), F32)
            for side in range(2):
                at = CC if side else 120
                moved = pltpu.roll(corner_s[t, side], at - 8 * f, 1)
                block = jnp.where((small >= at) & (small < at + 8), moved, block)
            ends.append(block)
    wide = []
    for f in range(3):
        wide.append(jnp.concatenate([
            cs[f, 0:8] + ends[f],
            cs[f, 8:8 + CR] + mid[f * CR:(f + 1) * CR],
            cs[f, WR - 8:WR] + ends[3 + f]], axis=0))
    s0, s1, s2 = wide

    def dr(x):
        return 0.5 * (pltpu.roll(x, WR - 1, 0) - pltpu.roll(x, 1, 0))

    def dc(x):
        return 0.5 * (col_next(x) - col_prev(x))

    def laplace(x):
        return pltpu.roll(x, WR - 1, 0) + pltpu.roll(x, 1, 0) + col_next(x) + col_prev(x) - 4.0 * x

    force_a = -(dr(s0) + dc(s1)) * inv_depth
    force_c = -(dr(s1) + dc(s2)) * inv_depth
    flow_a = wet * (CIRC_FORCE * force_a)
    flow_c = wet * (CIRC_FORCE * force_c)
    elevation = jnp.zeros_like(depth)
    for _ in range(CIRC - 1):
        level = elevation - CIRC_LEVEL * (dr(depth * flow_a) + dc(depth * flow_c))
        elevation = jnp.where(inside, level, 0.0)
        flow_a, flow_c = (
            wet * (flow_a + CIRC_FORCE * (force_a - dr(elevation))
                   - FRICTION * flow_a * inv_depth + VISCOSITY * laplace(flow_a)),
            wet * (flow_c + CIRC_FORCE * (force_c - dc(elevation))
                   - FRICTION * flow_c * inv_depth + VISCOSITY * laplace(flow_c)),
        )

    flow_out[0] = flow_a
    flow_out[1] = flow_c
    wait_send_all(copy_w, ALONG)
    wait_send_all(copy_s)


def finish(s_ref, u_ref, v_ref, flow_ref, mask_ref, cols_ref, rows_ref, s_out, u_out, v_out, ca_out, cc_out, cur, store_sem):
    stores = [
        pltpu.make_async_copy(ref.at[TOP:TOP + TR, 0:TC], out, store_sem.at[k])
        for k, (ref, out) in enumerate(((s_ref, s_out), (u_ref, u_out), (v_ref, v_out)))
    ]
    for cp in stores:
        cp.start()
    high, low = halves(flow_ref[...].reshape(2 * WR, 128))
    wide = dot(jnp.concatenate([high, low], axis=1), cols_ref[...])
    high, low = halves(jnp.concatenate([wide[0:WR], wide[WR:2 * WR]], axis=1))
    fine = dot(rows_ref[...], jnp.concatenate([high, low], axis=0))
    mask = mask_ref[...]
    for k, out in enumerate((ca_out, cc_out)):
        cur[k] = fine[:, k * TC:k * TC + TC] * mask
        stores.append(pltpu.make_async_copy(cur.at[k], out, store_sem.at[3 + k]))
        stores[-1].start()
    for cp in stores:
        cp.wait()


def solution(mesh):
    mesh_rows, mesh_cols = mesh.shape["along"], mesh.shape["cross"]
    hbm = pl.BlockSpec(memory_space=pltpu.HBM)
    vmem = pl.BlockSpec(memory_space=pltpu.VMEM)

    def shape(*dims):
        return jax.ShapeDtypeStruct(dims, F32)

    def per_device(surface, along_speed, cross_speed, water_depth, wet_mask, ship_cells, ship_pressure):
        ships = ship_pressure.shape[0]
        state = pl.pallas_call(
            functools.partial(kernel, mesh_rows, mesh_cols),
            out_shape=[shape(ER, TC)] * 3 + [shape(2, WR, 128), shape(TR, TC)] + [
                jax.ShapeDtypeStruct((256, TC), BF16), jax.ShapeDtypeStruct((TR, 2 * WR), BF16)],
            in_specs=[hbm] * 7,
            out_specs=[vmem] * 7,
            scratch_shapes=[
                pltpu.VMEM((5, ER, TC), F32),
                pltpu.VMEM((TR, TC), jnp.int32),
                pltpu.VMEM((STEPS, ships), jnp.int32),
                pltpu.VMEM((1, ships), F32),
                pltpu.VMEM((STEPS, ER, TC), F32),
                pltpu.VMEM((ER, TC), F32),
                pltpu.VMEM((ER, TC), F32),
                pltpu.VMEM((2, ER, TC), F32),
                pltpu.VMEM((10, TR, 128), F32),
                pltpu.VMEM((5, ER, EC), F32),
                pltpu.VMEM((STEPS, ER, EC), F32),
            ] + [pltpu.VMEM((ER, EC), F32)] * 7 + [
                pltpu.VMEM((3, TR, 128), F32),
                pltpu.VMEM((128, 128), F32),
                pltpu.VMEM((128, 128), F32),
            ] + [pltpu.VMEM((2, 8, 128), F32)] + [pltpu.VMEM((2, 2, 8, 128), F32)] * 3 + [
                pltpu.VMEM((2, 8, 128), F32),
                pltpu.VMEM((2, 8, 128), F32),
                pltpu.VMEM((128, 128), F32),
                pltpu.VMEM((128, 128), F32),
                pltpu.VMEM((2, WR, 128), F32),
                pltpu.VMEM((3, WR, 128), F32),
                pltpu.SemaphoreType.DMA((7,)),
            ] + [pltpu.SemaphoreType.DMA((8,))] * 6,
            compiler_params=pltpu.CompilerParams(
                collective_id=0, has_side_effects=True, vmem_limit_bytes=32 * 1024 * 1024),
        )(*(pltpu.with_memory_space_constraint(x, pltpu.HBM) for x in (
            surface, along_speed, cross_speed, water_depth, wet_mask, ship_cells,
            ship_pressure.reshape(1, ships))))
        return pl.pallas_call(
            finish,
            out_shape=[shape(TR, TC)] * 5,
            in_specs=[vmem] * 7,
            out_specs=[hbm] * 5,
            scratch_shapes=[pltpu.VMEM((2, TR, TC), F32), pltpu.SemaphoreType.DMA((5,))],
            compiler_params=pltpu.CompilerParams(vmem_limit_bytes=16 * 1024 * 1024),
        )(*state)

    tiled = P("along", "cross")
    return jax.shard_map(
        per_device,
        mesh=mesh,
        in_specs=(tiled,) * 5 + (P(), P()),
        out_specs=(tiled,) * 5,
        check_vma=False,
    )
```

```python
import functools

import jax
import jax.numpy as jnp
from jax import lax
from jax.experimental import pallas as pl
from jax.experimental.pallas import tpu as pltpu
from jax.sharding import PartitionSpec as P

STEPS = 2
CIRC = 3
CONTINUITY = 0.25
MOMENTUM = 0.3
POTENTIAL = 0.5
CIRC_LEVEL = 0.2
CIRC_FORCE = 0.3
FRICTION = 0.1
VISCOSITY = 0.1

MESH = pl.DeviceIdType.MESH
F32 = jnp.float32
BF16 = jnp.bfloat16

TR = 128
TC = 256
TOP = 16
ER = TR + 2 * TOP
EC = 128
SIDE = 58
CR = TR // 4
CC = TC // 4
WR = CR + 16
CHUNK = 32
OWN = [(r, CHUNK) for r in range(TOP, TOP + TR, CHUNK)]
ALL = [(TOP - 8, 8)] + OWN + [(TOP + TR, 8)]
CROSS = [(0, -1), (0, 1)]
ALONG = [(-1, 0), (1, 0)]
DIRS = CROSS + [(-1, -1), (-1, 1), (1, -1), (1, 1)] + ALONG
HALO = 6
SENT = (5, 5, 5, 3, 5)
FIRST = (0, 5, 10, 20, 15)
E_BOTH = [(TOP - 8, TR // 2 + 8), (TOP + TR // 2, TR // 2 + 8)]
E_OWN = [(TOP, TR // 2), (TOP + TR // 2, TR // 2)]
E_ALL = [(TOP - 8, 8)] + E_OWN + [(TOP + TR, 8)]


def iota(shape, dim):
    return lax.broadcasted_iota(jnp.int32, shape, dim)


def halves(x):
    high = x.astype(BF16)
    return high, (x - high.astype(F32)).astype(BF16)


def dot(x, y):
    return jnp.dot(x, y, preferred_element_type=F32)


def dot_nt(x, y):
    return lax.dot_general(x, y, (((1,), (1,)), ((), ())), preferred_element_type=F32)


def row_next(x, keep):
    return pltpu.roll(x, x.shape[0] - 1, 0)[keep]


def row_prev(x, keep):
    return pltpu.roll(x, 1, 0)[keep]


def col_next(x):
    return pltpu.roll(x, x.shape[1] - 1, 1)


def col_prev(x):
    return pltpu.roll(x, 1, 1)


def spread(fine, coarse, fine_dim, shape, first, wrap):
    f = iota(shape, fine_dim)
    c = iota(shape, 1 - fine_dim)
    base = lax.shift_right_logical(f, 2) + first
    k = f & 3
    weight = jnp.where((k == 0) | (k == 3), 0.375, 0.125)
    other = base + jnp.where(k < 2, -1, 1)
    if wrap:
        other = other & (coarse - 1)
    zero = jnp.zeros(shape, F32)
    return (jnp.where(c == base, 1.0 - weight, zero) + jnp.where(c == other, weight, zero)).astype(BF16)


def kernel(
    mesh_rows, mesh_cols,
    s_in, u_in, v_in, d_in, w_in, cells_in, press_in,
    s_out, u_out, v_out, flow_out, mask_out, cols_out, rows_out,
    ext, wraw, cells_ref, press_ref, forc, r1, curv, slope, planes,
    e_ext, e_forc, e_r1, e_s, e_u, e_v, e_curv, e_du, e_slope, e_planes,
    packt, got, corner_send, corner, corner_s_send, corner_s,
    ts_w, ts_s, side_w, side_s, cw, cs,
    load_sem, f_send, f_recv, w_send, w_recv, c_send, c_recv,
):
    a = lax.axis_index("along")
    c = lax.axis_index("cross")
    total_cols = TC * mesh_cols

    def there(da, dc):
        ok = None
        for cond in ([a > 0] if da < 0 else [a < mesh_rows - 1] if da > 0 else []) + (
            [c > 0] if dc < 0 else [c < mesh_cols - 1] if dc > 0 else []
        ):
            ok = cond if ok is None else ok & cond
        return ok

    def device(da, dc):
        return (a + da, c + dc)

    barrier = pltpu.get_barrier_semaphore()
    for da, dc in DIRS[2:6] + CROSS + ALONG:
        @pl.when(there(da, dc))
        def _(da=da, dc=dc):
            pl.semaphore_signal(barrier, inc=1, device_id=device(da, dc), device_id_type=MESH)

    loads = []
    for k, src in enumerate((s_in, u_in, v_in, d_in)):
        loads.append(pltpu.make_async_copy(src, ext.at[k, TOP:TOP + TR, 0:TC], load_sem.at[k]))
    loads.append(pltpu.make_async_copy(w_in, wraw, load_sem.at[4]))
    loads.append(pltpu.make_async_copy(cells_in, cells_ref, load_sem.at[5]))
    loads.append(pltpu.make_async_copy(press_in, press_ref, load_sem.at[6]))
    for cp in loads:
        cp.start()

    for ref in (ext, e_ext):
        for f in range(5):
            ref[f, 0:8, :] = jnp.zeros((8, ref.shape[2]), F32)
            ref[f, ER - 8:ER, :] = jnp.zeros((8, ref.shape[2]), F32)
    for ref in (r1, s_out, u_out, v_out, curv, e_r1, e_s, e_u, e_v, e_curv):
        ref[0:8, :] = jnp.zeros((8, ref.shape[1]), F32)
        ref[ER - 8:ER, :] = jnp.zeros((8, ref.shape[1]), F32)
    for k in range(2):
        got[32 * k + 24:32 * k + 32] = jnp.zeros((8, 128), F32)
    for side in (side_w, side_s):
        side[0:CC] = jnp.zeros((CC, 128), F32)
        side[CC + 8:120] = jnp.zeros((112 - CC, 128), F32)
    for da, dc in DIRS:
        @pl.when(jnp.logical_not(there(da, dc)))
        def _(da=da, dc=dc):
            if dc == 0:
                at = TOP - 8 if da < 0 else TOP + TR
                for f in range(5):
                    ext[f, at:at + 8, 0:TC] = jnp.zeros((8, TC), F32)
                at = 0 if da < 0 else WR - 8
                for ref, nf in ((cw, 2), (cs, 3)):
                    for f in range(nf):
                        ref[f, at:at + 8] = jnp.zeros((8, 128), F32)
                return
            right = 1 if dc > 0 else 0
            if da == 0:
                got[32 * right:32 * right + 24] = jnp.zeros((24, 128), F32)
                at = CC if right else 120
                side_w[at:at + 8] = jnp.zeros((8, 128), F32)
                side_s[at:at + 8] = jnp.zeros((8, 128), F32)
            else:
                corner[0 if da < 0 else 1, right] = jnp.zeros((8, 128), F32)
                corner_s[0 if da < 0 else 1, right] = jnp.zeros((8, 128), F32)

    rows_near = 1 + jnp.where(a > 0, 1, 0) + jnp.where(a < mesh_rows - 1, 1, 0)
    cols_near = 1 + jnp.where(c > 0, 1, 0) + jnp.where(c < mesh_cols - 1, 1, 0)
    for cp in loads:
        cp.wait()
    own_wet = wraw[...].astype(F32)
    ext[4, TOP:TOP + TR, 0:TC] = own_wet
    mask_out[...] = own_wet

    lane = iota((TR, 128), 1)
    packed = jnp.zeros((TR, 128), F32)
    for part in range(2):
        surface, along, cross, depth, wet = (
            ext[f, TOP:TOP + TR, 128 * part:128 * part + 128] for f in range(5))
        far = 128 - lane if part else lane + 1
        product = (far == 4) | (far == 5)
        flow = depth * cross
        beyond = -col_prev(flow) if part else col_next(flow)
        edges = (
            jnp.where(far == 5, surface - (0.5 * CONTINUITY) * beyond, surface),
            jnp.where(product, depth * along, along),
            jnp.where(product, flow, cross),
            depth, wet)
        for f in range(5):
            start = FIRST[f] + (0 if part else 32)
            move = start + (SENT[f] if part else 0)
            packed = jnp.where(
                (lane >= start) & (lane < start + SENT[f]), pltpu.roll(edges[f], move, 1), packed)
    packt[...] = packed.T
    corner_send[0] = packed[0:8]
    corner_send[1] = packed[TR - 8:TR]

    def fine_copy(n):
        da, dc = DIRS[n]
        if da == 0:
            at = 0 if dc > 0 else 32
            src, dst = packt.at[at:at + 24], got.at[at:at + 24]
        elif dc == 0:
            src = ext.at[:, TOP:TOP + 8, 0:TC] if da < 0 else ext.at[:, TOP + TR - 8:TOP + TR, 0:TC]
            dst = ext.at[:, TOP + TR:TOP + TR + 8, 0:TC] if da < 0 else ext.at[:, TOP - 8:TOP, 0:TC]
        else:
            side = 0 if dc > 0 else 1
            src = corner_send.at[0 if da < 0 else 1]
            dst = corner.at[1 if da < 0 else 0, side]
        return pltpu.make_async_remote_copy(
            src_ref=src, dst_ref=dst, send_sem=f_send.at[n], recv_sem=f_recv.at[n],
            device_id=device(da, dc), device_id_type=MESH)

    def coarse_copy(ts, side, field, send, recv):
        def make(n):
            da, dc = DIRS[n]
            if dc == 0:
                src = field.at[:, 8:16] if da < 0 else field.at[:, CR:CR + 8]
                dst = field.at[:, CR + 8:CR + 16] if da < 0 else field.at[:, 0:8]
            elif da == 0:
                at = CC if dc < 0 else 120
                src = ts.at[0 if dc < 0 else 1]
                dst = side.at[at:at + 8]
            else:
                src = corner_s_send.at[0 if da < 0 else 1, 0 if dc > 0 else 1]
                dst = corner_s.at[1 if da < 0 else 0, 0 if dc > 0 else 1]
            return pltpu.make_async_remote_copy(
                src_ref=src, dst_ref=dst, send_sem=send.at[n], recv_sem=recv.at[n],
                device_id=device(da, dc), device_id_type=MESH)
        return make

    def start_all(make, chosen=DIRS):
        for da, dc in chosen:
            n = DIRS.index((da, dc))
            @pl.when(there(da, dc))
            def _(n=n):
                make(n).start()

    def wait_recv_all(make, chosen=DIRS):
        for da, dc in chosen:
            n = DIRS.index((da, dc))
            @pl.when(there(-da, -dc))
            def _(n=n):
                make(n).wait_recv()

    def wait_send_all(make, chosen=DIRS):
        for da, dc in chosen:
            n = DIRS.index((da, dc))
            @pl.when(there(da, dc))
            def _(n=n):
                make(n).wait_send()

    pl.semaphore_wait(barrier, rows_near * cols_near - 1)
    copy_w = coarse_copy(ts_w, side_w, cw, w_send, w_recv)
    copy_s = coarse_copy(ts_s, side_s, cs, c_send, c_recv)
    start_all(fine_copy, DIRS[2:6] + CROSS + ALONG)

    def pool_matrix(width, wanted, shift, split):
        col = iota((width, 128), 0)
        col = jnp.where(col < split, col - shift[0], col - shift[1])
        to = iota((width, 128), 1)
        hit = (lax.shift_right_arithmetic(col, 2) == to) & wanted(to) & (to < CC)
        one = jnp.where(hit, 1.0, 0.0).astype(BF16)
        return jnp.concatenate([one, one], axis=0)

    def edge_matrix(width, shift, split):
        to = iota((16, width), 0)
        to = jnp.where(to < 8, to, to + (CC - 16))
        col = iota((16, width), 1)
        col = jnp.where(col < split, col - shift[0], col - shift[1])
        one = jnp.where(lax.shift_right_arithmetic(col, 2) == to, 1.0, 0.0).astype(BF16)
        return jnp.concatenate([one, one], axis=1)

    def row_means(ref, first, nf, nh, scale):
        tall = []
        for f in range(nf):
            wide = []
            for h in range(nh):
                n = nh * (first + f) + h
                total = ref[n, pl.ds(0, CR, stride=4), :]
                for k in range(1, 4):
                    total = total + ref[n, pl.ds(k, CR, stride=4), :]
                wide.append(total * scale)
            tall.append(jnp.concatenate(wide, axis=1) if nh > 1 else wide[0])
        tall.append(jnp.zeros((TR - nf * CR, 128 * nh), F32))
        return jnp.concatenate(halves(jnp.concatenate(tall, axis=0)), axis=1)

    own = (0, 0)
    sides = (HALO, 128 - HALO - TC)
    pool_all = pool_matrix(TC, lambda j: j >= 0, own, TC)
    pool_mid = pool_matrix(TC, lambda j: (j >= 8) & (j < CC - 8), own, TC)
    pool_side = pool_matrix(EC, lambda j: (j < 8) | (j >= CC - 8), sides, EC // 2)
    edge_all = edge_matrix(TC, own, TC)
    edge_side = edge_matrix(EC, sides, EC // 2)

    for h in range(2):
        planes[6 + h] = ext[3, TOP:TOP + TR, 128 * h:128 * h + 128]
        planes[8 + h] = ext[4, TOP:TOP + TR, 128 * h:128 * h + 128]
    means = row_means(planes, 3, 2, 2, 1.0 / 16.0)
    edges = dot_nt(edge_all, means)
    ts_w[0] = edges[0:8]
    ts_w[1] = edges[8:16]
    coarse = dot(means, pool_all)
    for f in range(2):
        cw[f, 8:8 + CR] = coarse[f * CR:(f + 1) * CR]
    start_all(copy_w, CROSS)

    ext_row = a * TR - TOP + iota((ER, 8), 0)
    own_col = c * TC + iota((TC, 8), 0)
    side_col = iota((EC, 8), 0)
    side_col = c * TC + jnp.where(side_col < EC // 2, side_col - sides[0], side_col - sides[1])
    for step in range(STEPS):
        cells = cells_ref[step:step + 1, :]
        row_hit = jnp.where(ext_row == lax.div(cells, total_cols), press_ref[...], 0.0)
        for ref, col in ((forc, own_col), (e_forc, side_col)):
            col_hit = jnp.where(col == lax.rem(cells, total_cols), 1.0, 0.0)
            ref[step] = lax.dot_general(
                row_hit, col_hit, (((1,), (1,)), ((), ())),
                precision=lax.Precision.HIGHEST, preferred_element_type=F32)

    def own_waves():
        base, force, first, last, bend = ext, forc, r1, s_out, curv
        u_ref, v_ref, stress_ref, nh = u_out, v_out, planes, 2
        surface, along, cross = base.at[0], base.at[1], base.at[2]
        for step in range(STEPS):
            raised = first if step == 0 else last
            for r, n in ALL:
                keep = slice(8, 8 + n)
                wide = slice(r - 8, r + n + 8)
                here = slice(r, r + n)
                depth = base[3, wide, :]
                du = depth * along[wide, :]
                dv = depth[keep] * cross[here, :]
                flux = (row_next(du, keep) - row_prev(du, keep)) + (col_next(dv) - col_prev(dv))
                raised[here, :] = base[4, here, :] * (
                    surface[here, :] - (0.5 * CONTINUITY) * flux + force[step, here, :])
            for r, n in ALL:
                keep = slice(8, 8 + n)
                x = raised[r - 8:r + n + 8, :]
                mid = x[keep]
                down, up, right, left = row_next(x, keep), row_prev(x, keep), col_next(mid), col_prev(mid)
                slope[0, r:r + n, :] = down - up
                slope[1, r:r + n, :] = right - left
                bend[r:r + n, :] = down + up + right + left - 4.0 * mid
            for r, n in (ALL if step < STEPS - 1 else OWN):
                keep = slice(8, 8 + n)
                here = slice(r, r + n)
                x = raised[here, :]
                k = bend[r - 8:r + n + 8, :]
                depth = base[3, here, :]
                wet = base[4, here, :]
                disp = depth * depth * (1.0 / 3.0)
                push_a = slope[0, here, :] + disp * (row_next(k, keep) - row_prev(k, keep))
                k = k[keep]
                push_c = slope[1, here, :] + disp * (col_next(k) - col_prev(k))
                u = wet * (along[here, :] - (0.5 * MOMENTUM) * push_a)
                v = wet * (cross[here, :] - (0.5 * MOMENTUM) * push_c)
                u_ref[here, :] = u
                v_ref[here, :] = v
                if (r, n) in OWN:
                    pot = POTENTIAL * x * x
                    stress = (depth * u * u + pot, depth * u * v, depth * v * v + pot)
                    at = slice(r - TOP, r - TOP + n)
                    for f in range(3):
                        for h in range(nh):
                            part = stress[f][:, 128 * h:128 * h + 128]
                            if step > 0:
                                part = part + stress_ref[nh * f + h, at]
                            stress_ref[nh * f + h, at] = part
            surface, along, cross = raised, u_ref, v_ref

    def edge_waves():
        surface, along, cross = e_ext.at[0], e_ext.at[1], e_ext.at[2]
        for step in range(STEPS):
            raised = e_r1 if step == 0 else e_s
            e_du[...] = e_ext[3] * along[...]
            for r, n in E_BOTH:
                here, down, up = slice(r, r + n), slice(r + 1, r + n + 1), slice(r - 1, r + n - 1)
                dv = e_ext[3, here, :] * cross[here, :]
                flux = (e_du[down, :] - e_du[up, :]) + (col_next(dv) - col_prev(dv))
                raised[here, :] = e_ext[4, here, :] * (
                    surface[here, :] - (0.5 * CONTINUITY) * flux + e_forc[step, here, :])
            for r, n in E_BOTH:
                here, down, up = slice(r, r + n), slice(r + 1, r + n + 1), slice(r - 1, r + n - 1)
                mid = raised[here, :]
                right, left = col_next(mid), col_prev(mid)
                e_slope[here, :] = right - left
                e_curv[here, :] = raised[down, :] + raised[up, :] + right + left - 4.0 * mid
            for r, n in (E_ALL if step < STEPS - 1 else E_OWN):
                here, down, up = slice(r, r + n), slice(r + 1, r + n + 1), slice(r - 1, r + n - 1)
                depth = e_ext[3, here, :]
                wet = e_ext[4, here, :]
                disp = depth * depth * (1.0 / 3.0)
                k = e_curv[here, :]
                push_a = (raised[down, :] - raised[up, :]) + disp * (e_curv[down, :] - e_curv[up, :])
                push_c = e_slope[here, :] + disp * (col_next(k) - col_prev(k))
                u = wet * (along[here, :] - (0.5 * MOMENTUM) * push_a)
                v = wet * (cross[here, :] - (0.5 * MOMENTUM) * push_c)
                e_u[here, :] = u
                e_v[here, :] = v
                if (r, n) in E_OWN:
                    x = raised[here, :]
                    pot = POTENTIAL * x * x
                    at = slice(r - TOP, r - TOP + n)
                    for f, part in enumerate((depth * u * u + pot, depth * u * v, depth * v * v + pot)):
                        e_planes[f, at] = part + e_planes[f, at] if step > 0 else part
            surface, along, cross = raised, e_u, e_v

    def corner_matrix(side):
        lane_of = iota((EC, 128), 0)
        to = (iota((EC, 128), 1) & 7) * 4 + (HALO if side else 128 - HALO - 32)
        one = jnp.where((lane_of >= to) & (lane_of < to + 4), 1.0, 0.0).astype(BF16)
        return jnp.concatenate([one, one], axis=0)

    pool_corner = jnp.concatenate([corner_matrix(0), corner_matrix(1)], axis=1)

    def fill_edge(r, n):
        at = iota((n, 128), 1)
        for f in range(5):
            left = pltpu.roll(ext[f, r:r + n, 0:128], HALO, 1)
            right = pltpu.roll(ext[f, r:r + n, 128:256], 128 - HALO, 1)
            both = jnp.where(at < EC // 2, left, right)
            rest = 0.0
            if f == 3:
                rest = jnp.where((at < HALO - SENT[f]) | (at >= 128 - HALO + SENT[f]), 1.0, 0.0)
            e_ext[f, r:r + n, :] = jnp.where((at >= HALO) & (at < 128 - HALO), both, rest)

    fill_edge(TOP, TR)

    n_lane = iota((192, 5 * 128), 0)
    to = iota((192, 5 * 128), 1)
    to_field, to_lane = lax.shift_right_logical(to, 7), to & 127
    hit = jnp.zeros((192, 5 * 128), jnp.bool_)
    for f in range(5):
        left = (to_lane >= HALO - SENT[f]) & (to_lane < HALO) & ((n_lane & 63) == to_lane - (HALO - SENT[f]) + FIRST[f])
        right = (to_lane >= 128 - HALO) & (to_lane < 128 - HALO + SENT[f]) & (
            (n_lane & 63) == to_lane - (128 - HALO) + 32 + FIRST[f])
        hit = hit | ((to_field == f) & (left | right))
    place = jnp.where(hit, 1.0, 0.0).astype(BF16)

    wait_recv_all(fine_copy, ALONG)
    own_waves()
    coarse_mid = dot(row_means(planes, 0, 3, 2, 1.0 / (16.0 * STEPS)), pool_mid)

    fill_edge(TOP - 8, 8)
    fill_edge(TOP + TR, 8)
    wait_recv_all(fine_copy, CROSS)
    arrived = got[0:64]
    high = arrived.astype(BF16)
    rest = arrived - high.astype(F32)
    middle = rest.astype(BF16)
    low = (rest - middle.astype(F32)).astype(BF16)
    moved = lax.dot_general(
        jnp.concatenate([high, middle, low], axis=0), place,
        (((0,), (0,)), ((), ())), preferred_element_type=F32)
    rows = slice(TOP, TOP + TR)
    for f in range(5):
        e_ext[f, rows, :] = e_ext[f, rows, :] + moved[:, 128 * f:128 * f + 128]
    wait_recv_all(fine_copy, DIRS[2:6])
    few = iota((8, 128), 1)
    for t in range(2):
        halo = jnp.where(few < 32, corner[t, 0], corner[t, 1])
        at = TOP - 8 if t == 0 else TOP + TR
        for f in range(5):
            left = pltpu.roll(halo, (HALO - SENT[f] - FIRST[f]) % 128, 1)
            right = pltpu.roll(halo, 128 - HALO - 32 - FIRST[f], 1)
            e_ext[f, at:at + 8, :] = jnp.where(
                (few >= HALO - SENT[f]) & (few < HALO), left,
                jnp.where((few >= 128 - HALO) & (few < 128 - HALO + SENT[f]), right, e_ext[f, at:at + 8, :]))
    edge_waves()

    means = row_means(e_planes, 0, 3, 1, 1.0 / (16.0 * STEPS))
    edges = dot_nt(edge_side, means)
    ts_s[0] = edges[0:8]
    ts_s[1] = edges[8:16]
    start_all(copy_s, CROSS)
    coarse = dot(means, pool_corner)
    small = iota((8, 128), 1)
    group = lax.shift_right_logical(small, 3)
    for t in range(2):
        for side in range(2):
            tile = jnp.zeros((8, 128), F32)
            for f in range(3):
                r = f * CR + (0 if t == 0 else CR - 8)
                tile = jnp.where(group == f, coarse[r:r + 8, 128 * side:128 * side + 128], tile)
            corner_s_send[t, side] = tile
    start_all(copy_s, DIRS[2:6])
    coarse = dot(means, pool_side) + coarse_mid
    for f in range(3):
        cs[f, 8:8 + CR] = coarse[f * CR:(f + 1) * CR]
    start_all(copy_s, ALONG)

    rows = slice(TOP, TOP + TR)
    for ref, edge in ((s_out, e_s), (u_out, e_u), (v_out, e_v)):
        ref[rows, 0:128] = jnp.where(lane < 16, pltpu.roll(edge[rows], 128 - HALO, 1), ref[rows, 0:128])
        ref[rows, 128:256] = jnp.where(lane >= 112, pltpu.roll(edge[rows], HALO, 1), ref[rows, 128:256])

    weights = spread(TC, 128, 1, (128, TC), 0, True)
    cols_out[...] = jnp.concatenate([weights, weights], axis=0)
    weights = spread(TR, WR, 0, (TR, WR), 8, False)
    rows_out[...] = jnp.concatenate([weights, weights], axis=1)

    wait_recv_all(copy_w, CROSS)
    mid = side_w[...].T
    for f in range(2):
        cw[f, 8:8 + CR] = cw[f, 8:8 + CR] + mid[f * CR:(f + 1) * CR]
    start_all(copy_w, ALONG)
    wait_recv_all(copy_w, ALONG)
    depth, wet = cw[0], cw[1]
    inside = depth > 0.25
    inv_depth = 1.0 / jnp.maximum(depth, 0.25)
    drive = (-0.5 * CIRC_FORCE) * wet * inv_depth
    hold = wet * (1.0 - 4.0 * VISCOSITY - FRICTION * inv_depth)
    spill = VISCOSITY * wet
    slope = (0.5 * CIRC_FORCE) * wet

    wait_send_all(fine_copy)
    wait_send_all(copy_w, CROSS)

    wait_recv_all(copy_s, CROSS + ALONG)
    mid = side_s[...].T
    wait_recv_all(copy_s, DIRS[2:6])
    ends = []
    for t in range(2):
        for f in range(3):
            block = jnp.zeros((8, 128), F32)
            for side in range(2):
                at = CC if side else 120
                moved = pltpu.roll(corner_s[t, side], at - 8 * f, 1)
                block = jnp.where((small >= at) & (small < at + 8), moved, block)
            ends.append(block)
    wide = []
    for f in range(3):
        wide.append(jnp.concatenate([
            cs[f, 0:8] + ends[f],
            cs[f, 8:8 + CR] + mid[f * CR:(f + 1) * CR],
            cs[f, WR - 8:WR] + ends[3 + f]], axis=0))
    s0, s1, s2 = wide

    def row_step(x):
        return pltpu.roll(x, WR - 1, 0) - pltpu.roll(x, 1, 0)

    def col_step(x):
        return col_next(x) - col_prev(x)

    def around(x):
        return pltpu.roll(x, WR - 1, 0) + pltpu.roll(x, 1, 0) + col_next(x) + col_prev(x)

    push_a = (row_step(s0) + col_step(s1)) * drive
    push_c = (row_step(s1) + col_step(s2)) * drive
    flow_a, flow_c = push_a, push_c
    elevation = jnp.zeros_like(depth)
    for _ in range(CIRC - 1):
        level = elevation - (0.5 * CIRC_LEVEL) * (row_step(depth * flow_a) + col_step(depth * flow_c))
        elevation = jnp.where(inside, level, 0.0)
        flow_a, flow_c = (
            push_a + hold * flow_a + spill * around(flow_a) - slope * row_step(elevation),
            push_c + hold * flow_c + spill * around(flow_c) - slope * col_step(elevation),
        )

    flow_out[0] = flow_a
    flow_out[1] = flow_c
    wait_send_all(copy_w, ALONG)
    wait_send_all(copy_s)


def finish(s_ref, u_ref, v_ref, flow_ref, mask_ref, cols_ref, rows_ref, s_out, u_out, v_out, ca_out, cc_out, cur, store_sem):
    stores = [
        pltpu.make_async_copy(ref.at[TOP:TOP + TR, 0:TC], out, store_sem.at[k])
        for k, (ref, out) in enumerate(((s_ref, s_out), (u_ref, u_out), (v_ref, v_out)))
    ]
    for cp in stores:
        cp.start()
    high, low = halves(flow_ref[...].reshape(2 * WR, 128))
    wide = dot(jnp.concatenate([high, low], axis=1), cols_ref[...])
    high, low = halves(jnp.concatenate([wide[0:WR], wide[WR:2 * WR]], axis=1))
    fine = dot(rows_ref[...], jnp.concatenate([high, low], axis=0))
    mask = mask_ref[...]
    for k, out in enumerate((ca_out, cc_out)):
        cur[k] = fine[:, k * TC:k * TC + TC] * mask
        stores.append(pltpu.make_async_copy(cur.at[k], out, store_sem.at[3 + k]))
        stores[-1].start()
    for cp in stores:
        cp.wait()


def solution(mesh):
    mesh_rows, mesh_cols = mesh.shape["along"], mesh.shape["cross"]
    hbm = pl.BlockSpec(memory_space=pltpu.HBM)
    vmem = pl.BlockSpec(memory_space=pltpu.VMEM)

    def shape(*dims):
        return jax.ShapeDtypeStruct(dims, F32)

    def per_device(surface, along_speed, cross_speed, water_depth, wet_mask, ship_cells, ship_pressure):
        ships = ship_pressure.shape[0]
        state = pl.pallas_call(
            functools.partial(kernel, mesh_rows, mesh_cols),
            out_shape=[shape(ER, TC)] * 3 + [shape(2, WR, 128), shape(TR, TC)] + [
                jax.ShapeDtypeStruct((256, TC), BF16), jax.ShapeDtypeStruct((TR, 2 * WR), BF16)],
            in_specs=[hbm] * 7,
            out_specs=[vmem] * 7,
            scratch_shapes=[
                pltpu.VMEM((5, ER, TC), F32),
                pltpu.VMEM((TR, TC), jnp.int32),
                pltpu.VMEM((STEPS, ships), jnp.int32),
                pltpu.VMEM((1, ships), F32),
                pltpu.VMEM((STEPS, ER, TC), F32),
                pltpu.VMEM((ER, TC), F32),
                pltpu.VMEM((ER, TC), F32),
                pltpu.VMEM((2, ER, TC), F32),
                pltpu.VMEM((10, TR, 128), F32),
                pltpu.VMEM((5, ER, EC), F32),
                pltpu.VMEM((STEPS, ER, EC), F32),
            ] + [pltpu.VMEM((ER, EC), F32)] * 7 + [
                pltpu.VMEM((3, TR, 128), F32),
                pltpu.VMEM((128, 128), F32),
                pltpu.VMEM((128, 128), F32),
            ] + [pltpu.VMEM((2, 8, 128), F32)] + [pltpu.VMEM((2, 2, 8, 128), F32)] * 3 + [
                pltpu.VMEM((2, 8, 128), F32),
                pltpu.VMEM((2, 8, 128), F32),
                pltpu.VMEM((128, 128), F32),
                pltpu.VMEM((128, 128), F32),
                pltpu.VMEM((2, WR, 128), F32),
                pltpu.VMEM((3, WR, 128), F32),
                pltpu.SemaphoreType.DMA((7,)),
            ] + [pltpu.SemaphoreType.DMA((8,))] * 6,
            compiler_params=pltpu.CompilerParams(
                collective_id=0, has_side_effects=True, vmem_limit_bytes=32 * 1024 * 1024),
        )(*(pltpu.with_memory_space_constraint(x, pltpu.HBM) for x in (
            surface, along_speed, cross_speed, water_depth, wet_mask, ship_cells,
            ship_pressure.reshape(1, ships))))
        return pl.pallas_call(
            finish,
            out_shape=[shape(TR, TC)] * 5,
            in_specs=[vmem] * 7,
            out_specs=[hbm] * 5,
            scratch_shapes=[pltpu.VMEM((2, TR, TC), F32), pltpu.SemaphoreType.DMA((5,))],
            compiler_params=pltpu.CompilerParams(vmem_limit_bytes=16 * 1024 * 1024),
        )(*state)

    tiled = P("along", "cross")
    return jax.shard_map(
        per_device,
        mesh=mesh,
        in_specs=(tiled,) * 5 + (P(), P()),
        out_specs=(tiled,) * 5,
        check_vma=False,
    )
```
